32 devices in a mesh: grp: 8 (over z, x), vocab: 4 (over y, core).
Axes of the slice: x: 2, y: 2, z: 4, core: 2. Of those that a mesh axis runs over, the one named last changes fastest.
Arguments:
- final_hidden: bfloat16 [2048, 2048], P('grp')
- norm_gain: float32 [2048], replicated, may hold values from 0.5 to 1.5
- head_weight: bfloat16 [25088, 2048], P(('vocab', 'grp'))
- token_ids: int32 [2048], replicated, may hold values from 0 to 25087
- group_lengths: int32 [8], replicated, may hold values from 1 to 256, as said below
- segment_ids: int32 [2048], P('grp'), may hold values from 0 to 3, as said below
- continues: int32 [8], replicated, may hold values from 0 to 1, as said below
- layer_input: bfloat16 [2048, 2048], P('grp')
- key_weight: bfloat16 [2048, 2048], P(None, 'vocab')
- key_gain: float32 [2048], P('vocab'), may hold values from 0.5 to 1.5
- positions: int32 [2048], P('grp'), may hold values from 0 to 16383
- key_rows: int32 [200], P('grp'), may hold values from 0 to 255, as said below
Outputs:
- token_logprob: float32 [2048], P('grp')
- token_entropy: float32 [2048], P('grp')
- request_mean: float32 [32], P('grp')
- keys: bfloat16 [200, 2048], P('grp', 'vocab')
The draws below stay inside these ranges and needn't reach their ends.
Inputs may be any that keep to these rules, and one draw needn't show every extreme that they name: For every g below 4, group_lengths[g] + group_lengths[g + 4] <= 320; groups 0 and 4 reach that bound, and group 0 fills all 256 slots. `segment_ids`: never falls along a group's slots. `continues`: 0 for odd g, 1 for g = 0 and for g = 6. `key_rows`: each entry is below its group's length.
All inputs are finite; a program needn't handle non-finite values.
Results may differ from the reference program's by a relative error of at most 0.0071.
Values may be sent and summed in bfloat16 or wider, within the bound.
No kernel may reach another device: no remote copies, remote signals or barrier semaphores. Data moves between devices by JAX's collectives and lax.ppermute only.
A program may use at most 128 MiB of HBM per device.

```python
import math
import jax
import jax.numpy as jnp
import numpy as np
from jax import lax

D = 2048
HD = 128
CAP = 256
SEGS = 4
BAL = 160
KROWS = 25
KD = 2048
VOCAB = 25088
TOKENS = 2048
N_GRP = 8


def raw_rows(key, index):
    base = jax.random.fold_in(key, 11)

    def one_row(item):
        return jax.random.normal(jax.random.fold_in(base, item), (D,), jnp.float32)
    return jnp.clip(jax.vmap(one_row)(index), -5.0, 5.0)


def head_table(key, index):
    raw = raw_rows(key, index)
    factor = 1.0 + 0.08 * (index.astype(jnp.float32) / VOCAB - 0.5)
    return raw * 0.075 * factor[:, None]


def anchor_picks(key):
    anchors = jax.random.randint(jax.random.fold_in(key, 12), (8,), 0, VOCAB)
    partners = (anchors + VOCAB // 2) % VOCAB
    strength = jnp.array([0.9, 1.2, 1.8, 0.9, 1.2, 1.8, 1.2, 1.8], jnp.float32)
    return (anchors, partners, strength)


def length_table(key):
    groups = TOKENS // CAP
    half = groups // 2
    base = jax.random.fold_in(key, 21)
    total = jax.random.randint(jax.random.fold_in(base, 1), (half,), BAL, 2 * BAL + 1)
    total = total.at[0].set(2 * BAL)
    lowest = jnp.maximum(1, total - CAP)
    highest = jnp.minimum(CAP, total - 1)
    choose = jax.random.randint(jax.random.fold_in(base, 2), (half,), 0, 1 << 20)
    first = lowest + choose % (highest - lowest + 1)
    first = first.at[0].set(CAP)
    return jnp.concatenate([first, total - first]).astype(jnp.int32)


def scaled_field(key):
    base = jnp.clip(jax.random.normal(jax.random.fold_in(key, 1), (TOKENS, D), jnp.float32), -5.0, 5.0)
    row_scale = jnp.exp(jax.random.uniform(jax.random.fold_in(key, 2), (TOKENS, 1), jnp.float32, 0.0, jnp.log(10.0)))
    col_scale = jnp.exp(jax.random.uniform(jax.random.fold_in(key, 3), (1, D), jnp.float32, 0.0, jnp.log(10.0)))
    return base * row_scale * col_scale


def draw_head_weight(key, part):
    table = head_table(key, jnp.arange(VOCAB, dtype=jnp.int32))
    anchors, partners, strength = anchor_picks(key)
    anchor_rows = raw_rows(key, anchors) * (120.0 / D) * strength[:, None]
    noise = jax.random.normal(jax.random.fold_in(key, 13), (8, D), jnp.float32) * 0.075 * 0.12
    partner_rows = anchor_rows * (1.0 - 0.016 / strength[:, None]) + noise
    table = table.at[anchors].set(anchor_rows).at[partners].set(partner_rows)
    return table.astype(jnp.bfloat16)


def draw_final_hidden(key, part):
    field = scaled_field(jax.random.fold_in(key, 51))
    anchors, partners, strength = anchor_picks(key)
    aligned = raw_rows(key, anchors)
    rows = jnp.arange(8, dtype=jnp.int32) * (TOKENS // 8)
    field = field.at[rows].set(aligned)
    return field.astype(jnp.bfloat16)


def draw_layer_input(key, part):
    return scaled_field(jax.random.fold_in(key, 61)).astype(jnp.bfloat16)


def draw_key_weight(key, part):
    base = jnp.clip(jax.random.normal(jax.random.fold_in(key, 71), (D, KD), jnp.float32), -5.0, 5.0)
    columns = jnp.arange(KD).astype(jnp.float32)
    rising = jnp.exp(0.5 * jnp.log(3.0) * columns / KD)
    return (base * rising[None, :] / jnp.sqrt(jnp.float32(D))).astype(jnp.bfloat16)


def draw_group_lengths(key, part):
    return length_table(key)


def draw_segment_ids(key, part):
    lengths = length_table(key)
    groups = TOKENS // CAP
    raw = jax.random.randint(jax.random.fold_in(key, 31), (groups, SEGS - 1), 0, 1 << 20)
    span = jnp.maximum(lengths - 1, 1)
    breaks = 1 + raw % span[:, None]
    slots = jnp.arange(CAP, dtype=jnp.int32)
    labels = jnp.sum((breaks[:, None, :] <= slots[None, :, None]).astype(jnp.int32), axis=2)
    return labels.reshape(-1).astype(jnp.int32)


def draw_continues(key, part):
    groups = TOKENS // CAP
    raw = jax.random.randint(jax.random.fold_in(key, 41), (groups,), 0, 2)
    even = jnp.arange(groups, dtype=jnp.int32) % 2 == 0
    flags = jnp.where(even, raw, 0)
    return flags.at[0].set(1).at[groups - 2].set(1).astype(jnp.int32)


def draw_key_rows(key, part):
    lengths = length_table(key)
    groups = TOKENS // CAP
    raw = jax.random.randint(jax.random.fold_in(key, 81), (groups, KROWS), 0, 1 << 20)
    rows = raw % lengths[:, None]
    rows = rows.at[0, 0].set(CAP - 1).at[1, 0].set(0)
    return rows.reshape(-1).astype(jnp.int32)


def plant(values, own_key, smallest, top_value):
    place = [jax.random.randint(jax.random.fold_in(own_key, axis), (), 0, length) for axis, length in enumerate(values.shape)]
    widest = values.shape.index(max(values.shape))
    beside = place[:widest] + [(place[widest] + 1) % values.shape[widest]] + place[widest + 1:]
    return values.at[tuple(place)].set(smallest).at[tuple(beside)].set(top_value)


def rank_table(count, lean):
    loads = [(1 << 20) // math.isqrt(standing ** lean) + 1 for standing in range(1, count + 1)]
    scale = 1 + sum(loads) // (1 << 30)
    return np.cumsum(np.array([max(1, weight // scale) for weight in loads]))


def ranked_ids(own_key, shape, number_of, skew):
    grid = rank_table(number_of, skew)
    lot = jax.random.randint(jax.random.fold_in(own_key, 1), shape, 0, int(grid[number_of - 1]))
    grade = jnp.searchsorted(jnp.asarray(grid, jnp.int32), lot, side="right")
    return jax.random.permutation(jax.random.fold_in(own_key, 2), number_of)[grade].astype(jnp.int32)


def setup_inputs(seed: int = 0) -> dict:
    arg_keys = jax.random.split(jax.random.key(seed), 13)
    return {
        "final_hidden": draw_final_hidden(jax.random.fold_in(arg_keys[12], 71), 0),
        "norm_gain": jnp.clip(1.0 + 0.1 * jax.random.normal(arg_keys[1], (D,), jnp.float32), 0.5, 1.5),
        "head_weight": draw_head_weight(jax.random.fold_in(arg_keys[12], 71), 0),
        "token_ids": plant(ranked_ids(arg_keys[3], (TOKENS,), VOCAB, 2), jax.random.fold_in(arg_keys[3], 3), 0, VOCAB - 1).astype(jnp.int32),
        "group_lengths": draw_group_lengths(jax.random.fold_in(arg_keys[12], 71), 0),
        "segment_ids": draw_segment_ids(jax.random.fold_in(arg_keys[12], 71), 0),
        "continues": draw_continues(jax.random.fold_in(arg_keys[12], 71), 0),
        "layer_input": draw_layer_input(jax.random.fold_in(arg_keys[12], 71), 0),
        "key_weight": draw_key_weight(jax.random.fold_in(arg_keys[12], 71), 0),
        "key_gain": jnp.clip(1.0 + 0.1 * jax.random.normal(arg_keys[9], (KD,), jnp.float32), 0.5, 1.5),
        "positions": plant(jax.random.randint(arg_keys[10], (TOKENS,), 0, 16384), jax.random.fold_in(arg_keys[10], 1), 0, 16383).astype(jnp.int32),
        "key_rows": draw_key_rows(jax.random.fold_in(arg_keys[12], 71), 0),
    }


NORM_EPS = 1e-06
ROPE_BASE = 500000.0

def normalize(hidden, gain):
    widened = hidden.astype(jnp.float32)
    meansq = lax.optimization_barrier(jnp.mean(widened * widened, axis=-1, keepdims=True))
    return (widened * lax.rsqrt(meansq + NORM_EPS) * gain).astype(jnp.bfloat16)

def group_stats(normed_rows, targets, weight):
    product = jnp.dot(normed_rows, weight.T, preferred_element_type=jnp.float32)
    logits = lax.optimization_barrier(product.astype(jnp.bfloat16)).astype(jnp.float32)
    highest = lax.optimization_barrier(jnp.max(logits, axis=1))
    shifted = jnp.exp(logits - highest[:, None])
    expsum = lax.optimization_barrier(jnp.sum(shifted, axis=1))
    moment = lax.optimization_barrier(jnp.sum(shifted * logits, axis=1))
    picked = jnp.take_along_axis(logits, targets[:, None], axis=1)[:, 0]
    logsum = highest + jnp.log(expsum)
    return (picked - logsum, logsum - moment / expsum)

def rotate(values, places):
    count = values.shape[0]
    heads = values.shape[1] // HD
    half = HD // 2
    shaped = values.reshape(count, heads, HD)
    steps = jnp.arange(half).astype(jnp.float32)
    freqs = jnp.exp(-(2.0 * steps / HD) * jnp.log(jnp.float32(ROPE_BASE)))
    angles = places[:, None] * freqs[None, :]
    cosine = jnp.cos(angles)[:, None, :]
    sine = jnp.sin(angles)[:, None, :]
    first = shaped[..., :half]
    second = shaped[..., half:]
    turned = jnp.concatenate([first * cosine - second * sine, second * cosine + first * sine], axis=-1)
    return turned.reshape(count, heads * HD)

def reference(final_hidden, norm_gain, head_weight, token_ids, group_lengths, segment_ids, continues, layer_input, key_weight, key_gain, positions, key_rows):
    groups = N_GRP
    normed = normalize(final_hidden, norm_gain).reshape(groups, CAP, D)
    targets = token_ids.reshape(groups, CAP)
    logprob, entropy = lax.map(lambda pair: group_stats(pair[0], pair[1], head_weight), (normed, targets))
    slots = jnp.arange(CAP, dtype=jnp.int32)
    live = slots[None, :] < group_lengths[:, None]
    logprob = jnp.where(live, logprob, 0.0)
    entropy = jnp.where(live, entropy, 0.0)
    segs = segment_ids.reshape(groups, CAP)
    labels = jnp.arange(SEGS, dtype=jnp.int32)
    member = (segs[:, :, None] == labels[None, None, :]) & live[:, :, None]
    sums = lax.optimization_barrier(jnp.sum(jnp.where(member, logprob[:, :, None], 0.0), axis=1))
    counts = lax.optimization_barrier(jnp.sum(member.astype(jnp.float32), axis=1))
    group_index = jnp.arange(groups, dtype=jnp.int32)
    partner = jnp.bitwise_xor(group_index, 1)
    partner_sums = sums[partner]
    partner_counts = counts[partner]
    is_even = group_index % 2 == 0
    joined = jnp.where(is_even, continues, continues[partner]) == 1
    my_last = jnp.take_along_axis(segs, (group_lengths - 1)[:, None].astype(jnp.int32), axis=1)[:, 0]
    partner_last = lax.optimization_barrier(jnp.max(jnp.where(partner_counts > 0, labels[None, :], 0), axis=1))
    extra_sum = jnp.where(is_even, partner_sums[:, 0], jnp.take_along_axis(partner_sums, partner_last[:, None], axis=1)[:, 0])
    extra_count = jnp.where(is_even, partner_counts[:, 0], jnp.take_along_axis(partner_counts, partner_last[:, None], axis=1)[:, 0])
    target_slot = jnp.where(is_even, my_last, 0)
    update = joined[:, None] & (labels[None, :] == target_slot[:, None])
    total_sum = sums + jnp.where(update, extra_sum[:, None], 0.0)
    total_count = counts + jnp.where(update, extra_count[:, None], 0.0)
    request_mean = total_sum / jnp.maximum(total_count, 1.0)
    row_index = jnp.arange(groups * KROWS, dtype=jnp.int32) // KROWS * CAP + key_rows
    chosen = jnp.take(layer_input, row_index, axis=0)
    projected = jnp.dot(chosen, key_weight, preferred_element_type=jnp.float32)
    scale = jnp.sqrt(lax.optimization_barrier(jnp.mean(projected * projected, axis=1)) + NORM_EPS)
    normal_keys = projected / scale[:, None] * key_gain
    places = jnp.take(positions, row_index).astype(jnp.float32)
    keys = rotate(normal_keys, places).astype(jnp.bfloat16)
    return (logprob.reshape(-1), entropy.reshape(-1), request_mean.reshape(-1), keys)
```

```python
import functools

import jax
import jax.numpy as jnp
from jax import lax
from jax.experimental import pallas as pl
from jax.experimental.pallas import tpu as pltpu
from jax.sharding import PartitionSpec as P

HD = 128
SEGS = 4
BAL = 160
CORES = 2

NORM_EPS = 1e-06
ROPE_BASE = 500000.0

VMEM_LIMIT = 48 * 1024 * 1024
WHOLE = pl.BlockSpec(memory_space=pltpu.VMEM)
SCALARS = pl.BlockSpec(memory_space=pltpu.SMEM)


def call(kernel, out_shape, in_specs, flops, moved, **more):
    return pl.pallas_call(
        kernel,
        out_shape=out_shape,
        in_specs=in_specs,
        compiler_params=pltpu.CompilerParams(vmem_limit_bytes=VMEM_LIMIT),
        cost_estimate=pl.CostEstimate(flops=flops, bytes_accessed=moved, transcendentals=0),
        **more,
    )


def source_row(place, quarter, is_first, quarters, rows):
    return jnp.where(
        is_first,
        quarters * place + quarter,
        quarters * (rows - 1 - place) + quarters - 1 - quarter,
    )


def prep_kernel(meta_ref, hidden_ref, gain_ref, out_ref):
    parts, rows, _ = out_ref.shape
    count = hidden_ref.shape[0]
    widened = hidden_ref[...].astype(jnp.float32)
    meansq = jnp.mean(widened * widened, axis=-1, keepdims=True)
    normed = (widened * lax.rsqrt(meansq + NORM_EPS) * gain_ref[...]).astype(jnp.bfloat16)
    place = lax.broadcasted_iota(jnp.int32, (rows, count), 0)
    column = lax.broadcasted_iota(jnp.int32, (rows, count), 1)
    for t in range(parts):
        quarter = (meta_ref[1] ^ t) * CORES + meta_ref[2]
        row = source_row(place, quarter, meta_ref[0] == 1, parts * CORES, rows)
        pick = (column == row).astype(jnp.float32).astype(jnp.bfloat16)
        out_ref[t] = jnp.dot(pick, normed, preferred_element_type=jnp.float32).astype(jnp.bfloat16)


def score_kernel(count, meta_ref, targets_ref, *refs):
    pieces, (near_ref, far_ref, out_ref, tokens_ref) = refs[:count], refs[count:]
    step = pl.program_id(0)
    tile = near_ref.shape[0]
    size = pieces[0].shape[0]

    @pl.when(step == 0)
    def _():
        for t, piece in enumerate(pieces):
            start = 0 if count == 1 else pl.multiple_of((meta_ref[2] ^ t) * size, 8)
            tokens_ref[pl.ds(start, size), :] = piece[...]
        out_ref[...] = jnp.zeros_like(out_ref)
        out_ref[0:1, :] = jnp.full((1, out_ref.shape[1]), -jnp.inf, jnp.float32)

    tokens = tokens_ref[...]
    targets = targets_ref[...]
    for which, weight_ref in enumerate((near_ref, far_ref)):
        logits = lax.dot_general(
            weight_ref[...], tokens, (((1,), (1,)), ((), ())), preferred_element_type=jnp.float32
        )
        logits = logits.astype(jnp.bfloat16).astype(jnp.float32)
        old = out_ref[0:1, :]
        top = jnp.maximum(old, jnp.max(logits, axis=0, keepdims=True))
        shifted = jnp.exp(logits - top)
        scale = jnp.exp(old - top)
        entry = lax.broadcasted_iota(jnp.int32, logits.shape, 0)
        wanted = targets - (meta_ref[which] + step * tile)
        out_ref[0:1, :] = top
        out_ref[1:2, :] = out_ref[1:2, :] * scale + jnp.sum(shifted, axis=0, keepdims=True)
        out_ref[2:3, :] = out_ref[2:3, :] * scale + jnp.sum(shifted * logits, axis=0, keepdims=True)
        out_ref[3:4, :] += jnp.sum(jnp.where(entry == wanted, logits, 0.0), axis=0, keepdims=True)


def score(meta, targets, pieces, near, far):
    vocab, width = near.shape
    tokens = sum(piece.shape[0] for piece in pieces)
    tile = vocab
    for parts in range(1, vocab // 16 + 1):
        if vocab % parts == 0 and (vocab // parts) % 16 == 0 and vocab // parts <= 128:
            tile = vocab // parts
            break
    head = pl.BlockSpec((tile, width), lambda i: (i, 0))
    return call(
        functools.partial(score_kernel, len(pieces)),
        jax.ShapeDtypeStruct((8, tokens), jnp.float32),
        [SCALARS, WHOLE] + [WHOLE] * len(pieces) + [head, head],
        4 * vocab * tokens * width,
        4 * vocab * width + 2 * tokens * width,
        out_specs=pl.BlockSpec((8, tokens), lambda i: (0, 0)),
        grid=(vocab // tile,),
        scratch_shapes=[pltpu.VMEM((tokens, width), jnp.bfloat16)],
    )(meta, targets, *pieces, near, far)


def keys_kernel(rows_ref, input_ref, weight_ref, gain_ref, cosine_ref, sine_ref, turned_ref, squares_ref):
    count, width = turned_ref.shape
    column = lax.broadcasted_iota(jnp.int32, (count, input_ref.shape[0]), 1)
    pick = (column == rows_ref[...]).astype(jnp.float32).astype(jnp.bfloat16)
    chosen = jnp.dot(pick, input_ref[...], preferred_element_type=jnp.float32).astype(jnp.bfloat16)
    projected = jnp.dot(chosen, weight_ref[...], preferred_element_type=jnp.float32)
    squares = jnp.sum(projected * projected, axis=1, keepdims=True)
    lanes = squares_ref.shape[1]
    diagonal = lax.broadcasted_iota(jnp.int32, (count, lanes), 0) == lax.broadcasted_iota(
        jnp.int32, (count, lanes), 1
    )
    squares_ref[...] = jnp.sum(jnp.where(diagonal, squares, 0.0), axis=0, keepdims=True)
    gained = projected * gain_ref[...]
    cosine, sine = cosine_ref[...], sine_ref[...]
    for start in range(0, width, HD):
        head = gained[:, start : start + HD]
        turned_ref[:, start : start + HD] = head * cosine + pltpu.roll(head, HD // 2, 1) * sine


def final_kernel(
    sizes,
    meta_ref,
    lengths_ref,
    continues_ref,
    got_ref,
    segments_ref,
    turned_ref,
    logprob_ref,
    entropy_ref,
    mean_ref,
    keys_ref,
):
    groups, shards = sizes
    parts, group = shards // CORES, meta_ref[0]
    cap, tokens = segments_ref.shape[1], got_ref.shape[3]
    columns = []
    for core in range(CORES):
        every = got_ref[:, core]
        top = jnp.max(every[:, 0:1, :], axis=0)
        scale = jnp.exp(every[:, 0:1, :] - top[None])
        expsum = jnp.sum(every[:, 1:2, :] * scale, axis=0)
        moment = jnp.sum(every[:, 2:3, :] * scale, axis=0)
        picked = jnp.sum(every[:, 3:4, :], axis=0)
        lse = top + jnp.log(expsum)
        columns.append(jnp.concatenate([picked - lse, lse - moment / expsum], axis=0))
    both = jnp.concatenate(columns, axis=1)
    values = jnp.concatenate([both, jnp.zeros((6, both.shape[1]), jnp.float32)], axis=0)

    slots = lax.broadcasted_iota(jnp.int32, (1, cap), 1)
    is_first = group < groups // 2
    quarter = jnp.where(is_first, slots % shards, shards - 1 - slots % shards)
    size = tokens // 2 // parts
    place = jnp.where(is_first, slots // shards, size - 1 - slots // shards)
    home = (quarter % CORES) * tokens + quarter // CORES * size + place
    stood = lax.broadcasted_iota(jnp.int32, (CORES * tokens, cap), 0)
    labels = lax.broadcasted_iota(jnp.int32, (1, SEGS), 1)

    def summed(who, segments):
        pick = (stood == home + who % 2 * (tokens // 2)).astype(jnp.float32)
        found = jnp.dot(
            values, pick, preferred_element_type=jnp.float32, precision=lax.Precision.HIGHEST
        )
        live = slots < lengths_ref[who]
        logprob = jnp.where(live, found[0:1, :], 0.0)
        entropy = jnp.where(live, found[1:2, :], 0.0)
        sums = jnp.zeros((1, SEGS), jnp.float32)
        counts = jnp.zeros((1, SEGS), jnp.float32)
        for label in range(SEGS):
            member = live & (segments == label)
            one_sum = jnp.sum(jnp.where(member, logprob, 0.0), axis=1, keepdims=True)
            one_count = jnp.sum(member.astype(jnp.float32), axis=1, keepdims=True)
            sums = jnp.where(labels == label, one_sum, sums)
            counts = jnp.where(labels == label, one_count, counts)
        return logprob, entropy, sums, counts

    partner = group ^ 1
    logprob, entropy, sums, counts = summed(group, segments_ref[0:1, :])
    _, _, partner_sums, partner_counts = summed(partner, segments_ref[1:2, :])
    is_even = group % 2 == 0
    joined = jnp.where(is_even, continues_ref[group], continues_ref[partner]) == 1
    last = slots == lengths_ref[group] - 1
    my_last = jnp.sum(jnp.where(last, segments_ref[0:1, :], 0), axis=1, keepdims=True)
    partner_last = jnp.max(jnp.where(partner_counts > 0, labels, 0), axis=1, keepdims=True)
    wanted = jnp.where(is_even, jnp.zeros_like(partner_last), partner_last)
    extra_sum = jnp.sum(jnp.where(labels == wanted, partner_sums, 0.0), axis=1, keepdims=True)
    extra_count = jnp.sum(jnp.where(labels == wanted, partner_counts, 0.0), axis=1, keepdims=True)
    target = jnp.where(is_even, my_last, jnp.zeros_like(my_last))
    update = joined & (labels == target)
    total_sum = sums + jnp.where(update, extra_sum, 0.0)
    total_count = counts + jnp.where(update, extra_count, 0.0)
    logprob_ref[...] = logprob
    entropy_ref[...] = entropy
    mean_ref[...] = total_sum / jnp.maximum(total_count, 1.0)

    count, width = turned_ref.shape
    squares = jnp.zeros((1, count), jnp.float32)
    for part in range(parts):
        for core in range(CORES):
            squares += got_ref[group * parts + part, core][4:5, :count]
    diagonal = lax.broadcasted_iota(jnp.int32, (count, count), 0) == lax.broadcasted_iota(
        jnp.int32, (count, count), 1
    )
    squares = jnp.sum(jnp.where(diagonal, squares, 0.0), axis=1, keepdims=True)
    scale = jnp.sqrt(squares / (width * shards) + NORM_EPS)
    keys_ref[...] = (turned_ref[...] / scale).astype(jnp.bfloat16)


def partners(axes, sizes, flips):
    (groups, shards), (group_flip, shard_flip) = sizes, flips
    return [
        (g * shards + v, (g ^ group_flip) * shards + (v ^ shard_flip))
        for g in range(groups)
        for v in range(shards)
    ]


def local(
    sizes,
    final_hidden,
    norm_gain,
    head_weight,
    token_ids,
    group_lengths,
    segment_ids,
    continues,
    layer_input,
    key_weight,
    key_gain,
    positions,
    key_rows,
):
    groups, shards = sizes
    parts, half = shards // CORES, groups // 2
    cap, width = final_hidden.shape
    rows = cap // shards
    size = 2 * BAL // shards
    tokens = 2 * parts * size
    group = lax.axis_index("grp")
    shard = lax.axis_index("vocab")
    y, core = shard // CORES, shard % CORES
    is_first = group < half
    axes = ("grp", "vocab")

    def swap(array, group_flip, shard_flip):
        return lax.ppermute(array, axes, partners(axes, sizes, (group_flip, shard_flip)))

    def front(which, quarter):
        return (group_lengths[which] - quarter + shards - 1) // shards

    def merge(own, other, which, quarter):
        first = jnp.where(is_first, own, other)
        second = jnp.where(is_first, other, own)
        gap = size - rows
        place = lax.broadcasted_iota(jnp.int32, (size, 1), 0)
        return jnp.where(
            place < front(which % half, quarter),
            jnp.pad(first, ((0, gap), (0, 0))),
            jnp.pad(second, ((gap, 0), (0, 0))),
        )

    vocab = head_weight.shape[0]
    far_weight = swap(head_weight, 0, 1)
    near_base = (shard * groups + group) * vocab
    far_base = ((shard ^ 1) * groups + group) * vocab
    segments = jnp.stack([segment_ids, swap(segment_ids, 1, 0)])

    dealt = token_ids.reshape(groups, rows, shards).transpose(0, 2, 1)
    gap = size - rows
    lower = jnp.pad(dealt[:half], ((0, 0), (0, 0), (0, gap)))
    upper = jnp.pad(dealt[half:, ::-1, ::-1], ((0, 0), (0, 0), (gap, 0)))
    taken = (group_lengths[:half, None] - jnp.arange(shards)[None, :] + shards - 1) // shards
    ids = jnp.where(jnp.arange(size)[None, None, :] < taken[:, :, None], lower, upper)
    ids = ids.reshape(half // 2, 2, parts, CORES, size)
    ids = lax.dynamic_index_in_dim(ids, core, 3, False).reshape(half // 2, 1, tokens)

    meta = jnp.stack([is_first.astype(jnp.int32), y, core])
    normed = call(
        prep_kernel,
        jax.ShapeDtypeStruct((parts, rows, width), jnp.bfloat16),
        [SCALARS, WHOLE, WHOLE],
        2 * parts * rows * cap * width,
        4 * cap * width,
    )(meta, final_hidden, norm_gain.reshape(1, width))

    places = jnp.sum(
        jnp.where(jnp.arange(cap)[None, :] == key_rows[:, None], positions[None, :], 0), axis=1
    ).astype(jnp.float32)
    steps = jnp.arange(HD // 2).astype(jnp.float32)
    freqs = jnp.exp(-(2.0 * steps / HD) * jnp.log(jnp.float32(ROPE_BASE)))
    angles = places[:, None] * freqs[None, :]
    cosine, sine = jnp.cos(angles), jnp.sin(angles)
    count, key_width = key_rows.shape[0], key_weight.shape[1]
    turned, squares = call(
        keys_kernel,
        (
            jax.ShapeDtypeStruct((count, key_width), jnp.float32),
            jax.ShapeDtypeStruct((1, tokens), jnp.float32),
        ),
        [WHOLE] * 6,
        2 * count * width * key_width,
        2 * width * key_width,
    )(
        key_rows.reshape(count, 1),
        layer_input,
        key_weight,
        key_gain.reshape(1, key_width),
        jnp.concatenate([cosine, cosine], axis=1),
        jnp.concatenate([-sine, sine], axis=1),
    )

    def statistics(slot, targets, pieces):
        where = jnp.stack([near_base, far_base, slot])
        return score(where, targets, pieces, head_weight, far_weight)

    if sizes == (8, 4):
        quarter, beyond = shard, shard ^ 2
        slot = group % 2 * parts + y
        here, there = normed[0], normed[1]
        other = swap(here, 4, 0)
        across = swap(normed, 1, 0)
        own = merge(here, other, group, quarter)
        far_own = swap(own, 2, 0)
        other_x = swap(other, 1, 0)
        other_y = swap(other, 0, 2)
        other_xy = swap(other, 1, 2)
        own_y = merge(there, other_y, group, beyond)
        own_x = merge(across[0], other_x, group ^ 1, quarter)
        own_xy = merge(across[1], other_xy, group ^ 1, beyond)
        far_x = swap(far_own, 1, 0)
        far_y = swap(far_own, 0, 2)
        far_xy = swap(own_xy, 2, 0)
        mine = (group % half) // 2
        own_stats = statistics(slot, ids[mine], (own, own_y, own_x, own_xy))
        far_stats = statistics(slot, ids[1 - mine], (far_own, far_y, far_x, far_xy))
        stats = jnp.where(
            (jnp.arange(half // 2) == mine)[:, None, None], own_stats[None], far_stats[None]
        )
    else:
        every = lax.all_gather(normed[0], axes).reshape(groups, parts, CORES, rows, width)
        every = lax.dynamic_index_in_dim(every, core, 2, False)
        first = jnp.pad(every[:half], ((0, 0), (0, 0), (0, gap), (0, 0)))
        second = jnp.pad(every[half:], ((0, 0), (0, 0), (gap, 0), (0, 0)))
        taken = lax.dynamic_index_in_dim(taken.reshape(half, parts, CORES), core, 2, False)
        every = jnp.where(
            jnp.arange(size)[None, None, :, None] < taken[:, :, None, None], first, second
        )
        stats = statistics(jnp.int32(0), ids.reshape(1, -1), (every.reshape(-1, width),))
        stats = stats.reshape(8, half // 2, tokens).transpose(1, 0, 2)

    row = jnp.arange(8)[None, :, None]
    stats = jnp.where(row == 4, squares[None], stats)
    sent = jnp.broadcast_to(
        stats[None, :, None, None], (2, half // 2, 2, shards, 8, tokens)
    ).reshape(groups * shards, 8, tokens)
    got = lax.all_to_all(sent, axes, 0, 0, tiled=False)

    logprob, entropy, means, keys = call(
        functools.partial(final_kernel, sizes),
        (
            jax.ShapeDtypeStruct((1, cap), jnp.float32),
            jax.ShapeDtypeStruct((1, cap), jnp.float32),
            jax.ShapeDtypeStruct((1, SEGS), jnp.float32),
            jax.ShapeDtypeStruct((count, key_width), jnp.bfloat16),
        ),
        [SCALARS] * 3 + [WHOLE] * 3,
        1 << 24,
        4 * groups * shards * 8 * tokens,
    )(
        group[None],
        group_lengths,
        continues,
        got.reshape(groups * parts, CORES, 8, tokens),
        segments,
        turned,
    )
    return logprob.reshape(cap), entropy.reshape(cap), means.reshape(SEGS), keys


def solution(mesh):
    sizes = (mesh.shape["grp"], mesh.shape["vocab"])
    in_specs = (
        P("grp", None),
        P(),
        P(("vocab", "grp"), None),
        P(),
        P(),
        P("grp"),
        P(),
        P("grp", None),
        P(None, "vocab"),
        P("vocab"),
        P("grp"),
        P("grp"),
    )
    out_specs = (P("grp"), P("grp"), P("grp"), P("grp", "vocab"))
    return jax.shard_map(
        functools.partial(local, sizes),
        mesh=mesh,
        in_specs=in_specs,
        out_specs=out_specs,
        check_vma=False,
    )
```

```python
import functools

import jax
import jax.numpy as jnp
from jax import lax
from jax.experimental import pallas as pl
from jax.experimental.pallas import tpu as pltpu
from jax.sharding import PartitionSpec as P

HD = 128
SEGS = 4
BAL = 160
CORES = 2
LANES = 128
BREAKS = 31

NORM_EPS = 1e-06
ROPE_BASE = 500000.0

VMEM_LIMIT = 24 * 1024 * 1024
WHOLE = pl.BlockSpec(memory_space=pltpu.VMEM)
SCALARS = pl.BlockSpec(memory_space=pltpu.SMEM)
FAR = pl.BlockSpec(memory_space=pltpu.HBM)


def call(kernel, out_shape, in_specs, flops, moved, vmem=VMEM_LIMIT, **more):
    return pl.pallas_call(
        kernel,
        out_shape=out_shape,
        in_specs=in_specs,
        compiler_params=pltpu.CompilerParams(vmem_limit_bytes=vmem),
        cost_estimate=pl.CostEstimate(flops=flops, bytes_accessed=moved, transcendentals=0),
        **more,
    )


def place_of(shards):
    shard = lax.axis_index("vocab")
    return lax.axis_index("grp"), lax.div(shard, CORES), lax.rem(shard, CORES)


def source_row(place, quarter, is_first, quarters, rows):
    return jnp.where(
        is_first,
        quarters * place + quarter,
        quarters * (rows - 1 - place) + quarters - 1 - quarter,
    )


def front(length, quarter, shards):
    return lax.div(length - quarter + shards - 1, shards)


def fetch(sources, targets, semaphores):
    copies = [
        pltpu.make_async_copy(source, target, semaphores.at[i])
        for i, (source, target) in enumerate(zip(sources, targets))
    ]
    for copy in copies:
        copy.start()
    return copies


def prep_kernel(sizes, hidden_ref, gain_ref, *refs):
    *known, out_ref = refs
    groups, shards = sizes
    rows, width = out_ref.shape[-2:]
    group, y, core = place_of(shards)
    place = lax.broadcasted_iota(jnp.int32, (rows, hidden_ref.shape[0]), 0)
    column = lax.broadcasted_iota(jnp.int32, place.shape, 1)
    for t, known_ref in enumerate(known):
        out_ref[t] = known_ref[...]
    for t in range(len(known), out_ref.shape[0] if known else 1):
        row = source_row(place, (y ^ t) * CORES + core, group < groups // 2, shards, rows)
        pick = (column == row).astype(jnp.float32).astype(jnp.bfloat16)
        dealt = jnp.dot(pick, hidden_ref[...], preferred_element_type=jnp.float32)
        meansq = jnp.sum(dealt * dealt, axis=-1, keepdims=True) / width
        dealt = (dealt * lax.rsqrt(meansq + NORM_EPS) * gain_ref[...]).astype(jnp.bfloat16)
        if known:
            out_ref[t] = dealt
        else:
            out_ref[...] = dealt


def pack(out_ref, start, is_first, own, other, length, quarter, shards):
    rows = own.shape[0]
    size = 2 * BAL // shards
    gap = size - rows
    place = lax.broadcasted_iota(jnp.int32, (rows - gap, own.shape[1]), 0) + gap
    is_lower = place < front(length, quarter, shards)

    def lay(lower, upper):
        middle = jnp.where(
            is_lower, lower[gap:rows, :].astype(jnp.float32), upper[0 : rows - gap, :].astype(jnp.float32)
        )
        out_ref[start : start + gap, :] = lower[0:gap, :]
        out_ref[start + gap : start + rows, :] = middle.astype(jnp.bfloat16)
        out_ref[start + rows : start + size, :] = upper[rows - gap : rows, :]

    @pl.when(is_first)
    def _():
        lay(own, other)

    @pl.when(jnp.logical_not(is_first))
    def _():
        lay(other, own)


def merge_kernel(sizes, flips, lengths_ref, own_ref, other_ref, out_ref):
    groups, shards = sizes
    x_flip, y_flip = flips
    half = groups // 2
    group, y, core = place_of(shards)
    own = own_ref if len(own_ref.shape) == 2 else own_ref.at[y_flip]
    pack(
        out_ref,
        0,
        group < half,
        own,
        other_ref,
        lengths_ref[lax.rem(group, half) ^ x_flip],
        (y ^ y_flip) * CORES + core,
        shards,
    )


def statistics(bases, targets, tokens, heads):
    state = None
    for base, head_ref in zip(bases, heads):
        logits = lax.dot_general(
            head_ref[...], tokens, (((1,), (1,)), ((), ())), preferred_element_type=jnp.float32
        )
        logits = logits.astype(jnp.bfloat16).astype(jnp.float32)
        entry = lax.broadcasted_iota(jnp.int32, logits.shape, 0)
        found = jnp.where(entry == targets - base, logits, 0.0)
        picked = jnp.sum(found, axis=0, keepdims=True)
        top = jnp.max(logits, axis=0, keepdims=True)
        if state is not None:
            top = jnp.maximum(top, state[0])
        shifted = jnp.exp(logits - top)
        expsum = jnp.sum(shifted, axis=0, keepdims=True)
        moment = jnp.sum(shifted * logits, axis=0, keepdims=True)
        if state is not None:
            scale = jnp.exp(state[0] - top)
            expsum += state[1] * scale
            moment += state[2] * scale
            picked += state[3]
        state = (top, expsum, moment, picked)
    top, expsum, moment, picked = state
    return top + jnp.log(expsum), moment / expsum, picked


def packed(state, extra):
    flat = [row[:, : 2 * LANES] for row in state] + [row[:, 2 * LANES :] for row in state] + [extra]
    flat = jnp.concatenate(flat, axis=1)
    return jnp.concatenate(
        [flat[:, i : i + LANES] for i in range(0, flat.shape[1], LANES)], axis=0
    )


def unpacked(every):
    places = ((0, 6, 0), (2, 6, LANES // 2), (4, 7, 0))
    return [
        jnp.concatenate(
            [
                every[:, row : row + 1, :],
                every[:, row + 1 : row + 2, :],
                every[:, last : last + 1, start : start + LANES // 2],
            ],
            axis=2,
        )
        for row, last, start in places
    ]


def bases_of(sizes, head_ref):
    groups, shards = sizes
    group, shard = lax.axis_index("grp"), lax.axis_index("vocab")
    return [((shard ^ flip) * groups + group) * head_ref.shape[0] for flip in (0, 1)]


def rows_of(state, out_ref):
    rows = jnp.concatenate([*state, jnp.zeros((5, out_ref.shape[1]), jnp.float32)], axis=0)
    out_ref[...] = rows


def plain_kernel(sizes, targets_ref, near_ref, far_ref, tokens_ref, out_ref):
    state = statistics(
        bases_of(sizes, near_ref), targets_ref[...], tokens_ref[...], (near_ref, far_ref)
    )
    rows_of(state, out_ref)


def early_kernel(
    sizes,
    lengths_ref,
    targets_ref,
    near_ref,
    far_ref,
    own_ref,
    dealt_ref,
    other_y_ref,
    across_ref,
    other_x_ref,
    own_xy_ref,
    far_own_ref,
    out_ref,
    tokens_ref,
):
    groups, shards = sizes
    half = groups // 2
    group, y, core = place_of(shards)
    is_first, column = group < half, lax.rem(group, half)
    size = own_ref.shape[0]
    quarter = y * CORES + core
    tokens_ref[0:size, :] = own_ref[...]
    lower = lengths_ref[column]
    pack(tokens_ref, size, is_first, dealt_ref.at[1], other_y_ref, lower, quarter ^ CORES, shards)
    lower = lengths_ref[column ^ 1]
    pack(tokens_ref, 2 * size, is_first, across_ref.at[0], other_x_ref, lower, quarter, shards)
    tokens_ref[3 * size : 4 * size, :] = own_xy_ref[...]
    tokens_ref[4 * size : 5 * size, :] = far_own_ref[...]
    state = statistics(
        bases_of(sizes, near_ref), targets_ref[...], tokens_ref[...], (near_ref, far_ref)
    )
    rows_of(state, out_ref)


def send_kernel(sizes, targets_ref, near_ref, far_ref, early_ref, extra_ref, *refs):
    *pieces, out_ref, tokens_ref = refs
    groups, shards = sizes
    size = pieces[0].shape[0]
    for t, piece in enumerate(pieces):
        tokens_ref[t * size : (t + 1) * size, :] = piece[...]
    state = statistics(
        bases_of(sizes, near_ref), targets_ref[...], tokens_ref[...], (near_ref, far_ref)
    )
    tokens = early_ref.shape[1] - size
    early = [early_ref[i : i + 1, :] for i in range(3)]
    own = packed([row[:, :tokens] for row in early], extra_ref[...])
    beyond = [jnp.concatenate([row[:, tokens:], late], axis=1) for row, late in zip(early, state)]
    beyond = packed(beyond, extra_ref[...])
    mine = lax.div(lax.rem(lax.axis_index("grp"), groups // 2), 2)
    for which in range(groups // 4):
        block = jnp.where(mine == which, own, beyond)
        for group in range(groups):
            if group % (groups // 2) // 2 == which:
                for shard in range(shards):
                    out_ref[group * shards + shard] = block


def score(kernel, out_shape, targets, heads, extras, count, scratch=True, scalars=()):
    vocab, width = heads[0].shape
    return call(
        kernel,
        out_shape,
        [SCALARS] * len(scalars) + [WHOLE] * (3 + len(extras)),
        4 * vocab * count * width,
        4 * vocab * width + 2 * count * width,
        out_specs=WHOLE,
        scratch_shapes=[pltpu.VMEM((count, width), jnp.bfloat16)] if scratch else [],
    )(*scalars, targets, *heads, *extras)


def upright(row):
    count = row.shape[1]
    diagonal = lax.broadcasted_iota(jnp.int32, (count, count), 0) == lax.broadcasted_iota(
        jnp.int32, (count, count), 1
    )
    return jnp.sum(jnp.where(diagonal, row, 0), axis=1, keepdims=True)


def side_kernel(
    sizes,
    swapped,
    lengths_ref,
    rows_ref,
    positions_ref,
    segments_ref,
    ids_ref,
    gain_ref,
    input_hbm,
    weight_hbm,
    turned_ref,
    extra_ref,
    early_ref,
    late_ref,
    input_ref,
    weight_ref,
    semaphores,
):
    groups, shards = sizes
    copies = fetch((input_hbm, weight_hbm), (input_ref, weight_ref), semaphores)
    cap = segments_ref.shape[1]
    if swapped:
        tokens = (early_ref.shape[1] + late_ref.shape[1]) // 2
        half, size = groups // 2, 2 * BAL // shards
        group, y, core = place_of(shards)
        lane = lax.broadcasted_iota(jnp.int32, (1, 2 * tokens), 1)
        row = jnp.zeros((1, 2 * tokens), jnp.int32)
        source = jnp.zeros((1, 2 * tokens), jnp.int32)
        for slot in range(8):
            place = lane - slot * size
            lower = lax.rem(group, half) ^ (slot // 4 * 2) ^ (slot // 2 % 2)
            quarter = (y ^ (slot % 2)) * CORES + core
            is_lower = place < front(lengths_ref[lower], quarter, shards)
            here = (place >= 0) & (place < size)
            stands = jnp.where(
                is_lower, shards * place + quarter, shards * (size - 1 - place) + shards - 1 - quarter
            )
            row = jnp.where(here, stands, row)
            source = jnp.where(here, jnp.where(is_lower, lower, lower + half), source)
        ids = jnp.concatenate([ids_ref[0:1, g * cap : (g + 1) * cap] for g in range(groups)], axis=0)
        halves = jnp.concatenate([ids >> 8, ids & 255], axis=0)
        stood = lax.broadcasted_iota(jnp.int32, (cap, 2 * tokens), 0)
        pick = (stood == row).astype(jnp.float32).astype(jnp.bfloat16)
        found = jnp.dot(
            halves.astype(jnp.float32).astype(jnp.bfloat16), pick, preferred_element_type=jnp.float32
        )
        found = found[:groups] * 256.0 + found[groups:]
        of_group = lax.broadcasted_iota(jnp.int32, found.shape, 0) == source
        targets = jnp.sum(jnp.where(of_group, found, 0.0), axis=0, keepdims=True).astype(jnp.int32)
        early_ref[...] = targets[:, : early_ref.shape[1]]
        late_ref[...] = targets[:, early_ref.shape[1] :]
    else:
        early_ref[...] = jnp.zeros_like(early_ref)
        late_ref[...] = jnp.zeros_like(late_ref)

    count, width = turned_ref.shape
    column = lax.broadcasted_iota(jnp.int32, (count, cap), 1)
    chosen = column == upright(rows_ref[...])
    places = jnp.sum(jnp.where(chosen, positions_ref[...], 0), axis=1, keepdims=True)
    half_head = HD // 2
    steps = lax.broadcasted_iota(jnp.int32, (count, half_head), 1).astype(jnp.float32)
    freqs = jnp.exp(-(2.0 * steps / HD) * jnp.log(jnp.full(steps.shape, ROPE_BASE, jnp.float32)))
    angles = places.astype(jnp.float32) * freqs
    cosine, sine = jnp.cos(angles), jnp.sin(angles)
    cosine = jnp.concatenate([cosine, cosine], axis=1)
    sine = jnp.concatenate([-sine, sine], axis=1)
    for copy in copies:
        copy.wait()
    pick = chosen.astype(jnp.float32).astype(jnp.bfloat16)
    rows = jnp.dot(pick, input_ref[...], preferred_element_type=jnp.float32).astype(jnp.bfloat16)
    projected = jnp.dot(rows, weight_ref[...], preferred_element_type=jnp.float32)
    squares = jnp.sum(projected * projected, axis=1, keepdims=True)
    lane = lax.broadcasted_iota(jnp.int32, (count, extra_ref.shape[1]), 1)
    diagonal = lax.broadcasted_iota(jnp.int32, lane.shape, 0) == lane
    extra = jnp.sum(jnp.where(diagonal, squares, 0.0), axis=0, keepdims=True)
    for label in range(1, SEGS):
        before = (segments_ref[...] < label).astype(jnp.float32)
        before = jnp.sum(before, axis=1, keepdims=True)
        extra = jnp.where(lane[0:1] == BREAKS + label, before, extra)
    extra_ref[...] = extra
    gained = projected * gain_ref[...]
    for start in range(0, width, HD):
        head = gained[:, start : start + HD]
        turned_ref[:, start : start + HD] = head * cosine + pltpu.roll(head, half_head, 1) * sine


def combine(tops, expsums, moments, pickeds):
    top = jnp.max(tops, axis=0)
    scale = jnp.exp(tops - top[None])
    return (
        top,
        jnp.sum(expsums * scale, axis=0),
        jnp.sum(moments * scale, axis=0),
        jnp.sum(pickeds, axis=0),
    )


def final_kernel(
    sizes,
    swapped,
    lengths_ref,
    continues_ref,
    got_ref,
    segments_ref,
    turned_ref,
    logprob_ref,
    entropy_ref,
    mean_ref,
    keys_ref,
):
    groups, shards = sizes
    parts, group = shards // CORES, lax.axis_index("grp")
    cap = segments_ref.shape[1]
    size = 2 * BAL // shards
    tokens = 2 * parts * size
    columns = []
    for core in range(CORES):
        if swapped:
            whole = []
            for x in range(2):
                for y in range(parts):
                    lse, mean, picked = unpacked(got_ref[:, x, y, core])
                    merged = combine(lse, jnp.ones_like(lse), mean, picked)
                    blocks = [(x * parts + y) ^ slot for slot in range(2 * parts)]
                    rows = jnp.concatenate(merged, axis=0)
                    rows = [rows[:, b * size : (b + 1) * size] for b in blocks]
                    whole.append(jnp.concatenate(rows, axis=1))
            whole = jnp.stack(whole)
            merged = combine(*(whole[:, i : i + 1, :] for i in range(4)))
        else:
            every = got_ref[:, :, :, core]
            every = every.reshape((groups * parts,) + every.shape[3:])
            lse, mean, picked = unpacked(every)
            merged = combine(lse, jnp.ones_like(lse), mean, picked)
        top, expsum, moment, picked = merged
        lse = top + jnp.log(expsum)
        columns.append(jnp.concatenate([picked - lse, lse - moment / expsum], axis=0))

    column, span = lax.rem(group, 2), tokens // 2
    halves = [[both[:, :span], both[:, span:]] for both in columns]
    own = jnp.concatenate([jnp.where(column == 0, a, b) for a, b in halves], axis=1)
    beside = jnp.concatenate([jnp.where(column == 0, b, a) for a, b in halves], axis=1)
    rest = jnp.concatenate([own, beside], axis=0)
    terms = []
    for _ in range(3):
        term = rest.astype(jnp.bfloat16).astype(jnp.float32)
        terms.append(term)
        rest = rest - term
    terms = jnp.concatenate(terms + [jnp.zeros_like(rest)], axis=0).astype(jnp.bfloat16)

    slots = lax.broadcasted_iota(jnp.int32, (1, cap), 1)
    is_first = group < groups // 2
    quarter = jnp.where(is_first, slots % shards, shards - 1 - slots % shards)
    place = jnp.where(is_first, slots // shards, size - 1 - slots // shards)
    home = quarter % CORES * span + quarter // CORES * size + place
    stood = lax.broadcasted_iota(jnp.int32, (CORES * span, cap), 0)
    pick = (stood == home).astype(jnp.float32).astype(jnp.bfloat16)
    found = jnp.dot(terms, pick, preferred_element_type=jnp.float32)
    found = found[0:4] + found[4:8] + found[8:12]
    labels = lax.broadcasted_iota(jnp.int32, (1, SEGS), 1)

    def summed(who, logprob, breaks):
        live = slots < lengths_ref[who]
        logprob = jnp.where(live, logprob, 0.0)
        sums = jnp.zeros((1, SEGS), jnp.float32)
        counts = jnp.zeros((1, SEGS), jnp.float32)
        for label in range(SEGS):
            member = live
            if label > 0:
                member = member & (slots >= breaks[label - 1])
            if label < SEGS - 1:
                member = member & (slots < breaks[label])
            one_sum = jnp.sum(jnp.where(member, logprob, 0.0), axis=1, keepdims=True)
            one_count = jnp.sum(member.astype(jnp.float32), axis=1, keepdims=True)
            sums = jnp.where(labels == label, one_sum, sums)
            counts = jnp.where(labels == label, one_count, counts)
        return logprob, sums, counts

    partner = group ^ 1
    messages = [got_ref[who // 2, who % 2, 0, 0][7:8, LANES // 2 :] for who in (group, partner)]
    breaks = [
        [message[:, BREAKS + i : BREAKS + i + 1].astype(jnp.int32) for i in range(1, SEGS)]
        for message in messages
    ]
    logprob, sums, counts = summed(group, found[0:1], breaks[0])
    _, partner_sums, partner_counts = summed(partner, found[2:3], breaks[1])
    entropy = jnp.where(slots < lengths_ref[group], found[1:2], 0.0)
    segments = segments_ref[...]
    is_even = group % 2 == 0
    joined = jnp.where(is_even, continues_ref[group], continues_ref[partner]) == 1
    last = slots == lengths_ref[group] - 1
    my_last = jnp.sum(jnp.where(last, segments, 0), axis=1, keepdims=True)
    partner_last = jnp.max(jnp.where(partner_counts > 0, labels, 0), axis=1, keepdims=True)
    wanted = jnp.where(is_even, jnp.zeros_like(partner_last), partner_last)
    extra_sum = jnp.sum(jnp.where(labels == wanted, partner_sums, 0.0), axis=1, keepdims=True)
    extra_count = jnp.sum(jnp.where(labels == wanted, partner_counts, 0.0), axis=1, keepdims=True)
    target = jnp.where(is_even, my_last, jnp.zeros_like(my_last))
    update = joined & (labels == target)
    total_sum = sums + jnp.where(update, extra_sum, 0.0)
    total_count = counts + jnp.where(update, extra_count, 0.0)
    logprob_ref[...] = logprob
    entropy_ref[...] = entropy
    mean_ref[...] = total_sum / jnp.maximum(total_count, 1.0)

    count, width = turned_ref.shape
    squares = jnp.zeros((1, count), jnp.float32)
    for part in range(parts):
        for core in range(CORES):
            squares += got_ref[group // 2, group % 2, part, core][7:8, LANES // 2 : LANES // 2 + count]
    squares = upright(squares)
    scale = jnp.sqrt(squares / (width * shards) + NORM_EPS)
    keys_ref[...] = (turned_ref[...] / scale).astype(jnp.bfloat16)


def partners(sizes, flips):
    (groups, shards), (group_flip, shard_flip) = sizes, flips
    return [
        (g * shards + v, (g ^ group_flip) * shards + (v ^ shard_flip))
        for g in range(groups)
        for v in range(shards)
    ]


def local(
    sizes,
    final_hidden,
    norm_gain,
    head_weight,
    token_ids,
    group_lengths,
    segment_ids,
    continues,
    layer_input,
    key_weight,
    key_gain,
    positions,
    key_rows,
):
    groups, shards = sizes
    parts, half = shards // CORES, groups // 2
    cap, width = final_hidden.shape
    rows = cap // shards
    size = 2 * BAL // shards
    tokens = 2 * parts * size
    core = lax.axis_index("vocab") % CORES
    axes = ("grp", "vocab")
    swapped = sizes == (8, 4)

    def swap(array, group_flip, shard_flip):
        return lax.ppermute(array, axes, partners(sizes, (group_flip, shard_flip)))

    def merge(own, other, flips):
        return call(
            functools.partial(merge_kernel, sizes, flips),
            jax.ShapeDtypeStruct((size, width), jnp.bfloat16),
            [SCALARS, WHOLE, WHOLE],
            size * width,
            4 * size * width,
            out_specs=WHOLE,
        )(group_lengths, own, other)

    def prep(shape, *known):
        return call(
            functools.partial(prep_kernel, sizes),
            jax.ShapeDtypeStruct(shape, jnp.bfloat16),
            [WHOLE] * (2 + len(known)),
            2 * rows * cap * width,
            4 * cap * width,
            out_specs=WHOLE,
        )(final_hidden, norm_gain.reshape(1, width), *known)

    here = prep((rows, width))
    count, key_width = key_rows.shape[0], key_weight.shape[1]
    turned, extra, early_ids, late_ids = call(
        functools.partial(side_kernel, sizes, swapped),
        (
            jax.ShapeDtypeStruct((count, key_width), jnp.float32),
            jax.ShapeDtypeStruct((1, LANES // 2), jnp.float32),
            jax.ShapeDtypeStruct((1, tokens + size), jnp.int32),
            jax.ShapeDtypeStruct((1, tokens - size), jnp.int32),
        ),
        [SCALARS] + [WHOLE] * 5 + [FAR, FAR],
        2 * count * width * key_width,
        2 * width * key_width,
        scratch_shapes=[
            pltpu.VMEM(layer_input.shape, jnp.bfloat16),
            pltpu.VMEM(key_weight.shape, jnp.bfloat16),
            pltpu.SemaphoreType.DMA((2,)),
        ],
    )(
        group_lengths,
        key_rows.reshape(1, count),
        positions.reshape(1, cap),
        segment_ids.reshape(1, cap),
        token_ids.reshape(1, groups * cap),
        key_gain.reshape(1, key_width),
        layer_input,
        key_weight,
    )

    far_head = swap(head_weight, 0, 1)
    heads = (head_weight, far_head)
    sent_shape = jax.ShapeDtypeStruct((groups * shards, 8, LANES), jnp.float32)
    if swapped:
        other = swap(here, 4, 0)
        dealt = prep((parts, rows, width), here)
        across = swap(dealt, 1, 0)
        other, across, far_head, early_ids, late_ids, extra, turned = lax.optimization_barrier(
            (other, across, far_head, early_ids, late_ids, extra, turned)
        )
        heads = (head_weight, far_head)
        own = merge(here, other, (0, 0))
        other_xy = swap(other, 1, 2)
        far_own = swap(own, 2, 0)
        other_x = swap(other, 1, 0)
        other_y = swap(other, 0, 2)
        own_xy = merge(across, other_xy, (1, 1))
        far_x = swap(far_own, 1, 0)
        far_y = swap(far_own, 0, 2)
        far_xy = swap(own_xy, 2, 0)
        early = score(
            functools.partial(early_kernel, sizes),
            jax.ShapeDtypeStruct((8, tokens + size), jnp.float32),
            early_ids,
            heads,
            (own, dealt, other_y, across, other_x, own_xy, far_own),
            tokens + size,
            scalars=(group_lengths,),
        )
        sent = score(
            functools.partial(send_kernel, sizes),
            sent_shape,
            late_ids,
            heads,
            (early, extra, far_y, far_x, far_xy),
            tokens - size,
        )
    else:
        gap = size - rows
        taken = front(group_lengths[:half, None], jnp.arange(shards)[None, :], shards)
        ids = token_ids.reshape(groups, rows, shards).transpose(0, 2, 1)
        lower = jnp.pad(ids[:half], ((0, 0), (0, 0), (0, gap)))
        upper = jnp.pad(ids[half:, ::-1, ::-1], ((0, 0), (0, 0), (gap, 0)))
        is_lower = jnp.arange(size)[None, None, :] < taken[:, :, None]
        ids = jnp.where(is_lower, lower, upper).reshape(half, parts, CORES, size)
        ids = lax.dynamic_index_in_dim(ids, core, 2, False).reshape(1, -1)
        every = lax.all_gather(here, axes).reshape(groups, parts, CORES, rows, width)
        every = lax.dynamic_index_in_dim(every, core, 2, False)
        first = jnp.pad(every[:half], ((0, 0), (0, 0), (0, gap), (0, 0)))
        second = jnp.pad(every[half:], ((0, 0), (0, 0), (gap, 0), (0, 0)))
        is_lower = is_lower.reshape(half, parts, CORES, size)
        is_lower = lax.dynamic_index_in_dim(is_lower, core, 2, False)
        every = jnp.where(is_lower[..., None], first, second)
        stats = score(
            functools.partial(plain_kernel, sizes),
            jax.ShapeDtypeStruct((8, half // 2 * tokens), jnp.float32),
            ids,
            heads,
            (every.reshape(-1, width),),
            half // 2 * tokens,
            scratch=False,
        )
        sets = half // 2
        state = [row.reshape(sets, tokens) for row in stats[:3]]
        extra = jnp.broadcast_to(extra, (sets, LANES // 2))
        stats = packed(state, extra).reshape(8, sets, LANES).transpose(1, 0, 2)
        sent = jnp.broadcast_to(
            stats[None, :, None, None], (2, sets, 2, shards, 8, LANES)
        ).reshape(sent_shape.shape)
    got = lax.all_to_all(sent, axes, 0, 0, tiled=False)

    logprob, entropy, means, keys = call(
        functools.partial(final_kernel, sizes, swapped),
        (
            jax.ShapeDtypeStruct((1, cap), jnp.float32),
            jax.ShapeDtypeStruct((1, cap), jnp.float32),
            jax.ShapeDtypeStruct((1, SEGS), jnp.float32),
            jax.ShapeDtypeStruct((count, key_width), jnp.bfloat16),
        ),
        [SCALARS] * 2 + [WHOLE] * 3,
        1 << 24,
        4 * groups * shards * 8 * LANES,
    )(
        group_lengths,
        continues,
        got.reshape(half, 2, parts, CORES, 8, LANES),
        segment_ids.reshape(1, cap),
        turned,
    )
    return logprob.reshape(cap), entropy.reshape(cap), means.reshape(SEGS), keys


def solution(mesh):
    sizes = (mesh.shape["grp"], mesh.shape["vocab"])
    in_specs = (
        P("grp", None),
        P(),
        P(("vocab", "grp"), None),
        P(),
        P(),
        P("grp"),
        P(),
        P("grp", None),
        P(None, "vocab"),
        P("vocab"),
        P("grp"),
        P("grp"),
    )
    out_specs = (P("grp"), P("grp"), P("grp"), P("grp", "vocab"))
    return jax.shard_map(
        functools.partial(local, sizes),
        mesh=mesh,
        in_specs=in_specs,
        out_specs=out_specs,
        check_vma=False,
    )
```

```python
import functools

import jax
import jax.numpy as jnp
from jax import lax
from jax.experimental import pallas as pl
from jax.experimental.pallas import tpu as pltpu
from jax.sharding import PartitionSpec as P

HD = 128
SEGS = 4
BAL = 160
CORES = 2
LANES = 128
BREAKS = 31
SLOTS = (0, 3, 4, 1, 2, 5, 6, 7)

NORM_EPS = 1e-06
ROPE_BASE = 500000.0

VMEM_LIMIT = 24 * 1024 * 1024
WHOLE = pl.BlockSpec(memory_space=pltpu.VMEM)
SCALARS = pl.BlockSpec(memory_space=pltpu.SMEM)
FAR = pl.BlockSpec(memory_space=pltpu.HBM)


def call(kernel, out_shape, in_specs, flops, moved, vmem=VMEM_LIMIT, **more):
    return pl.pallas_call(
        kernel,
        out_shape=out_shape,
        in_specs=in_specs,
        compiler_params=pltpu.CompilerParams(vmem_limit_bytes=vmem),
        cost_estimate=pl.CostEstimate(flops=flops, bytes_accessed=moved, transcendentals=0),
        **more,
    )


def place_of(shards):
    shard = lax.axis_index("vocab")
    return lax.axis_index("grp"), lax.div(shard, CORES), lax.rem(shard, CORES)


def source_row(place, quarter, is_first, quarters, rows):
    return jnp.where(
        is_first,
        quarters * place + quarter,
        quarters * (rows - 1 - place) + quarters - 1 - quarter,
    )


def front(length, quarter, shards):
    return lax.div(length - quarter + shards - 1, shards)


def fetch(sources, targets, semaphores):
    copies = [
        pltpu.make_async_copy(source, target, semaphores.at[i])
        for i, (source, target) in enumerate(zip(sources, targets))
    ]
    for copy in copies:
        copy.start()
    return copies


def dealt(sizes, hidden_ref, gain_ref, t, rows, turned):
    groups, shards = sizes
    group, y, core = place_of(shards)
    is_first = group < groups // 2
    count = hidden_ref.shape[0] // shards
    place = lax.broadcasted_iota(jnp.int32, (rows, hidden_ref.shape[0]), 0)
    column = lax.broadcasted_iota(jnp.int32, place.shape, 1)
    if turned:
        gap = 2 * BAL // shards - count
        back = jnp.where(place < gap, place + (count - gap), place - gap)
        place = jnp.where(is_first, place, back)
    row = source_row(place, (y ^ t) * CORES + core, is_first, shards, count)
    pick = (column == row).astype(jnp.float32).astype(jnp.bfloat16)
    found = jnp.dot(pick, hidden_ref[...], preferred_element_type=jnp.float32)
    meansq = jnp.sum(found * found, axis=-1, keepdims=True) / found.shape[1]
    return (found * lax.rsqrt(meansq + NORM_EPS) * gain_ref[...]).astype(jnp.bfloat16)


def prep_kernel(sizes, turned, hidden_ref, gain_ref, out_ref):
    out_ref[...] = dealt(sizes, hidden_ref, gain_ref, 0, out_ref.shape[0], turned)


def ends_kernel(sizes, hidden_ref, gain_ref, here_ref, out_ref):
    rows = out_ref.shape[1]
    out_ref[0] = here_ref[0:rows, :]
    for t in range(1, out_ref.shape[0]):
        out_ref[t] = dealt(sizes, hidden_ref, gain_ref, t, rows, True)


def mix_kernel(sizes, lengths_ref, here_ref, other_ref, out_ref):
    groups, shards = sizes
    half = groups // 2
    group, y, core = place_of(shards)
    rows, width = here_ref.shape
    gap = 2 * BAL // shards - rows
    length = front(lengths_ref[lax.rem(group, half)], y * CORES + core, shards)
    is_lower = lax.broadcasted_iota(jnp.int32, (rows - gap, width), 0) + gap < length

    def lay(lower_ref, upper_ref):
        lower, upper = (ref[gap:rows, :].astype(jnp.float32) for ref in (lower_ref, upper_ref))
        out_ref[0 : rows - gap, :] = jnp.where(is_lower, lower, upper).astype(jnp.bfloat16)

    @pl.when(group < half)
    def _():
        lay(here_ref, other_ref)

    @pl.when(group >= half)
    def _():
        lay(other_ref, here_ref)

    out_ref[rows - gap : rows, :] = other_ref[0:gap, :]


def gather_pieces(pieces, tokens_ref):
    start = 0
    for end, rest_ref in pieces:
        gap, rows = end.shape[0], rest_ref.shape[0]
        tokens_ref[start : start + gap, :] = end[...]
        tokens_ref[start + gap : start + gap + rows, :] = rest_ref[...]
        start += gap + rows
    return tokens_ref[...]


def statistics(bases, targets, tokens, heads):
    state = None
    for base, head_ref in zip(bases, heads):
        logits = lax.dot_general(
            head_ref[...], tokens, (((1,), (1,)), ((), ())), preferred_element_type=jnp.float32
        )
        logits = logits.astype(jnp.bfloat16).astype(jnp.float32)
        entry = lax.broadcasted_iota(jnp.int32, logits.shape, 0)
        found = jnp.where(entry == targets - base, logits, 0.0)
        picked = jnp.sum(found, axis=0, keepdims=True)
        top = jnp.max(logits, axis=0, keepdims=True)
        if state is not None:
            top = jnp.maximum(top, state[0])
        shifted = jnp.exp(logits - top)
        expsum = jnp.sum(shifted, axis=0, keepdims=True)
        moment = jnp.sum(shifted * logits, axis=0, keepdims=True)
        if state is not None:
            scale = jnp.exp(state[0] - top)
            expsum += state[1] * scale
            moment += state[2] * scale
            picked += state[3]
        state = (top, expsum, moment, picked)
    top, expsum, moment, picked = state
    return top + jnp.log(expsum), moment / expsum, picked


def packed(state, extra):
    flat = [row[:, : 2 * LANES] for row in state] + [row[:, 2 * LANES :] for row in state] + [extra]
    flat = jnp.concatenate(flat, axis=1)
    return jnp.concatenate(
        [flat[:, i : i + LANES] for i in range(0, flat.shape[1], LANES)], axis=0
    )


def merged(every):
    half = LANES // 2
    row = lax.broadcasted_iota(jnp.int32, every.shape[1:], 0)
    top = jnp.max(every, axis=0)
    scale = jnp.exp(every - top[None])
    means = [
        jnp.where(row == 6, pltpu.roll(one, half, 1), pltpu.roll(one, one.shape[0] - 2, 0))
        for one in (every[i] for i in range(every.shape[0]))
    ]
    expsum = jnp.sum(scale, axis=0)
    moment = sum(scale[i] * mean for i, mean in enumerate(means))
    picked = jnp.sum(every, axis=0)
    lse = top + jnp.log(expsum)
    entropy = lse - moment / expsum

    def lay(block, first, last):
        return jnp.concatenate([block[first : first + 1], block[first + 1 : first + 2], last], axis=1)

    lse_row = lay(lse, 0, lse[6:7, :half])
    return jnp.concatenate(
        [lay(picked, 4, picked[7:8, :half]) - lse_row, lay(entropy, 0, entropy[6:7, :half])], axis=0
    )


def bases_of(sizes, head_ref):
    groups, shards = sizes
    group, shard = lax.axis_index("grp"), lax.axis_index("vocab")
    return [((shard ^ flip) * groups + group) * head_ref.shape[0] for flip in (0, 1)]


def rows_of(state, out_ref):
    rows = jnp.concatenate([*state, jnp.zeros((5, out_ref.shape[1]), jnp.float32)], axis=0)
    out_ref[...] = rows


def plain_kernel(sizes, targets_ref, near_ref, far_ref, tokens_ref, out_ref):
    state = statistics(
        bases_of(sizes, near_ref), targets_ref[...], tokens_ref[...], (near_ref, far_ref)
    )
    rows_of(state, out_ref)


def piece_kernel(sizes, picks, targets_ref, near_ref, far_ref, *refs):
    *pieces, out_ref, tokens_ref = refs
    ends = [ref.at[which] for ref, which in zip(pieces, picks)]
    tokens = gather_pieces(zip(ends, pieces[len(picks) :]), tokens_ref)
    state = statistics(bases_of(sizes, near_ref), targets_ref[...], tokens, (near_ref, far_ref))
    rows_of(state, out_ref)


def send_kernel(
    sizes, targets_ref, near_ref, far_ref, first_ref, second_ref, extra_ref, beyond_ref, corner_ref, *refs
):
    *rests, out_ref, tokens_ref = refs
    groups, shards = sizes
    size = 2 * BAL // shards
    ends = (beyond_ref.at[1], corner_ref.at[0], corner_ref.at[1])
    tokens = gather_pieces(zip(ends, rests), tokens_ref)
    state = statistics(bases_of(sizes, near_ref), targets_ref[...], tokens, (near_ref, far_ref))
    group, y, _ = place_of(shards)
    gap = beyond_ref.shape[1]

    def settled(rows):
        blocks = [rows[:, i * size : (i + 1) * size] for i in range(4)]
        blocks = [
            jnp.concatenate([b[:, size - gap :], b[:, gap : size - gap], b[:, :gap]], axis=1) for b in blocks
        ]
        rows = jnp.where(group < groups // 2, rows, jnp.concatenate(blocks, axis=1))
        turned = jnp.concatenate([rows[:, 2 * size :], rows[:, : 2 * size]], axis=1)
        rows = jnp.where(lax.rem(group, 2) == 1, turned, rows)
        quarters = [rows[:, i * size : (i + 1) * size] for i in (1, 0, 3, 2)]
        return jnp.where(y == 1, jnp.concatenate(quarters, axis=1), rows)

    first, second = first_ref[0:4, :], second_ref[0:4, :]
    third = jnp.concatenate([*state, jnp.zeros_like(state[0])], axis=0)
    own = settled(jnp.concatenate([first[:, :size], second, first[:, size : 2 * size]], axis=1))
    beyond = settled(jnp.concatenate([first[:, 2 * size :], third], axis=1))
    own, beyond = (
        packed([rows[i : i + 1] for i in range(3)], extra_ref[...]) for rows in (own, beyond)
    )
    mine = lax.div(lax.rem(group, groups // 2), 2)
    for which in range(groups // 4):
        block = jnp.where(mine == which, own, beyond)
        for group in range(groups):
            if group % (groups // 2) // 2 == which:
                for shard in range(shards):
                    out_ref[group * shards + shard] = block


def score(kernel, out_shape, targets, heads, extras, count, scratch=True):
    vocab, width = heads[0].shape
    return call(
        kernel,
        out_shape,
        [WHOLE] * (3 + len(extras)),
        4 * vocab * count * width,
        4 * vocab * width + 2 * count * width,
        out_specs=WHOLE,
        scratch_shapes=[pltpu.VMEM((count, width), jnp.bfloat16)] if scratch else [],
    )(targets, *heads, *extras)


def upright(row):
    count = row.shape[1]
    diagonal = lax.broadcasted_iota(jnp.int32, (count, count), 0) == lax.broadcasted_iota(
        jnp.int32, (count, count), 1
    )
    return jnp.sum(jnp.where(diagonal, row, 0), axis=1, keepdims=True)


def side_kernel(
    sizes,
    swapped,
    lengths_ref,
    rows_ref,
    positions_ref,
    segments_ref,
    ids_ref,
    gain_ref,
    input_hbm,
    weight_hbm,
    turned_ref,
    extra_ref,
    first_ref,
    second_ref,
    third_ref,
    input_ref,
    weight_ref,
    semaphores,
):
    groups, shards = sizes
    copies = fetch((input_hbm, weight_hbm), (input_ref, weight_ref), semaphores)
    cap = segments_ref.shape[1]
    if swapped:
        tokens = first_ref.shape[1] + second_ref.shape[1] // 2
        half, size = groups // 2, 2 * BAL // shards
        group, y, core = place_of(shards)
        lane = lax.broadcasted_iota(jnp.int32, (1, 2 * tokens), 1)
        row = jnp.zeros((1, 2 * tokens), jnp.int32)
        source = jnp.zeros((1, 2 * tokens), jnp.int32)
        for start, slot in enumerate(SLOTS):
            place = lane - start * size
            here = (place >= 0) & (place < size)
            gap = size - cap // shards
            back = jnp.where(place < gap, place + size - gap, place - (size - gap))
            back = jnp.where((place >= gap) & (place < size - gap), place, back)
            place = jnp.where(group < half, place, back)
            lower = lax.rem(group, half) ^ (slot // 4 * 2) ^ (slot // 2 % 2)
            quarter = (y ^ (slot % 2)) * CORES + core
            is_lower = place < front(lengths_ref[lower], quarter, shards)
            stands = jnp.where(
                is_lower, shards * place + quarter, shards * (size - 1 - place) + shards - 1 - quarter
            )
            row = jnp.where(here, stands, row)
            source = jnp.where(here, jnp.where(is_lower, lower, lower + half), source)
        ids = jnp.concatenate([ids_ref[0:1, g * cap : (g + 1) * cap] for g in range(groups)], axis=0)
        halves = jnp.concatenate([ids >> 8, ids & 255], axis=0)
        stood = lax.broadcasted_iota(jnp.int32, (cap, 2 * tokens), 0)
        pick = (stood == row).astype(jnp.float32).astype(jnp.bfloat16)
        found = jnp.dot(
            halves.astype(jnp.float32).astype(jnp.bfloat16), pick, preferred_element_type=jnp.float32
        )
        found = found[:groups] * 256.0 + found[groups:]
        of_group = lax.broadcasted_iota(jnp.int32, found.shape, 0) == source
        targets = jnp.sum(jnp.where(of_group, found, 0.0), axis=0, keepdims=True).astype(jnp.int32)
        start = 0
        for ref in (first_ref, second_ref, third_ref):
            ref[...] = targets[:, start : start + ref.shape[1]]
            start += ref.shape[1]
    else:
        for ref in (first_ref, second_ref, third_ref):
            ref[...] = jnp.zeros_like(ref)

    count, width = turned_ref.shape
    column = lax.broadcasted_iota(jnp.int32, (count, cap), 1)
    chosen = column == upright(rows_ref[...])
    places = jnp.sum(jnp.where(chosen, positions_ref[...], 0), axis=1, keepdims=True)
    half_head = HD // 2
    steps = lax.broadcasted_iota(jnp.int32, (count, half_head), 1).astype(jnp.float32)
    freqs = jnp.exp(-(2.0 * steps / HD) * jnp.log(jnp.full(steps.shape, ROPE_BASE, jnp.float32)))
    angles = places.astype(jnp.float32) * freqs
    cosine, sine = jnp.cos(angles), jnp.sin(angles)
    cosine = jnp.concatenate([cosine, cosine], axis=1)
    sine = jnp.concatenate([-sine, sine], axis=1)
    for copy in copies:
        copy.wait()
    pick = chosen.astype(jnp.float32).astype(jnp.bfloat16)
    rows = jnp.dot(pick, input_ref[...], preferred_element_type=jnp.float32).astype(jnp.bfloat16)
    projected = jnp.dot(rows, weight_ref[...], preferred_element_type=jnp.float32)
    squares = jnp.sum(projected * projected, axis=1, keepdims=True)
    lane = lax.broadcasted_iota(jnp.int32, (count, extra_ref.shape[1]), 1)
    diagonal = lax.broadcasted_iota(jnp.int32, lane.shape, 0) == lane
    extra = jnp.sum(jnp.where(diagonal, squares, 0.0), axis=0, keepdims=True)
    for label in range(1, SEGS):
        before = (segments_ref[...] < label).astype(jnp.float32)
        before = jnp.sum(before, axis=1, keepdims=True)
        extra = jnp.where(lane[0:1] == BREAKS + label, before, extra)
    extra_ref[...] = extra
    gained = projected * gain_ref[...]
    for start in range(0, width, HD):
        head = gained[:, start : start + HD]
        turned_ref[:, start : start + HD] = head * cosine + pltpu.roll(head, half_head, 1) * sine


def final_kernel(
    sizes,
    lengths_ref,
    continues_ref,
    got_ref,
    segments_ref,
    turned_ref,
    logprob_ref,
    entropy_ref,
    mean_ref,
    keys_ref,
):
    groups, shards = sizes
    parts, group = shards // CORES, lax.axis_index("grp")
    cap = segments_ref.shape[1]
    size = 2 * BAL // shards
    tokens = 2 * parts * size
    columns = [merged(got_ref[:, core]) for core in range(CORES)]

    column, span = lax.rem(group, 2), tokens // 2
    halves = [[both[:, :span], both[:, span:]] for both in columns]
    own = jnp.concatenate([jnp.where(column == 0, a, b) for a, b in halves], axis=1)
    beside = jnp.concatenate([jnp.where(column == 0, b, a) for a, b in halves], axis=1)
    rest = jnp.concatenate([own, beside], axis=0)
    terms = []
    for _ in range(3):
        term = rest.astype(jnp.bfloat16).astype(jnp.float32)
        terms.append(term)
        rest = rest - term
    terms = jnp.concatenate(terms + [jnp.zeros_like(rest)], axis=0).astype(jnp.bfloat16)

    slots = lax.broadcasted_iota(jnp.int32, (1, cap), 1)
    is_first = group < groups // 2
    quarter = jnp.where(is_first, slots % shards, shards - 1 - slots % shards)
    place = jnp.where(is_first, slots // shards, size - 1 - slots // shards)
    home = quarter % CORES * span + quarter // CORES * size + place
    stood = lax.broadcasted_iota(jnp.int32, (CORES * span, cap), 0)
    pick = (stood == home).astype(jnp.float32).astype(jnp.bfloat16)
    found = jnp.dot(terms, pick, preferred_element_type=jnp.float32)
    found = found[0:4] + found[4:8] + found[8:12]
    labels = lax.broadcasted_iota(jnp.int32, (1, SEGS), 1)

    def summed(who, logprob, breaks):
        live = slots < lengths_ref[who]
        logprob = jnp.where(live, logprob, 0.0)
        sums = jnp.zeros((1, SEGS), jnp.float32)
        counts = jnp.zeros((1, SEGS), jnp.float32)
        for label in range(SEGS):
            member = live
            if label > 0:
                member = member & (slots >= breaks[label - 1])
            if label < SEGS - 1:
                member = member & (slots < breaks[label])
            one_sum = jnp.sum(jnp.where(member, logprob, 0.0), axis=1, keepdims=True)
            one_count = jnp.sum(member.astype(jnp.float32), axis=1, keepdims=True)
            sums = jnp.where(labels == label, one_sum, sums)
            counts = jnp.where(labels == label, one_count, counts)
        return logprob, sums, counts

    partner = group ^ 1
    messages = [got_ref[who * parts, 0][7:8, LANES // 2 :] for who in (group, partner)]
    breaks = [
        [message[:, BREAKS + i : BREAKS + i + 1].astype(jnp.int32) for i in range(1, SEGS)]
        for message in messages
    ]
    logprob, sums, counts = summed(group, found[0:1], breaks[0])
    _, partner_sums, partner_counts = summed(partner, found[2:3], breaks[1])
    entropy = jnp.where(slots < lengths_ref[group], found[1:2], 0.0)
    segments = segments_ref[...]
    is_even = group % 2 == 0
    joined = jnp.where(is_even, continues_ref[group], continues_ref[partner]) == 1
    last = slots == lengths_ref[group] - 1
    my_last = jnp.sum(jnp.where(last, segments, 0), axis=1, keepdims=True)
    partner_last = jnp.max(jnp.where(partner_counts > 0, labels, 0), axis=1, keepdims=True)
    wanted = jnp.where(is_even, jnp.zeros_like(partner_last), partner_last)
    extra_sum = jnp.sum(jnp.where(labels == wanted, partner_sums, 0.0), axis=1, keepdims=True)
    extra_count = jnp.sum(jnp.where(labels == wanted, partner_counts, 0.0), axis=1, keepdims=True)
    target = jnp.where(is_even, my_last, jnp.zeros_like(my_last))
    update = joined & (labels == target)
    total_sum = sums + jnp.where(update, extra_sum, 0.0)
    total_count = counts + jnp.where(update, extra_count, 0.0)
    logprob_ref[...] = logprob
    entropy_ref[...] = entropy
    mean_ref[...] = total_sum / jnp.maximum(total_count, 1.0)

    count, width = turned_ref.shape
    squares = jnp.zeros((1, count), jnp.float32)
    for part in range(parts):
        for core in range(CORES):
            squares += got_ref[group * parts + part, core][7:8, LANES // 2 : LANES // 2 + count]
    squares = upright(squares)
    scale = jnp.sqrt(squares / (width * shards) + NORM_EPS)
    keys_ref[...] = (turned_ref[...] / scale).astype(jnp.bfloat16)


def partners(sizes, flips):
    (groups, shards), (group_flip, shard_flip) = sizes, flips
    return [
        (g * shards + v, (g ^ group_flip) * shards + (v ^ shard_flip))
        for g in range(groups)
        for v in range(shards)
    ]


def local(
    sizes,
    final_hidden,
    norm_gain,
    head_weight,
    token_ids,
    group_lengths,
    segment_ids,
    continues,
    layer_input,
    key_weight,
    key_gain,
    positions,
    key_rows,
):
    groups, shards = sizes
    parts, half = shards // CORES, groups // 2
    cap, width = final_hidden.shape
    rows = cap // shards
    size = 2 * BAL // shards
    tokens = 2 * parts * size
    core = lax.axis_index("vocab") % CORES
    axes = ("grp", "vocab")
    swapped = sizes == (8, 4)

    def swap(array, group_flip, shard_flip):
        return lax.ppermute(array, axes, partners(sizes, (group_flip, shard_flip)))

    def lay(kernel, shape, *operands, scalars=()):
        return call(
            kernel,
            jax.ShapeDtypeStruct(shape, jnp.bfloat16),
            [SCALARS] * len(scalars) + [WHOLE] * len(operands),
            size * cap * width,
            4 * size * width,
            out_specs=WHOLE,
        )(*scalars, *operands)

    gap = size - rows
    hidden = (final_hidden, norm_gain.reshape(1, width))
    here = lay(functools.partial(prep_kernel, sizes, swapped), (rows, width), *hidden)

    count, key_width = key_rows.shape[0], key_weight.shape[1]
    turned, extra, *ids = call(
        functools.partial(side_kernel, sizes, swapped),
        (
            jax.ShapeDtypeStruct((count, key_width), jnp.float32),
            jax.ShapeDtypeStruct((1, LANES // 2), jnp.float32),
            jax.ShapeDtypeStruct((1, 3 * size), jnp.int32),
            jax.ShapeDtypeStruct((1, 2 * size), jnp.int32),
            jax.ShapeDtypeStruct((1, 3 * size), jnp.int32),
        ),
        [SCALARS] + [WHOLE] * 5 + [FAR, FAR],
        2 * count * width * key_width,
        2 * width * key_width,
        scratch_shapes=[
            pltpu.VMEM(layer_input.shape, jnp.bfloat16),
            pltpu.VMEM(key_weight.shape, jnp.bfloat16),
            pltpu.SemaphoreType.DMA((2,)),
        ],
    )(
        group_lengths,
        key_rows.reshape(1, count),
        positions.reshape(1, cap),
        segment_ids.reshape(1, cap),
        token_ids.reshape(1, groups * cap),
        key_gain.reshape(1, key_width),
        layer_input,
        key_weight,
    )

    head_weight, here = lax.optimization_barrier((head_weight, here))
    far_head = swap(head_weight, 0, 1)
    heads = (head_weight, far_head)
    sent_shape = jax.ShapeDtypeStruct((groups * shards, 8, LANES), jnp.float32)
    if swapped:
        other = swap(here, 4, 0)
        ends = lay(functools.partial(ends_kernel, sizes), (parts, gap, width), *hidden, here)
        across = swap(ends, 1, 0)
        beyond = swap(ends, 2, 0)
        corner = swap(ends, 3, 0)
        other, across, beyond, corner, far_head, ids, extra, turned = lax.optimization_barrier(
            (other, across, beyond, corner, far_head, ids, extra, turned)
        )
        heads = (head_weight, far_head)
        rest = lay(
            functools.partial(mix_kernel, sizes), (rows, width), here, other, scalars=(group_lengths,)
        )
        far_rest = swap(rest, 2, 0)
        rest_xy = swap(rest, 1, 2)
        rest_x = swap(rest, 1, 0)
        rest_y = swap(rest, 0, 2)
        far_x = swap(far_rest, 1, 0)
        far_y = swap(far_rest, 0, 2)
        far_xy = swap(rest_xy, 2, 0)
        first = score(
            functools.partial(piece_kernel, sizes, (0, 1, 0)),
            jax.ShapeDtypeStruct((8, 3 * size), jnp.float32),
            ids[0],
            heads,
            (ends, across, beyond, rest, rest_xy, far_rest),
            3 * size,
        )
        rest_y, rest_x, first = lax.optimization_barrier((rest_y, rest_x, first))
        second = score(
            functools.partial(piece_kernel, sizes, (1, 0)),
            jax.ShapeDtypeStruct((8, 2 * size), jnp.float32),
            ids[1],
            heads,
            (ends, across, rest_y, rest_x),
            2 * size,
        )
        sent = score(
            functools.partial(send_kernel, sizes),
            sent_shape,
            ids[2],
            heads,
            (first, second, extra, beyond, corner, far_y, far_x, far_xy),
            3 * size,
        )
    else:
        taken = front(group_lengths[:half, None], jnp.arange(shards)[None, :], shards)
        ids = token_ids.reshape(groups, rows, shards).transpose(0, 2, 1)
        lower = jnp.pad(ids[:half], ((0, 0), (0, 0), (0, gap)))
        upper = jnp.pad(ids[half:, ::-1, ::-1], ((0, 0), (0, 0), (gap, 0)))
        is_lower = jnp.arange(size)[None, None, :] < taken[:, :, None]
        ids = jnp.where(is_lower, lower, upper).reshape(half, parts, CORES, size)
        ids = lax.dynamic_index_in_dim(ids, core, 2, False).reshape(1, -1)
        every = lax.all_gather(here, axes).reshape(groups, parts, CORES, rows, width)
        every = lax.dynamic_index_in_dim(every, core, 2, False)
        first = jnp.pad(every[:half], ((0, 0), (0, 0), (0, gap), (0, 0)))
        second = jnp.pad(every[half:], ((0, 0), (0, 0), (gap, 0), (0, 0)))
        is_lower = is_lower.reshape(half, parts, CORES, size)
        is_lower = lax.dynamic_index_in_dim(is_lower, core, 2, False)
        every = jnp.where(is_lower[..., None], first, second)
        stats = score(
            functools.partial(plain_kernel, sizes),
            jax.ShapeDtypeStruct((8, half // 2 * tokens), jnp.float32),
            ids,
            heads,
            (every.reshape(-1, width),),
            half // 2 * tokens,
            scratch=False,
        )
        sets = half // 2
        state = [row.reshape(sets, tokens) for row in stats[:3]]
        extra = jnp.broadcast_to(extra, (sets, LANES // 2))
        stats = packed(state, extra).reshape(8, sets, LANES).transpose(1, 0, 2)
        sent = jnp.broadcast_to(
            stats[None, :, None, None], (2, sets, 2, shards, 8, LANES)
        ).reshape(sent_shape.shape)
    got = lax.all_to_all(sent, axes, 0, 0, tiled=False)

    logprob, entropy, means, keys = call(
        functools.partial(final_kernel, sizes),
        (
            jax.ShapeDtypeStruct((1, cap), jnp.float32),
            jax.ShapeDtypeStruct((1, cap), jnp.float32),
            jax.ShapeDtypeStruct((1, SEGS), jnp.float32),
            jax.ShapeDtypeStruct((count, key_width), jnp.bfloat16),
        ),
        [SCALARS] * 2 + [WHOLE] * 3,
        1 << 24,
        4 * groups * shards * 8 * LANES,
    )(
        group_lengths,
        continues,
        got.reshape(groups * parts, CORES, 8, LANES),
        segment_ids.reshape(1, cap),
        turned,
    )
    return logprob.reshape(cap), entropy.reshape(cap), means.reshape(SEGS), keys


def solution(mesh):
    sizes = (mesh.shape["grp"], mesh.shape["vocab"])
    in_specs = (
        P("grp", None),
        P(),
        P(("vocab", "grp"), None),
        P(),
        P(),
        P("grp"),
        P(),
        P("grp", None),
        P(None, "vocab"),
        P("vocab"),
        P("grp"),
        P("grp"),
    )
    out_specs = (P("grp"), P("grp"), P("grp"), P("grp", "vocab"))
    return jax.shard_map(
        functools.partial(local, sizes),
        mesh=mesh,
        in_specs=in_specs,
        out_specs=out_specs,
        check_vma=False,
    )
```

```python
import functools

import jax
import jax.numpy as jnp
from jax import lax
from jax.experimental import pallas as pl
from jax.experimental.pallas import tpu as pltpu
from jax.sharding import PartitionSpec as P

HD = 128
SEGS = 4
BAL = 160
CORES = 2
LANES = 128
BREAKS = 31
SLOTS = (0, 3, 4, 1, 2, 5, 6, 7)

NORM_EPS = 1e-06
ROPE_BASE = 500000.0

VMEM_LIMIT = 24 * 1024 * 1024
WHOLE = pl.BlockSpec(memory_space=pltpu.VMEM)
SCALARS = pl.BlockSpec(memory_space=pltpu.SMEM)
FAR = pl.BlockSpec(memory_space=pltpu.HBM)


def call(kernel, out_shape, in_specs, flops, moved, vmem=VMEM_LIMIT, **more):
    return pl.pallas_call(
        kernel,
        out_shape=out_shape,
        in_specs=in_specs,
        compiler_params=pltpu.CompilerParams(vmem_limit_bytes=vmem),
        cost_estimate=pl.CostEstimate(flops=flops, bytes_accessed=moved, transcendentals=0),
        **more,
    )


def place_of(shards):
    shard = lax.axis_index("vocab")
    return lax.axis_index("grp"), lax.div(shard, CORES), lax.rem(shard, CORES)


def source_row(place, quarter, is_first, quarters, rows):
    return jnp.where(
        is_first,
        quarters * place + quarter,
        quarters * (rows - 1 - place) + quarters - 1 - quarter,
    )


def front(length, quarter, shards):
    return lax.div(length - quarter + shards - 1, shards)


def fetch(sources, targets, semaphores):
    copies = [
        pltpu.make_async_copy(source, target, semaphores.at[i])
        for i, (source, target) in enumerate(zip(sources, targets))
    ]
    for copy in copies:
        copy.start()
    return copies


def dealt(sizes, hidden_ref, gain_ref, t, rows, turned):
    groups, shards = sizes
    group, y, core = place_of(shards)
    is_first = group < groups // 2
    count = hidden_ref.shape[0] // shards
    place = lax.broadcasted_iota(jnp.int32, (rows, hidden_ref.shape[0]), 0)
    column = lax.broadcasted_iota(jnp.int32, place.shape, 1)
    if turned:
        gap = 2 * BAL // shards - count
        back = jnp.where(place < gap, place + (count - gap), place - gap)
        place = jnp.where(is_first, place, back)
    row = source_row(place, (y ^ t) * CORES + core, is_first, shards, count)
    pick = (column == row).astype(jnp.float32).astype(jnp.bfloat16)
    found = jnp.dot(pick, hidden_ref[...], preferred_element_type=jnp.float32)
    meansq = jnp.sum(found * found, axis=-1, keepdims=True) / found.shape[1]
    return (found * lax.rsqrt(meansq + NORM_EPS) * gain_ref[...]).astype(jnp.bfloat16)


def prep_kernel(sizes, turned, hidden_ref, gain_ref, out_ref):
    out_ref[...] = dealt(sizes, hidden_ref, gain_ref, 0, out_ref.shape[0], turned)


def ends_kernel(sizes, hidden_ref, gain_ref, here_ref, out_ref):
    rows = out_ref.shape[1]
    out_ref[0] = here_ref[0:rows, :]
    for t in range(1, out_ref.shape[0]):
        out_ref[t] = dealt(sizes, hidden_ref, gain_ref, t, rows, True)


def mix_kernel(sizes, lengths_ref, here_ref, other_ref, out_ref):
    groups, shards = sizes
    half = groups // 2
    group, y, core = place_of(shards)
    rows, width = here_ref.shape
    gap = 2 * BAL // shards - rows
    length = front(lengths_ref[lax.rem(group, half)], y * CORES + core, shards)
    is_lower = lax.broadcasted_iota(jnp.int32, (rows - gap, width), 0) + gap < length

    def lay(lower_ref, upper_ref):
        lower, upper = (ref[gap:rows, :].astype(jnp.float32) for ref in (lower_ref, upper_ref))
        out_ref[0 : rows - gap, :] = jnp.where(is_lower, lower, upper).astype(jnp.bfloat16)

    @pl.when(group < half)
    def _():
        lay(here_ref, other_ref)

    @pl.when(group >= half)
    def _():
        lay(other_ref, here_ref)

    out_ref[rows - gap : rows, :] = other_ref[0:gap, :]


def gather_pieces(pieces, tokens_ref):
    start = 0
    for end, rest_ref in pieces:
        gap, rows = end.shape[0], rest_ref.shape[0]
        tokens_ref[start : start + gap, :] = end[...]
        tokens_ref[start + gap : start + gap + rows, :] = rest_ref[...]
        start += gap + rows
    return tokens_ref[...]


def statistics(bases, targets, tokens, heads):
    state = None
    for base, head_ref in zip(bases, heads):
        logits = lax.dot_general(
            head_ref[...], tokens, (((1,), (1,)), ((), ())), preferred_element_type=jnp.float32
        )
        logits = logits.astype(jnp.bfloat16).astype(jnp.float32)
        entry = lax.broadcasted_iota(jnp.int32, logits.shape, 0)
        found = jnp.where(entry == targets - base, logits, 0.0)
        picked = jnp.sum(found, axis=0, keepdims=True)
        top = jnp.max(logits, axis=0, keepdims=True)
        if state is not None:
            top = jnp.maximum(top, state[0])
        shifted = jnp.exp(logits - top)
        expsum = jnp.sum(shifted, axis=0, keepdims=True)
        moment = jnp.sum(shifted * logits, axis=0, keepdims=True)
        if state is not None:
            scale = jnp.exp(state[0] - top)
            expsum += state[1] * scale
            moment += state[2] * scale
            picked += state[3]
        state = (top, expsum, moment, picked)
    top, expsum, moment, picked = state
    return top + jnp.log(expsum), moment / expsum, picked


def packed(state, extra):
    flat = [row[:, : 2 * LANES] for row in state] + [row[:, 2 * LANES :] for row in state] + [extra]
    flat = jnp.concatenate(flat, axis=1)
    return jnp.concatenate(
        [flat[:, i : i + LANES] for i in range(0, flat.shape[1], LANES)], axis=0
    )


def merged(every):
    half = LANES // 2
    row = lax.broadcasted_iota(jnp.int32, every.shape[1:], 0)
    top = jnp.max(every, axis=0)
    scale = jnp.exp(every - top[None])
    means = [
        jnp.where(row == 6, pltpu.roll(one, half, 1), pltpu.roll(one, one.shape[0] - 2, 0))
        for one in (every[i] for i in range(every.shape[0]))
    ]
    expsum = jnp.sum(scale, axis=0)
    moment = sum(scale[i] * mean for i, mean in enumerate(means))
    picked = jnp.sum(every, axis=0)
    lse = top + jnp.log(expsum)
    entropy = lse - moment / expsum

    def lay(block, first, last):
        return jnp.concatenate([block[first : first + 1], block[first + 1 : first + 2], last], axis=1)

    lse_row = lay(lse, 0, lse[6:7, :half])
    return jnp.concatenate(
        [lay(picked, 4, picked[7:8, :half]) - lse_row, lay(entropy, 0, entropy[6:7, :half])], axis=0
    )


def bases_of(sizes, head_ref):
    groups, shards = sizes
    group, shard = lax.axis_index("grp"), lax.axis_index("vocab")
    return [((shard ^ flip) * groups + group) * head_ref.shape[0] for flip in (0, 1)]


def rows_of(state, out_ref):
    rows = jnp.concatenate([*state, jnp.zeros((5, out_ref.shape[1]), jnp.float32)], axis=0)
    out_ref[...] = rows


def plain_kernel(sizes, targets_ref, near_ref, far_ref, tokens_ref, out_ref):
    state = statistics(
        bases_of(sizes, near_ref), targets_ref[...], tokens_ref[...], (near_ref, far_ref)
    )
    rows_of(state, out_ref)


def piece_kernel(sizes, picks, targets_ref, near_ref, far_ref, *refs):
    *pieces, out_ref, tokens_ref = refs
    ends = [ref.at[which] for ref, which in zip(pieces, picks)]
    tokens = gather_pieces(zip(ends, pieces[len(picks) :]), tokens_ref)
    state = statistics(bases_of(sizes, near_ref), targets_ref[...], tokens, (near_ref, far_ref))
    rows_of(state, out_ref)


def send_kernel(
    sizes, targets_ref, near_ref, far_ref, first_ref, second_ref, extra_ref, beyond_ref, corner_ref, *refs
):
    *rests, out_ref, tokens_ref = refs
    groups, shards = sizes
    size = 2 * BAL // shards
    ends = (beyond_ref.at[1], corner_ref.at[0], corner_ref.at[1])
    tokens = gather_pieces(zip(ends, rests), tokens_ref)
    state = statistics(bases_of(sizes, near_ref), targets_ref[...], tokens, (near_ref, far_ref))
    group, y, _ = place_of(shards)
    gap = beyond_ref.shape[1]

    def settled(rows):
        blocks = [rows[:, i * size : (i + 1) * size] for i in range(4)]
        blocks = [
            jnp.concatenate([b[:, size - gap :], b[:, gap : size - gap], b[:, :gap]], axis=1) for b in blocks
        ]
        rows = jnp.where(group < groups // 2, rows, jnp.concatenate(blocks, axis=1))
        turned = jnp.concatenate([rows[:, 2 * size :], rows[:, : 2 * size]], axis=1)
        rows = jnp.where(lax.rem(group, 2) == 1, turned, rows)
        quarters = [rows[:, i * size : (i + 1) * size] for i in (1, 0, 3, 2)]
        return jnp.where(y == 1, jnp.concatenate(quarters, axis=1), rows)

    first, second = first_ref[0:4, :], second_ref[0:4, :]
    third = jnp.concatenate([*state, jnp.zeros_like(state[0])], axis=0)
    own = settled(jnp.concatenate([first[:, :size], second, first[:, size : 2 * size]], axis=1))
    beyond = settled(jnp.concatenate([first[:, 2 * size :], third], axis=1))
    own, beyond = (
        packed([rows[i : i + 1] for i in range(3)], extra_ref[...]) for rows in (own, beyond)
    )
    mine = lax.div(lax.rem(group, groups // 2), 2)
    for which in range(groups // 4):
        block = jnp.where(mine == which, own, beyond)
        for group in range(groups):
            if group % (groups // 2) // 2 == which:
                for shard in range(shards):
                    out_ref[group * shards + shard] = block


def score(kernel, out_shape, targets, heads, extras, count, scratch=True):
    vocab, width = heads[0].shape
    return call(
        kernel,
        out_shape,
        [WHOLE] * (3 + len(extras)),
        4 * vocab * count * width,
        4 * vocab * width + 2 * count * width,
        out_specs=WHOLE,
        scratch_shapes=[pltpu.VMEM((count, width), jnp.bfloat16)] if scratch else [],
    )(targets, *heads, *extras)


def upright(row):
    count = row.shape[1]
    diagonal = lax.broadcasted_iota(jnp.int32, (count, count), 0) == lax.broadcasted_iota(
        jnp.int32, (count, count), 1
    )
    return jnp.sum(jnp.where(diagonal, row, 0), axis=1, keepdims=True)


def side_kernel(
    sizes,
    swapped,
    lengths_ref,
    rows_ref,
    positions_ref,
    segments_ref,
    ids_ref,
    gain_ref,
    input_hbm,
    weight_hbm,
    turned_ref,
    extra_ref,
    first_ref,
    second_ref,
    third_ref,
    input_ref,
    weight_ref,
    semaphores,
):
    groups, shards = sizes
    copies = fetch((input_hbm, weight_hbm), (input_ref, weight_ref), semaphores)
    cap = segments_ref.shape[1]
    if swapped:
        tokens = first_ref.shape[1] + second_ref.shape[1] // 2
        half, size = groups // 2, 2 * BAL // shards
        group, y, core = place_of(shards)
        lane = lax.broadcasted_iota(jnp.int32, (1, 2 * tokens), 1)
        row = jnp.zeros((1, 2 * tokens), jnp.int32)
        source = jnp.zeros((1, 2 * tokens), jnp.int32)
        for start, slot in enumerate(SLOTS):
            place = lane - start * size
            here = (place >= 0) & (place < size)
            gap = size - cap // shards
            back = jnp.where(place < gap, place + size - gap, place - (size - gap))
            back = jnp.where((place >= gap) & (place < size - gap), place, back)
            place = jnp.where(group < half, place, back)
            lower = lax.rem(group, half) ^ (slot // 4 * 2) ^ (slot // 2 % 2)
            quarter = (y ^ (slot % 2)) * CORES + core
            is_lower = place < front(lengths_ref[lower], quarter, shards)
            stands = jnp.where(
                is_lower, shards * place + quarter, shards * (size - 1 - place) + shards - 1 - quarter
            )
            row = jnp.where(here, stands, row)
            source = jnp.where(here, jnp.where(is_lower, lower, lower + half), source)
        ids = jnp.concatenate([ids_ref[0:1, g * cap : (g + 1) * cap] for g in range(groups)], axis=0)
        halves = jnp.concatenate([ids >> 8, ids & 255], axis=0)
        stood = lax.broadcasted_iota(jnp.int32, (cap, 2 * tokens), 0)
        pick = (stood == row).astype(jnp.float32).astype(jnp.bfloat16)
        found = jnp.dot(
            halves.astype(jnp.float32).astype(jnp.bfloat16), pick, preferred_element_type=jnp.float32
        )
        found = found[:groups] * 256.0 + found[groups:]
        of_group = lax.broadcasted_iota(jnp.int32, found.shape, 0) == source
        targets = jnp.sum(jnp.where(of_group, found, 0.0), axis=0, keepdims=True).astype(jnp.int32)
        start = 0
        for ref in (first_ref, second_ref, third_ref):
            ref[...] = targets[:, start : start + ref.shape[1]]
            start += ref.shape[1]
    else:
        for ref in (first_ref, second_ref, third_ref):
            ref[...] = jnp.zeros_like(ref)

    count, width = turned_ref.shape
    column = lax.broadcasted_iota(jnp.int32, (count, cap), 1)
    chosen = column == upright(rows_ref[...])
    places = jnp.sum(jnp.where(chosen, positions_ref[...], 0), axis=1, keepdims=True)
    half_head = HD // 2
    steps = lax.broadcasted_iota(jnp.int32, (count, half_head), 1).astype(jnp.float32)
    freqs = jnp.exp(-(2.0 * steps / HD) * jnp.log(jnp.full(steps.shape, ROPE_BASE, jnp.float32)))
    angles = places.astype(jnp.float32) * freqs
    cosine, sine = jnp.cos(angles), jnp.sin(angles)
    cosine = jnp.concatenate([cosine, cosine], axis=1)
    sine = jnp.concatenate([-sine, sine], axis=1)
    for copy in copies:
        copy.wait()
    pick = chosen.astype(jnp.float32).astype(jnp.bfloat16)
    rows = jnp.dot(pick, input_ref[...], preferred_element_type=jnp.float32).astype(jnp.bfloat16)
    projected = jnp.dot(rows, weight_ref[...], preferred_element_type=jnp.float32)
    squares = jnp.sum(projected * projected, axis=1, keepdims=True)
    lane = lax.broadcasted_iota(jnp.int32, (count, extra_ref.shape[1]), 1)
    diagonal = lax.broadcasted_iota(jnp.int32, lane.shape, 0) == lane
    extra = jnp.sum(jnp.where(diagonal, squares, 0.0), axis=0, keepdims=True)
    for label in range(1, SEGS):
        before = (segments_ref[...] < label).astype(jnp.float32)
        before = jnp.sum(before, axis=1, keepdims=True)
        extra = jnp.where(lane[0:1] == BREAKS + label, before, extra)
    extra_ref[...] = extra
    gained = projected * gain_ref[...]
    for start in range(0, width, HD):
        head = gained[:, start : start + HD]
        turned_ref[:, start : start + HD] = head * cosine + pltpu.roll(head, half_head, 1) * sine


def final_kernel(
    sizes,
    lengths_ref,
    continues_ref,
    got_ref,
    turned_ref,
    logprob_ref,
    entropy_ref,
    mean_ref,
    keys_ref,
):
    groups, shards = sizes
    parts, group = shards // CORES, lax.axis_index("grp")
    cap = logprob_ref.shape[1]
    size = 2 * BAL // shards
    tokens = 2 * parts * size
    columns = [merged(got_ref[:, core]) for core in range(CORES)]

    column, span = lax.rem(group, 2), tokens // 2
    halves = [[both[:, :span], both[:, span:]] for both in columns]
    own = jnp.concatenate([jnp.where(column == 0, a, b) for a, b in halves], axis=1)
    beside = jnp.concatenate([jnp.where(column == 0, b, a) for a, b in halves], axis=1)
    rest = jnp.concatenate([own, beside], axis=0)
    terms = []
    for _ in range(3):
        term = rest.astype(jnp.bfloat16).astype(jnp.float32)
        terms.append(term)
        rest = rest - term
    terms = jnp.concatenate(terms + [jnp.zeros_like(rest)], axis=0).astype(jnp.bfloat16)

    slots = lax.broadcasted_iota(jnp.int32, (1, cap), 1)
    is_first = group < groups // 2
    quarter = jnp.where(is_first, slots % shards, shards - 1 - slots % shards)
    place = jnp.where(is_first, slots // shards, size - 1 - slots // shards)
    home = quarter % CORES * span + quarter // CORES * size + place
    stood = lax.broadcasted_iota(jnp.int32, (CORES * span, cap), 0)
    pick = (stood == home).astype(jnp.float32).astype(jnp.bfloat16)
    found = jnp.dot(terms, pick, preferred_element_type=jnp.float32)
    found = found[0:4] + found[4:8] + found[8:12]
    def summed(who, logprob):
        note = got_ref[who * parts, 0][7:8, LANES // 2 :]
        breaks = [note[:, BREAKS + i : BREAKS + i + 1].astype(jnp.int32) for i in range(1, SEGS)]
        live = slots < lengths_ref[who]
        logprob = jnp.where(live, logprob, 0.0)
        sums, counts = [], []
        for label in range(SEGS):
            member = live
            if label > 0:
                member = member & (slots >= breaks[label - 1])
            if label < SEGS - 1:
                member = member & (slots < breaks[label])
            sums.append(jnp.sum(jnp.where(member, logprob, 0.0), axis=1, keepdims=True))
            counts.append(jnp.sum(member.astype(jnp.float32), axis=1, keepdims=True))
        return logprob, sums, counts, breaks

    partner = group ^ 1
    logprob, sums, counts, breaks = summed(group, found[0:1])
    _, partner_sums, partner_counts, _ = summed(partner, found[2:3])
    entropy = jnp.where(slots < lengths_ref[group], found[1:2], 0.0)
    is_even = group % 2 == 0
    joined = jnp.where(is_even, continues_ref[group], continues_ref[partner]) == 1
    my_last = sum((lengths_ref[group] - 1 >= begin).astype(jnp.int32) for begin in breaks)
    target = jnp.where(is_even, my_last, jnp.zeros_like(my_last))
    extra_sum, extra_count = partner_sums[0], partner_counts[0]
    for label in range(1, SEGS):
        later = jnp.logical_not(is_even) & (partner_counts[label] > 0)
        extra_sum = jnp.where(later, partner_sums[label], extra_sum)
        extra_count = jnp.where(later, partner_counts[label], extra_count)
    labels = lax.broadcasted_iota(jnp.int32, (1, SEGS), 1)
    means = jnp.zeros((1, SEGS), jnp.float32)
    for label in range(SEGS):
        update = joined & (target == label)
        total_sum = sums[label] + jnp.where(update, extra_sum, 0.0)
        total_count = counts[label] + jnp.where(update, extra_count, 0.0)
        means = jnp.where(labels == label, total_sum / jnp.maximum(total_count, 1.0), means)
    logprob_ref[...] = logprob
    entropy_ref[...] = entropy
    mean_ref[...] = means

    count, width = turned_ref.shape
    squares = jnp.zeros((1, count), jnp.float32)
    for part in range(parts):
        for core in range(CORES):
            squares += got_ref[group * parts + part, core][7:8, LANES // 2 : LANES // 2 + count]
    squares = upright(squares)
    scale = jnp.sqrt(squares / (width * shards) + NORM_EPS)
    keys_ref[...] = (turned_ref[...] / scale).astype(jnp.bfloat16)


def partners(sizes, flips):
    (groups, shards), (group_flip, shard_flip) = sizes, flips
    return [
        (g * shards + v, (g ^ group_flip) * shards + (v ^ shard_flip))
        for g in range(groups)
        for v in range(shards)
    ]


def local(
    sizes,
    final_hidden,
    norm_gain,
    head_weight,
    token_ids,
    group_lengths,
    segment_ids,
    continues,
    layer_input,
    key_weight,
    key_gain,
    positions,
    key_rows,
):
    groups, shards = sizes
    parts, half = shards // CORES, groups // 2
    cap, width = final_hidden.shape
    rows = cap // shards
    size = 2 * BAL // shards
    tokens = 2 * parts * size
    core = lax.axis_index("vocab") % CORES
    axes = ("grp", "vocab")
    swapped = sizes == (8, 4)

    def swap(array, group_flip, shard_flip):
        return lax.ppermute(array, axes, partners(sizes, (group_flip, shard_flip)))

    def lay(kernel, shape, *operands, scalars=()):
        return call(
            kernel,
            jax.ShapeDtypeStruct(shape, jnp.bfloat16),
            [SCALARS] * len(scalars) + [WHOLE] * len(operands),
            size * cap * width,
            4 * size * width,
            out_specs=WHOLE,
        )(*scalars, *operands)

    gap = size - rows
    hidden = (final_hidden, norm_gain.reshape(1, width))
    here = lay(functools.partial(prep_kernel, sizes, swapped), (rows, width), *hidden)

    count, key_width = key_rows.shape[0], key_weight.shape[1]
    turned, extra, *ids = call(
        functools.partial(side_kernel, sizes, swapped),
        (
            jax.ShapeDtypeStruct((count, key_width), jnp.float32),
            jax.ShapeDtypeStruct((1, LANES // 2), jnp.float32),
            jax.ShapeDtypeStruct((1, 3 * size), jnp.int32),
            jax.ShapeDtypeStruct((1, 2 * size), jnp.int32),
            jax.ShapeDtypeStruct((1, 3 * size), jnp.int32),
        ),
        [SCALARS] + [WHOLE] * 5 + [FAR, FAR],
        2 * count * width * key_width,
        2 * width * key_width,
        scratch_shapes=[
            pltpu.VMEM(layer_input.shape, jnp.bfloat16),
            pltpu.VMEM(key_weight.shape, jnp.bfloat16),
            pltpu.SemaphoreType.DMA((2,)),
        ],
    )(
        group_lengths,
        key_rows.reshape(1, count),
        positions.reshape(1, cap),
        segment_ids.reshape(1, cap),
        token_ids.reshape(1, groups * cap),
        key_gain.reshape(1, key_width),
        layer_input,
        key_weight,
    )

    head_weight, here = lax.optimization_barrier((head_weight, here))
    far_head = swap(head_weight, 0, 1)
    heads = (head_weight, far_head)
    sent_shape = jax.ShapeDtypeStruct((groups * shards, 8, LANES), jnp.float32)
    if swapped:
        other = swap(here, 4, 0)
        ends = lay(functools.partial(ends_kernel, sizes), (parts, gap, width), *hidden, here)
        across = swap(ends, 1, 0)
        beyond = swap(ends, 2, 0)
        corner = swap(ends, 3, 0)
        other, across, beyond, corner, far_head, ids, extra, turned = lax.optimization_barrier(
            (other, across, beyond, corner, far_head, ids, extra, turned)
        )
        heads = (head_weight, far_head)
        rest = lay(
            functools.partial(mix_kernel, sizes), (rows, width), here, other, scalars=(group_lengths,)
        )
        far_rest = swap(rest, 2, 0)
        rest_xy = swap(rest, 1, 2)
        rest_x = swap(rest, 1, 0)
        rest_y = swap(rest, 0, 2)
        far_x = swap(far_rest, 1, 0)
        far_y = swap(far_rest, 0, 2)
        far_xy = swap(rest_xy, 2, 0)
        first = score(
            functools.partial(piece_kernel, sizes, (0, 1, 0)),
            jax.ShapeDtypeStruct((8, 3 * size), jnp.float32),
            ids[0],
            heads,
            (ends, across, beyond, rest, rest_xy, far_rest),
            3 * size,
        )
        rest_y, rest_x, first = lax.optimization_barrier((rest_y, rest_x, first))
        second = score(
            functools.partial(piece_kernel, sizes, (1, 0)),
            jax.ShapeDtypeStruct((8, 2 * size), jnp.float32),
            ids[1],
            heads,
            (ends, across, rest_y, rest_x),
            2 * size,
        )
        sent = score(
            functools.partial(send_kernel, sizes),
            sent_shape,
            ids[2],
            heads,
            (first, second, extra, beyond, corner, far_y, far_x, far_xy),
            3 * size,
        )
    else:
        taken = front(group_lengths[:half, None], jnp.arange(shards)[None, :], shards)
        ids = token_ids.reshape(groups, rows, shards).transpose(0, 2, 1)
        lower = jnp.pad(ids[:half], ((0, 0), (0, 0), (0, gap)))
        upper = jnp.pad(ids[half:, ::-1, ::-1], ((0, 0), (0, 0), (gap, 0)))
        is_lower = jnp.arange(size)[None, None, :] < taken[:, :, None]
        ids = jnp.where(is_lower, lower, upper).reshape(half, parts, CORES, size)
        ids = lax.dynamic_index_in_dim(ids, core, 2, False).reshape(1, -1)
        every = lax.all_gather(here, axes).reshape(groups, parts, CORES, rows, width)
        every = lax.dynamic_index_in_dim(every, core, 2, False)
        first = jnp.pad(every[:half], ((0, 0), (0, 0), (0, gap), (0, 0)))
        second = jnp.pad(every[half:], ((0, 0), (0, 0), (gap, 0), (0, 0)))
        is_lower = is_lower.reshape(half, parts, CORES, size)
        is_lower = lax.dynamic_index_in_dim(is_lower, core, 2, False)
        every = jnp.where(is_lower[..., None], first, second)
        stats = score(
            functools.partial(plain_kernel, sizes),
            jax.ShapeDtypeStruct((8, half // 2 * tokens), jnp.float32),
            ids,
            heads,
            (every.reshape(-1, width),),
            half // 2 * tokens,
            scratch=False,
        )
        sets = half // 2
        state = [row.reshape(sets, tokens) for row in stats[:3]]
        extra = jnp.broadcast_to(extra, (sets, LANES // 2))
        stats = packed(state, extra).reshape(8, sets, LANES).transpose(1, 0, 2)
        sent = jnp.broadcast_to(
            stats[None, :, None, None], (2, sets, 2, shards, 8, LANES)
        ).reshape(sent_shape.shape)
    got = lax.all_to_all(sent, axes, 0, 0, tiled=False)

    logprob, entropy, means, keys = call(
        functools.partial(final_kernel, sizes),
        (
            jax.ShapeDtypeStruct((1, cap), jnp.float32),
            jax.ShapeDtypeStruct((1, cap), jnp.float32),
            jax.ShapeDtypeStruct((1, SEGS), jnp.float32),
            jax.ShapeDtypeStruct((count, key_width), jnp.bfloat16),
        ),
        [SCALARS] * 2 + [WHOLE] * 2,
        1 << 24,
        4 * groups * shards * 8 * LANES,
    )(
        group_lengths,
        continues,
        got.reshape(groups * parts, CORES, 8, LANES),
        turned,
    )
    return logprob.reshape(cap), entropy.reshape(cap), means.reshape(SEGS), keys


def solution(mesh):
    sizes = (mesh.shape["grp"], mesh.shape["vocab"])
    in_specs = (
        P("grp", None),
        P(),
        P(("vocab", "grp"), None),
        P(),
        P(),
        P("grp"),
        P(),
        P("grp", None),
        P(None, "vocab"),
        P("vocab"),
        P("grp"),
        P("grp"),
    )
    out_specs = (P("grp"), P("grp"), P("grp"), P("grp", "vocab"))
    return jax.shard_map(
        functools.partial(local, sizes),
        mesh=mesh,
        in_specs=in_specs,
        out_specs=out_specs,
        check_vma=False,
    )
```

```python
import functools

import jax
import jax.numpy as jnp
from jax import lax
from jax.experimental import pallas as pl
from jax.experimental.pallas import tpu as pltpu
from jax.sharding import PartitionSpec as P

HD = 128
SEGS = 4
BAL = 160
CORES = 2
LANES = 128
BREAKS = 31
SLOTS = (0, 3, 4, 1, 2, 5, 6, 7)

NORM_EPS = 1e-06
ROPE_BASE = 500000.0

VMEM_LIMIT = 24 * 1024 * 1024
WHOLE = pl.BlockSpec(memory_space=pltpu.VMEM)
SCALARS = pl.BlockSpec(memory_space=pltpu.SMEM)
FAR = pl.BlockSpec(memory_space=pltpu.HBM)


def call(kernel, out_shape, in_specs, flops, moved, vmem=VMEM_LIMIT, **more):
    return pl.pallas_call(
        kernel,
        out_shape=out_shape,
        in_specs=in_specs,
        compiler_params=pltpu.CompilerParams(vmem_limit_bytes=vmem),
        cost_estimate=pl.CostEstimate(flops=flops, bytes_accessed=moved, transcendentals=0),
        **more,
    )


def place_of(shards):
    shard = lax.axis_index("vocab")
    return lax.axis_index("grp"), lax.div(shard, CORES), lax.rem(shard, CORES)


def source_row(place, quarter, is_first, quarters, rows):
    return jnp.where(
        is_first,
        quarters * place + quarter,
        quarters * (rows - 1 - place) + quarters - 1 - quarter,
    )


def front(length, quarter, shards):
    return (length - quarter + shards - 1) // shards


def chosen(row_ref, index):
    row = row_ref[...]
    lane = lax.broadcasted_iota(jnp.int32, row.shape, 1)
    return jnp.sum(jnp.where(lane == index, row, 0), axis=1, keepdims=True)


def fetch(sources, targets, semaphores):
    copies = [
        pltpu.make_async_copy(source, target, semaphores.at[i])
        for i, (source, target) in enumerate(zip(sources, targets))
    ]
    for copy in copies:
        copy.start()
    return copies


def dealt(sizes, hidden_ref, gain_ref, t, rows, turned):
    groups, shards = sizes
    group, y, core = place_of(shards)
    is_first = group < groups // 2
    count = hidden_ref.shape[0] // shards
    place = lax.broadcasted_iota(jnp.int32, (rows, hidden_ref.shape[0]), 0)
    column = lax.broadcasted_iota(jnp.int32, place.shape, 1)
    if turned:
        gap = 2 * BAL // shards - count
        back = jnp.where(place < gap, place + (count - gap), place - gap)
        place = jnp.where(is_first, place, back)
    row = source_row(place, (y ^ t) * CORES + core, is_first, shards, count)
    pick = (column == row).astype(jnp.float32).astype(jnp.bfloat16)
    found = jnp.dot(pick, hidden_ref[...], preferred_element_type=jnp.float32)
    meansq = jnp.sum(found * found, axis=-1, keepdims=True) / found.shape[1]
    return (found * lax.rsqrt(meansq + NORM_EPS) * gain_ref[...]).astype(jnp.bfloat16)


def prep_kernel(sizes, turned, hidden_ref, gain_ref, out_ref):
    out_ref[...] = dealt(sizes, hidden_ref, gain_ref, 0, out_ref.shape[0], turned)


def ends_kernel(sizes, hidden_ref, gain_ref, here_ref, out_ref):
    rows = out_ref.shape[1]
    out_ref[0] = here_ref[0:rows, :]
    for t in range(1, out_ref.shape[0]):
        out_ref[t] = dealt(sizes, hidden_ref, gain_ref, t, rows, True)


def mix_kernel(sizes, lengths_ref, here_ref, other_ref, out_ref):
    groups, shards = sizes
    half = groups // 2
    group, y, core = place_of(shards)
    rows, width = here_ref.shape
    gap = 2 * BAL // shards - rows
    length = front(chosen(lengths_ref, lax.rem(group, half)), y * CORES + core, shards)
    is_lower = lax.broadcasted_iota(jnp.int32, (rows - gap, width), 0) + gap < length

    def lay(lower_ref, upper_ref):
        lower, upper = (ref[gap:rows, :].astype(jnp.float32) for ref in (lower_ref, upper_ref))
        out_ref[0 : rows - gap, :] = jnp.where(is_lower, lower, upper).astype(jnp.bfloat16)

    @pl.when(group < half)
    def _():
        lay(here_ref, other_ref)

    @pl.when(group >= half)
    def _():
        lay(other_ref, here_ref)

    out_ref[rows - gap : rows, :] = other_ref[0:gap, :]


def gather_pieces(pieces, tokens_ref):
    start = 0
    for end, rest_ref in pieces:
        gap, rows = end.shape[0], rest_ref.shape[0]
        tokens_ref[start : start + gap, :] = end[...]
        tokens_ref[start + gap : start + gap + rows, :] = rest_ref[...]
        start += gap + rows
    return tokens_ref[...]


def statistics(bases, targets, tokens, heads):
    state = None
    for base, head_ref in zip(bases, heads):
        logits = lax.dot_general(
            head_ref[...], tokens, (((1,), (1,)), ((), ())), preferred_element_type=jnp.float32
        )
        logits = logits.astype(jnp.bfloat16).astype(jnp.float32)
        entry = lax.broadcasted_iota(jnp.int32, logits.shape, 0)
        found = jnp.where(entry == targets - base, logits, 0.0)
        picked = jnp.sum(found, axis=0, keepdims=True)
        top = jnp.max(logits, axis=0, keepdims=True)
        if state is not None:
            top = jnp.maximum(top, state[0])
        shifted = jnp.exp(logits - top)
        expsum = jnp.sum(shifted, axis=0, keepdims=True)
        moment = jnp.sum(shifted * logits, axis=0, keepdims=True)
        if state is not None:
            scale = jnp.exp(state[0] - top)
            expsum += state[1] * scale
            moment += state[2] * scale
            picked += state[3]
        state = (top, expsum, moment, picked)
    top, expsum, moment, picked = state
    return top + jnp.log(expsum), moment / expsum, picked


def packed(state, extra):
    flat = [row[:, : 2 * LANES] for row in state] + [row[:, 2 * LANES :] for row in state] + [extra]
    flat = jnp.concatenate(flat, axis=1)
    return jnp.concatenate(
        [flat[:, i : i + LANES] for i in range(0, flat.shape[1], LANES)], axis=0
    )


def merged(every):
    half = LANES // 2
    row = lax.broadcasted_iota(jnp.int32, every.shape[1:], 0)
    top = jnp.max(every, axis=0)
    scale = jnp.exp(every - top[None])
    means = [
        jnp.where(row == 6, pltpu.roll(one, half, 1), pltpu.roll(one, one.shape[0] - 2, 0))
        for one in (every[i] for i in range(every.shape[0]))
    ]
    expsum = jnp.sum(scale, axis=0)
    moment = sum(scale[i] * mean for i, mean in enumerate(means))
    picked = jnp.sum(every, axis=0)
    lse = top + jnp.log(expsum)
    entropy = lse - moment / expsum

    def lay(block, first, last):
        return jnp.concatenate([block[first : first + 1], block[first + 1 : first + 2], last], axis=1)

    lse_row = lay(lse, 0, lse[6:7, :half])
    return jnp.concatenate(
        [lay(picked, 4, picked[7:8, :half]) - lse_row, lay(entropy, 0, entropy[6:7, :half])], axis=0
    )


def bases_of(sizes, head_ref):
    groups, shards = sizes
    group, shard = lax.axis_index("grp"), lax.axis_index("vocab")
    return [((shard ^ flip) * groups + group) * head_ref.shape[0] for flip in (0, 1)]


def rows_of(state, out_ref):
    rows = jnp.concatenate([*state, jnp.zeros((5, out_ref.shape[1]), jnp.float32)], axis=0)
    out_ref[...] = rows


def plain_kernel(sizes, targets_ref, near_ref, far_ref, tokens_ref, out_ref):
    state = statistics(
        bases_of(sizes, near_ref), targets_ref[...], tokens_ref[...], (near_ref, far_ref)
    )
    rows_of(state, out_ref)


def piece_kernel(sizes, picks, targets_ref, near_ref, far_ref, *refs):
    *pieces, out_ref, tokens_ref = refs
    ends = [ref.at[which] for ref, which in zip(pieces, picks)]
    tokens = gather_pieces(zip(ends, pieces[len(picks) :]), tokens_ref)
    state = statistics(bases_of(sizes, near_ref), targets_ref[...], tokens, (near_ref, far_ref))
    rows_of(state, out_ref)


def send_kernel(
    sizes, targets_ref, near_ref, far_ref, first_ref, second_ref, extra_ref, beyond_ref, corner_ref, *refs
):
    *rests, out_ref, tokens_ref = refs
    groups, shards = sizes
    size = 2 * BAL // shards
    ends = (beyond_ref.at[1], corner_ref.at[0], corner_ref.at[1])
    tokens = gather_pieces(zip(ends, rests), tokens_ref)
    state = statistics(bases_of(sizes, near_ref), targets_ref[...], tokens, (near_ref, far_ref))
    group, y, _ = place_of(shards)
    gap = beyond_ref.shape[1]

    def settled(rows):
        blocks = [rows[:, i * size : (i + 1) * size] for i in range(4)]
        blocks = [
            jnp.concatenate([b[:, size - gap :], b[:, gap : size - gap], b[:, :gap]], axis=1) for b in blocks
        ]
        rows = jnp.where(group < groups // 2, rows, jnp.concatenate(blocks, axis=1))
        turned = jnp.concatenate([rows[:, 2 * size :], rows[:, : 2 * size]], axis=1)
        rows = jnp.where(lax.rem(group, 2) == 1, turned, rows)
        quarters = [rows[:, i * size : (i + 1) * size] for i in (1, 0, 3, 2)]
        return jnp.where(y == 1, jnp.concatenate(quarters, axis=1), rows)

    first, second = first_ref[0:4, :], second_ref[0:4, :]
    third = jnp.concatenate([*state, jnp.zeros_like(state[0])], axis=0)
    own = settled(jnp.concatenate([first[:, :size], second, first[:, size : 2 * size]], axis=1))
    beyond = settled(jnp.concatenate([first[:, 2 * size :], third], axis=1))
    own, beyond = (
        packed([rows[i : i + 1] for i in range(3)], extra_ref[...]) for rows in (own, beyond)
    )
    mine = lax.div(lax.rem(group, groups // 2), 2)
    for which in range(groups // 4):
        block = jnp.where(mine == which, own, beyond)
        for group in range(groups):
            if group % (groups // 2) // 2 == which:
                for shard in range(shards):
                    out_ref[group * shards + shard] = block


def score(kernel, out_shape, targets, heads, extras, count, scratch=True):
    vocab, width = heads[0].shape
    return call(
        kernel,
        out_shape,
        [WHOLE] * (3 + len(extras)),
        4 * vocab * count * width,
        4 * vocab * width + 2 * count * width,
        out_specs=WHOLE,
        scratch_shapes=[pltpu.VMEM((count, width), jnp.bfloat16)] if scratch else [],
    )(targets, *heads, *extras)


def upright(row):
    count = row.shape[1]
    diagonal = lax.broadcasted_iota(jnp.int32, (count, count), 0) == lax.broadcasted_iota(
        jnp.int32, (count, count), 1
    )
    return jnp.sum(jnp.where(diagonal, row, 0), axis=1, keepdims=True)


def side_kernel(
    sizes,
    swapped,
    lengths_ref,
    rows_ref,
    positions_ref,
    segments_ref,
    ids_ref,
    gain_ref,
    input_hbm,
    weight_hbm,
    turned_ref,
    extra_ref,
    first_ref,
    second_ref,
    third_ref,
    input_ref,
    weight_ref,
    semaphores,
):
    groups, shards = sizes
    copies = fetch((input_hbm, weight_hbm), (input_ref, weight_ref), semaphores)
    cap = segments_ref.shape[1]
    if swapped:
        tokens = first_ref.shape[1] + second_ref.shape[1] // 2
        half, size = groups // 2, 2 * BAL // shards
        group, y, core = place_of(shards)
        lane = lax.broadcasted_iota(jnp.int32, (1, 2 * tokens), 1)
        row = jnp.zeros((1, 2 * tokens), jnp.int32)
        source = jnp.zeros((1, 2 * tokens), jnp.int32)
        for start, slot in enumerate(SLOTS):
            place = lane - start * size
            here = (place >= 0) & (place < size)
            gap = size - cap // shards
            back = jnp.where(place < gap, place + size - gap, place - (size - gap))
            back = jnp.where((place >= gap) & (place < size - gap), place, back)
            place = jnp.where(group < half, place, back)
            lower = lax.rem(group, half) ^ (slot // 4 * 2) ^ (slot // 2 % 2)
            quarter = (y ^ (slot % 2)) * CORES + core
            is_lower = place < front(lengths_ref[lower], quarter, shards)
            stands = jnp.where(
                is_lower, shards * place + quarter, shards * (size - 1 - place) + shards - 1 - quarter
            )
            row = jnp.where(here, stands, row)
            source = jnp.where(here, jnp.where(is_lower, lower, lower + half), source)
        ids = jnp.concatenate([ids_ref[0:1, g * cap : (g + 1) * cap] for g in range(groups)], axis=0)
        halves = jnp.concatenate([ids >> 8, ids & 255], axis=0)
        stood = lax.broadcasted_iota(jnp.int32, (cap, 2 * tokens), 0)
        pick = (stood == row).astype(jnp.float32).astype(jnp.bfloat16)
        found = jnp.dot(
            halves.astype(jnp.float32).astype(jnp.bfloat16), pick, preferred_element_type=jnp.float32
        )
        found = found[:groups] * 256.0 + found[groups:]
        of_group = lax.broadcasted_iota(jnp.int32, found.shape, 0) == source
        targets = jnp.sum(jnp.where(of_group, found, 0.0), axis=0, keepdims=True).astype(jnp.int32)
        start = 0
        for ref in (first_ref, second_ref, third_ref):
            ref[...] = targets[:, start : start + ref.shape[1]]
            start += ref.shape[1]
    else:
        for ref in (first_ref, second_ref, third_ref):
            ref[...] = jnp.zeros_like(ref)

    count, width = turned_ref.shape
    column = lax.broadcasted_iota(jnp.int32, (count, cap), 1)
    chosen = column == upright(rows_ref[...])
    places = jnp.sum(jnp.where(chosen, positions_ref[...], 0), axis=1, keepdims=True)
    half_head = HD // 2
    steps = lax.broadcasted_iota(jnp.int32, (count, half_head), 1).astype(jnp.float32)
    freqs = jnp.exp(-(2.0 * steps / HD) * jnp.log(jnp.full(steps.shape, ROPE_BASE, jnp.float32)))
    angles = places.astype(jnp.float32) * freqs
    cosine, sine = jnp.cos(angles), jnp.sin(angles)
    cosine = jnp.concatenate([cosine, cosine], axis=1)
    sine = jnp.concatenate([-sine, sine], axis=1)
    for copy in copies:
        copy.wait()
    pick = chosen.astype(jnp.float32).astype(jnp.bfloat16)
    rows = jnp.dot(pick, input_ref[...], preferred_element_type=jnp.float32).astype(jnp.bfloat16)
    projected = jnp.dot(rows, weight_ref[...], preferred_element_type=jnp.float32)
    squares = jnp.sum(projected * projected, axis=1, keepdims=True)
    lane = lax.broadcasted_iota(jnp.int32, (count, extra_ref.shape[1]), 1)
    diagonal = lax.broadcasted_iota(jnp.int32, lane.shape, 0) == lane
    extra = jnp.sum(jnp.where(diagonal, squares, 0.0), axis=0, keepdims=True)
    for label in range(1, SEGS):
        before = (segments_ref[...] < label).astype(jnp.float32)
        before = jnp.sum(before, axis=1, keepdims=True)
        extra = jnp.where(lane[0:1] == BREAKS + label, before, extra)
    extra_ref[...] = extra
    gained = projected * gain_ref[...]
    for start in range(0, width, HD):
        head = gained[:, start : start + HD]
        turned_ref[:, start : start + HD] = head * cosine + pltpu.roll(head, half_head, 1) * sine


def final_kernel(
    sizes,
    lengths_ref,
    continues_ref,
    got_ref,
    turned_ref,
    logprob_ref,
    entropy_ref,
    mean_ref,
    keys_ref,
):
    groups, shards = sizes
    parts, group = shards // CORES, lax.axis_index("grp")
    cap = logprob_ref.shape[1]
    size = 2 * BAL // shards
    tokens = 2 * parts * size
    columns = [merged(got_ref[:, core]) for core in range(CORES)]

    column, span = lax.rem(group, 2), tokens // 2
    halves = [[both[:, :span], both[:, span:]] for both in columns]
    own = jnp.concatenate([jnp.where(column == 0, a, b) for a, b in halves], axis=1)
    beside = jnp.concatenate([jnp.where(column == 0, b, a) for a, b in halves], axis=1)
    rest = jnp.concatenate([own, beside], axis=0)
    terms = []
    for _ in range(3):
        term = rest.astype(jnp.bfloat16).astype(jnp.float32)
        terms.append(term)
        rest = rest - term
    terms = jnp.concatenate(terms + [jnp.zeros_like(rest)], axis=0).astype(jnp.bfloat16)

    slots = lax.broadcasted_iota(jnp.int32, (1, cap), 1)
    is_first = group < groups // 2
    quarter = jnp.where(is_first, slots % shards, shards - 1 - slots % shards)
    place = jnp.where(is_first, slots // shards, size - 1 - slots // shards)
    home = quarter % CORES * span + quarter // CORES * size + place
    stood = lax.broadcasted_iota(jnp.int32, (CORES * span, cap), 0)
    pick = (stood == home).astype(jnp.float32).astype(jnp.bfloat16)
    found = jnp.dot(terms, pick, preferred_element_type=jnp.float32)
    found = found[0:4] + found[4:8] + found[8:12]
    def summed(who, logprob):
        note = got_ref[who * parts, 0][7:8, LANES // 2 :]
        breaks = [note[:, BREAKS + i : BREAKS + i + 1].astype(jnp.int32) for i in range(1, SEGS)]
        live = slots < chosen(lengths_ref, who)
        logprob = jnp.where(live, logprob, 0.0)
        sums, counts = [], []
        for label in range(SEGS):
            member = live
            if label > 0:
                member = member & (slots >= breaks[label - 1])
            if label < SEGS - 1:
                member = member & (slots < breaks[label])
            sums.append(jnp.sum(jnp.where(member, logprob, 0.0), axis=1, keepdims=True))
            counts.append(jnp.sum(member.astype(jnp.float32), axis=1, keepdims=True))
        return logprob, sums, counts, breaks

    partner = group ^ 1
    logprob, sums, counts, breaks = summed(group, found[0:1])
    _, partner_sums, partner_counts, _ = summed(partner, found[2:3])
    length = chosen(lengths_ref, group)
    entropy = jnp.where(slots < length, found[1:2], 0.0)
    is_even = group % 2 == 0
    joined = chosen(continues_ref, jnp.where(is_even, group, partner)) == 1
    my_last = sum((length - 1 >= begin).astype(jnp.int32) for begin in breaks)
    target = jnp.where(is_even, my_last, jnp.zeros_like(my_last))
    extra_sum, extra_count = partner_sums[0], partner_counts[0]
    for label in range(1, SEGS):
        later = jnp.logical_not(is_even) & (partner_counts[label] > 0)
        extra_sum = jnp.where(later, partner_sums[label], extra_sum)
        extra_count = jnp.where(later, partner_counts[label], extra_count)
    labels = lax.broadcasted_iota(jnp.int32, (1, SEGS), 1)
    means = jnp.zeros((1, SEGS), jnp.float32)
    for label in range(SEGS):
        update = joined & (target == label)
        total_sum = sums[label] + jnp.where(update, extra_sum, 0.0)
        total_count = counts[label] + jnp.where(update, extra_count, 0.0)
        means = jnp.where(labels == label, total_sum / jnp.maximum(total_count, 1.0), means)
    logprob_ref[...] = logprob
    entropy_ref[...] = entropy
    mean_ref[...] = means

    count, width = turned_ref.shape
    squares = jnp.zeros((1, count), jnp.float32)
    for part in range(parts):
        for core in range(CORES):
            squares += got_ref[group * parts + part, core][7:8, LANES // 2 : LANES // 2 + count]
    squares = upright(squares)
    scale = jnp.sqrt(squares / (width * shards) + NORM_EPS)
    keys_ref[...] = (turned_ref[...] / scale).astype(jnp.bfloat16)


def partners(sizes, flips):
    (groups, shards), (group_flip, shard_flip) = sizes, flips
    return [
        (g * shards + v, (g ^ group_flip) * shards + (v ^ shard_flip))
        for g in range(groups)
        for v in range(shards)
    ]


def local(
    sizes,
    final_hidden,
    norm_gain,
    head_weight,
    token_ids,
    group_lengths,
    segment_ids,
    continues,
    layer_input,
    key_weight,
    key_gain,
    positions,
    key_rows,
):
    groups, shards = sizes
    parts, half = shards // CORES, groups // 2
    cap, width = final_hidden.shape
    rows = cap // shards
    size = 2 * BAL // shards
    tokens = 2 * parts * size
    core = lax.axis_index("vocab") % CORES
    axes = ("grp", "vocab")
    swapped = sizes == (8, 4)

    def swap(array, group_flip, shard_flip):
        return lax.ppermute(array, axes, partners(sizes, (group_flip, shard_flip)))

    def lay(kernel, shape, *operands):
        return call(
            kernel,
            jax.ShapeDtypeStruct(shape, jnp.bfloat16),
            [WHOLE] * len(operands),
            size * cap * width,
            4 * size * width,
            out_specs=WHOLE,
        )(*operands)

    gap = size - rows
    hidden = (final_hidden, norm_gain.reshape(1, width))
    here = lay(functools.partial(prep_kernel, sizes, swapped), (rows, width), *hidden)

    count, key_width = key_rows.shape[0], key_weight.shape[1]
    turned, extra, *ids = call(
        functools.partial(side_kernel, sizes, swapped),
        (
            jax.ShapeDtypeStruct((count, key_width), jnp.float32),
            jax.ShapeDtypeStruct((1, LANES // 2), jnp.float32),
            jax.ShapeDtypeStruct((1, 3 * size), jnp.int32),
            jax.ShapeDtypeStruct((1, 2 * size), jnp.int32),
            jax.ShapeDtypeStruct((1, 3 * size), jnp.int32),
        ),
        [SCALARS] + [WHOLE] * 5 + [FAR, FAR],
        2 * count * width * key_width,
        2 * width * key_width,
        scratch_shapes=[
            pltpu.VMEM(layer_input.shape, jnp.bfloat16),
            pltpu.VMEM(key_weight.shape, jnp.bfloat16),
            pltpu.SemaphoreType.DMA((2,)),
        ],
    )(
        group_lengths,
        key_rows.reshape(1, count),
        positions.reshape(1, cap),
        segment_ids.reshape(1, cap),
        token_ids.reshape(1, groups * cap),
        key_gain.reshape(1, key_width),
        layer_input,
        key_weight,
    )

    head_weight, here = lax.optimization_barrier((head_weight, here))
    far_head = swap(head_weight, 0, 1)
    heads = (head_weight, far_head)
    sent_shape = jax.ShapeDtypeStruct((groups * shards, 8, LANES), jnp.float32)
    if swapped:
        other = swap(here, 4, 0)
        ends = lay(functools.partial(ends_kernel, sizes), (parts, gap, width), *hidden, here)
        across = swap(ends, 1, 0)
        beyond = swap(ends, 2, 0)
        corner = swap(ends, 3, 0)
        other, across, beyond, corner, far_head, ids, extra, turned = lax.optimization_barrier(
            (other, across, beyond, corner, far_head, ids, extra, turned)
        )
        heads = (head_weight, far_head)
        rest = lay(
            functools.partial(mix_kernel, sizes), (rows, width), group_lengths.reshape(1, groups), here, other
        )
        far_rest = swap(rest, 2, 0)
        rest_xy = swap(rest, 1, 2)
        rest_x = swap(rest, 1, 0)
        rest_y = swap(rest, 0, 2)
        far_x = swap(far_rest, 1, 0)
        far_y = swap(far_rest, 0, 2)
        far_xy = swap(rest_xy, 2, 0)
        first = score(
            functools.partial(piece_kernel, sizes, (0, 1, 0)),
            jax.ShapeDtypeStruct((8, 3 * size), jnp.float32),
            ids[0],
            heads,
            (ends, across, beyond, rest, rest_xy, far_rest),
            3 * size,
        )
        rest_y, rest_x, first = lax.optimization_barrier((rest_y, rest_x, first))
        second = score(
            functools.partial(piece_kernel, sizes, (1, 0)),
            jax.ShapeDtypeStruct((8, 2 * size), jnp.float32),
            ids[1],
            heads,
            (ends, across, rest_y, rest_x),
            2 * size,
        )
        sent = score(
            functools.partial(send_kernel, sizes),
            sent_shape,
            ids[2],
            heads,
            (first, second, extra, beyond, corner, far_y, far_x, far_xy),
            3 * size,
        )
    else:
        taken = front(group_lengths[:half, None], jnp.arange(shards)[None, :], shards)
        ids = token_ids.reshape(groups, rows, shards).transpose(0, 2, 1)
        lower = jnp.pad(ids[:half], ((0, 0), (0, 0), (0, gap)))
        upper = jnp.pad(ids[half:, ::-1, ::-1], ((0, 0), (0, 0), (gap, 0)))
        is_lower = jnp.arange(size)[None, None, :] < taken[:, :, None]
        ids = jnp.where(is_lower, lower, upper).reshape(half, parts, CORES, size)
        ids = lax.dynamic_index_in_dim(ids, core, 2, False).reshape(1, -1)
        every = lax.all_gather(here, axes).reshape(groups, parts, CORES, rows, width)
        every = lax.dynamic_index_in_dim(every, core, 2, False)
        first = jnp.pad(every[:half], ((0, 0), (0, 0), (0, gap), (0, 0)))
        second = jnp.pad(every[half:], ((0, 0), (0, 0), (gap, 0), (0, 0)))
        is_lower = is_lower.reshape(half, parts, CORES, size)
        is_lower = lax.dynamic_index_in_dim(is_lower, core, 2, False)
        every = jnp.where(is_lower[..., None], first, second)
        stats = score(
            functools.partial(plain_kernel, sizes),
            jax.ShapeDtypeStruct((8, half // 2 * tokens), jnp.float32),
            ids,
            heads,
            (every.reshape(-1, width),),
            half // 2 * tokens,
            scratch=False,
        )
        sets = half // 2
        state = [row.reshape(sets, tokens) for row in stats[:3]]
        extra = jnp.broadcast_to(extra, (sets, LANES // 2))
        stats = packed(state, extra).reshape(8, sets, LANES).transpose(1, 0, 2)
        sent = jnp.broadcast_to(
            stats[None, :, None, None], (2, sets, 2, shards, 8, LANES)
        ).reshape(sent_shape.shape)
    got = lax.all_to_all(sent, axes, 0, 0, tiled=False)

    logprob, entropy, means, keys = call(
        functools.partial(final_kernel, sizes),
        (
            jax.ShapeDtypeStruct((1, cap), jnp.float32),
            jax.ShapeDtypeStruct((1, cap), jnp.float32),
            jax.ShapeDtypeStruct((1, SEGS), jnp.float32),
            jax.ShapeDtypeStruct((count, key_width), jnp.bfloat16),
        ),
        [WHOLE] * 4,
        1 << 24,
        4 * groups * shards * 8 * LANES,
    )(
        group_lengths.reshape(1, groups),
        continues.reshape(1, groups),
        got.reshape(groups * parts, CORES, 8, LANES),
        turned,
    )
    return logprob.reshape(cap), entropy.reshape(cap), means.reshape(SEGS), keys


def solution(mesh):
    sizes = (mesh.shape["grp"], mesh.shape["vocab"])
    in_specs = (
        P("grp", None),
        P(),
        P(("vocab", "grp"), None),
        P(),
        P(),
        P("grp"),
        P(),
        P("grp", None),
        P(None, "vocab"),
        P("vocab"),
        P("grp"),
        P("grp"),
    )
    out_specs = (P("grp"), P("grp"), P("grp"), P("grp", "vocab"))
    return jax.shard_map(
        functools.partial(local, sizes),
        mesh=mesh,
        in_specs=in_specs,
        out_specs=out_specs,
        check_vma=False,
    )
```

```python
import functools

import jax
import jax.numpy as jnp
from jax import lax
from jax.experimental import pallas as pl
from jax.experimental.pallas import tpu as pltpu
from jax.sharding import PartitionSpec as P

HD = 128
SEGS = 4
BAL = 160
CORES = 2
LANES = 128
BREAKS = 31
SLOTS = (0, 3, 4, 1, 2, 5, 6, 7)

NORM_EPS = 1e-06
ROPE_BASE = 500000.0

VMEM_LIMIT = 24 * 1024 * 1024
WHOLE = pl.BlockSpec(memory_space=pltpu.VMEM)
SCALARS = pl.BlockSpec(memory_space=pltpu.SMEM)
FAR = pl.BlockSpec(memory_space=pltpu.HBM)


def call(kernel, out_shape, in_specs, flops, moved, vmem=VMEM_LIMIT, **more):
    return pl.pallas_call(
        kernel,
        out_shape=out_shape,
        in_specs=in_specs,
        compiler_params=pltpu.CompilerParams(vmem_limit_bytes=vmem),
        cost_estimate=pl.CostEstimate(flops=flops, bytes_accessed=moved, transcendentals=0),
        **more,
    )


def place_of(shards):
    shard = lax.axis_index("vocab")
    return lax.axis_index("grp"), lax.div(shard, CORES), lax.rem(shard, CORES)


def source_row(place, quarter, is_first, quarters, rows):
    return jnp.where(
        is_first,
        quarters * place + quarter,
        quarters * (rows - 1 - place) + quarters - 1 - quarter,
    )


def front(length, quarter, shards):
    return (length - quarter + shards - 1) // shards


def chosen(row_ref, index):
    row = row_ref[...]
    lane = lax.broadcasted_iota(jnp.int32, row.shape, 1)
    return jnp.sum(jnp.where(lane == index, row, 0), axis=1, keepdims=True)


def fetch(sources, targets, semaphores):
    copies = [
        pltpu.make_async_copy(source, target, semaphores.at[i])
        for i, (source, target) in enumerate(zip(sources, targets))
    ]
    for copy in copies:
        copy.start()
    return copies


def dealt(sizes, hidden_ref, gain_ref, t, rows, turned):
    groups, shards = sizes
    group, y, core = place_of(shards)
    is_first = group < groups // 2
    count = hidden_ref.shape[0] // shards
    place = lax.broadcasted_iota(jnp.int32, (rows, hidden_ref.shape[0]), 0)
    column = lax.broadcasted_iota(jnp.int32, place.shape, 1)
    if turned:
        gap = 2 * BAL // shards - count
        back = jnp.where(place < gap, place + (count - gap), place - gap)
        place = jnp.where(is_first, place, back)
    row = source_row(place, (y ^ t) * CORES + core, is_first, shards, count)
    pick = (column == row).astype(jnp.float32).astype(jnp.bfloat16)
    found = jnp.dot(pick, hidden_ref[...], preferred_element_type=jnp.float32)
    meansq = jnp.sum(found * found, axis=-1, keepdims=True) / found.shape[1]
    return (found * lax.rsqrt(meansq + NORM_EPS) * gain_ref[...]).astype(jnp.bfloat16)


def prep_kernel(sizes, turned, hidden_ref, gain_ref, out_ref):
    out_ref[...] = dealt(sizes, hidden_ref, gain_ref, 0, out_ref.shape[0], turned)


def ends_kernel(sizes, hidden_ref, gain_ref, here_ref, out_ref):
    rows = out_ref.shape[1]
    out_ref[0] = here_ref[0:rows, :]
    for t in range(1, out_ref.shape[0]):
        out_ref[t] = dealt(sizes, hidden_ref, gain_ref, t, rows, True)


def mix_kernel(sizes, lengths_ref, here_ref, other_ref, out_ref):
    groups, shards = sizes
    half = groups // 2
    group, y, core = place_of(shards)
    rows, width = here_ref.shape
    gap = 2 * BAL // shards - rows
    length = front(chosen(lengths_ref, lax.rem(group, half)), y * CORES + core, shards)
    is_lower = lax.broadcasted_iota(jnp.int32, (rows - gap, width), 0) + gap < length

    def lay(lower_ref, upper_ref):
        lower, upper = (ref[gap:rows, :].astype(jnp.float32) for ref in (lower_ref, upper_ref))
        out_ref[0 : rows - gap, :] = jnp.where(is_lower, lower, upper).astype(jnp.bfloat16)

    @pl.when(group < half)
    def _():
        lay(here_ref, other_ref)

    @pl.when(group >= half)
    def _():
        lay(other_ref, here_ref)

    out_ref[rows - gap : rows, :] = other_ref[0:gap, :]


def gather_pieces(sizes, pieces, tokens_ref):
    is_first = lax.axis_index("grp") < sizes[0] // 2
    start = 0
    for end, rest_ref in pieces:
        gap, rows = end.shape[0], rest_ref.shape[0]
        last = start + rows
        own, partner = jnp.where(is_first, start, last), jnp.where(is_first, last, start)
        tokens_ref[pl.ds(pl.multiple_of(own, 16), gap), :] = end[...]
        tokens_ref[start + gap : last, :] = rest_ref[0 : rows - gap, :]
        tokens_ref[pl.ds(pl.multiple_of(partner, 16), gap), :] = rest_ref[rows - gap : rows, :]
        start += gap + rows
    return tokens_ref[...]


def statistics(bases, targets, tokens, heads):
    vocab = heads[0].shape[0]
    cuts = [0, vocab]
    if vocab % 16 == 0:
        cuts = [vocab * i // 2 // 16 * 16 for i in range(2)] + [vocab]
    chunks = [
        (base + start, head_ref, start, stop)
        for base, head_ref in zip(bases, heads)
        for start, stop in zip(cuts, cuts[1:])
    ]

    def logits_of(chunk):
        _, head_ref, start, stop = chunk
        product = lax.dot_general(
            head_ref[start:stop, :], tokens, (((1,), (1,)), ((), ())), preferred_element_type=jnp.float32
        )
        return product.astype(jnp.bfloat16).astype(jnp.float32)

    state = None
    ready = [logits_of(chunk) for chunk in chunks[:1]]
    for i, chunk in enumerate(chunks):
        if i + 1 < len(chunks):
            ready.append(logits_of(chunks[i + 1]))
        logits = ready[i]
        entry = lax.broadcasted_iota(jnp.int32, logits.shape, 0)
        found = jnp.where(entry == targets - chunk[0], logits, 0.0)
        picked = jnp.sum(found, axis=0, keepdims=True)
        top = jnp.max(logits, axis=0, keepdims=True)
        if state is not None:
            top = jnp.maximum(top, state[0])
        shifted = jnp.exp(logits - top)
        expsum = jnp.sum(shifted, axis=0, keepdims=True)
        moment = jnp.sum(shifted * logits, axis=0, keepdims=True)
        if state is not None:
            scale = jnp.exp(state[0] - top)
            expsum += state[1] * scale
            moment += state[2] * scale
            picked += state[3]
        state = (top, expsum, moment, picked)
    top, expsum, moment, picked = state
    return top + jnp.log(expsum), moment / expsum, picked


def packed(state, extra):
    flat = [row[:, : 2 * LANES] for row in state] + [row[:, 2 * LANES :] for row in state] + [extra]
    flat = jnp.concatenate(flat, axis=1)
    return jnp.concatenate(
        [flat[:, i : i + LANES] for i in range(0, flat.shape[1], LANES)], axis=0
    )


def merged(every):
    half = LANES // 2
    row = lax.broadcasted_iota(jnp.int32, every.shape[1:], 0)
    top = jnp.max(every, axis=0)
    scale = jnp.exp(every - top[None])
    means = [
        jnp.where(row == 6, pltpu.roll(one, half, 1), pltpu.roll(one, one.shape[0] - 2, 0))
        for one in (every[i] for i in range(every.shape[0]))
    ]
    expsum = jnp.sum(scale, axis=0)
    moment = sum(scale[i] * mean for i, mean in enumerate(means))
    picked = jnp.sum(every, axis=0)
    lse = top + jnp.log(expsum)
    entropy = lse - moment / expsum

    def lay(block, first, last):
        return jnp.concatenate([block[first : first + 1], block[first + 1 : first + 2], last], axis=1)

    lse_row = lay(lse, 0, lse[6:7, :half])
    return jnp.concatenate(
        [lay(picked, 4, picked[7:8, :half]) - lse_row, lay(entropy, 0, entropy[6:7, :half])], axis=0
    )


def bases_of(sizes, head_ref):
    groups, shards = sizes
    group, shard = lax.axis_index("grp"), lax.axis_index("vocab")
    return [((shard ^ flip) * groups + group) * head_ref.shape[0] for flip in (0, 1)]


def rows_of(state, out_ref):
    rows = jnp.concatenate([*state, jnp.zeros((5, out_ref.shape[1]), jnp.float32)], axis=0)
    out_ref[...] = rows


def plain_kernel(sizes, targets_ref, near_ref, far_ref, tokens_ref, out_ref):
    state = statistics(
        bases_of(sizes, near_ref), targets_ref[...], tokens_ref[...], (near_ref, far_ref)
    )
    rows_of(state, out_ref)


def piece_kernel(sizes, picks, targets_ref, near_ref, far_ref, *refs):
    *pieces, out_ref, tokens_ref = refs
    ends = [ref.at[which] for ref, which in zip(pieces, picks)]
    tokens = gather_pieces(sizes, zip(ends, pieces[len(picks) :]), tokens_ref)
    state = statistics(bases_of(sizes, near_ref), targets_ref[...], tokens, (near_ref, far_ref))
    rows_of(state, out_ref)


def send_kernel(
    sizes, targets_ref, near_ref, far_ref, first_ref, second_ref, extra_ref, beyond_ref, corner_ref, *refs
):
    *rests, out_ref, tokens_ref = refs
    groups, shards = sizes
    size = 2 * BAL // shards
    ends = (beyond_ref.at[1], corner_ref.at[0], corner_ref.at[1])
    tokens = gather_pieces(sizes, zip(ends, rests), tokens_ref)
    state = statistics(bases_of(sizes, near_ref), targets_ref[...], tokens, (near_ref, far_ref))
    group, y, _ = place_of(shards)

    def settled(rows):
        turned = jnp.concatenate([rows[:, 2 * size :], rows[:, : 2 * size]], axis=1)
        rows = jnp.where(lax.rem(group, 2) == 1, turned, rows)
        quarters = [rows[:, i * size : (i + 1) * size] for i in (1, 0, 3, 2)]
        return jnp.where(y == 1, jnp.concatenate(quarters, axis=1), rows)

    first, second = first_ref[0:4, :], second_ref[0:4, :]
    third = jnp.concatenate([*state, jnp.zeros_like(state[0])], axis=0)
    own = settled(jnp.concatenate([first[:, :size], second, first[:, size : 2 * size]], axis=1))
    beyond = settled(jnp.concatenate([first[:, 2 * size :], third], axis=1))
    own, beyond = (
        packed([rows[i : i + 1] for i in range(3)], extra_ref[...]) for rows in (own, beyond)
    )
    mine = lax.div(lax.rem(group, groups // 2), 2)
    for which in range(groups // 4):
        block = jnp.where(mine == which, own, beyond)
        for group in range(groups):
            if group % (groups // 2) // 2 == which:
                for shard in range(shards):
                    out_ref[group * shards + shard] = block


def score(kernel, out_shape, targets, heads, extras, count, scratch=True):
    vocab, width = heads[0].shape
    return call(
        kernel,
        out_shape,
        [WHOLE] * (3 + len(extras)),
        4 * vocab * count * width,
        4 * vocab * width + 2 * count * width,
        out_specs=WHOLE,
        scratch_shapes=[pltpu.VMEM((count, width), jnp.bfloat16)] if scratch else [],
    )(targets, *heads, *extras)


def upright(row):
    count = row.shape[1]
    diagonal = lax.broadcasted_iota(jnp.int32, (count, count), 0) == lax.broadcasted_iota(
        jnp.int32, (count, count), 1
    )
    return jnp.sum(jnp.where(diagonal, row, 0), axis=1, keepdims=True)


def side_kernel(
    sizes,
    swapped,
    lengths_ref,
    rows_ref,
    positions_ref,
    segments_ref,
    ids_ref,
    gain_ref,
    input_hbm,
    weight_hbm,
    turned_ref,
    extra_ref,
    first_ref,
    second_ref,
    third_ref,
    input_ref,
    weight_ref,
    semaphores,
):
    groups, shards = sizes
    copies = fetch((input_hbm, weight_hbm), (input_ref, weight_ref), semaphores)
    cap = segments_ref.shape[1]
    if swapped:
        tokens = first_ref.shape[1] + second_ref.shape[1] // 2
        half, size = groups // 2, 2 * BAL // shards
        group, y, core = place_of(shards)
        lane = lax.broadcasted_iota(jnp.int32, (1, 2 * tokens), 1)
        row = jnp.zeros((1, 2 * tokens), jnp.int32)
        source = jnp.zeros((1, 2 * tokens), jnp.int32)
        for start, slot in enumerate(SLOTS):
            place = lane - start * size
            here = (place >= 0) & (place < size)
            lower = lax.rem(group, half) ^ (slot // 4 * 2) ^ (slot // 2 % 2)
            quarter = (y ^ (slot % 2)) * CORES + core
            is_lower = place < front(lengths_ref[lower], quarter, shards)
            stands = jnp.where(
                is_lower, shards * place + quarter, shards * (size - 1 - place) + shards - 1 - quarter
            )
            row = jnp.where(here, stands, row)
            source = jnp.where(here, jnp.where(is_lower, lower, lower + half), source)
        ids = jnp.concatenate([ids_ref[0:1, g * cap : (g + 1) * cap] for g in range(groups)], axis=0)
        halves = jnp.concatenate([ids >> 8, ids & 255], axis=0)
        stood = lax.broadcasted_iota(jnp.int32, (cap, 2 * tokens), 0)
        pick = (stood == row).astype(jnp.float32).astype(jnp.bfloat16)
        found = jnp.dot(
            halves.astype(jnp.float32).astype(jnp.bfloat16), pick, preferred_element_type=jnp.float32
        )
        found = found[:groups] * 256.0 + found[groups:]
        of_group = lax.broadcasted_iota(jnp.int32, found.shape, 0) == source
        targets = jnp.sum(jnp.where(of_group, found, 0.0), axis=0, keepdims=True).astype(jnp.int32)
        start = 0
        for ref in (first_ref, second_ref, third_ref):
            ref[...] = targets[:, start : start + ref.shape[1]]
            start += ref.shape[1]
    else:
        for ref in (first_ref, second_ref, third_ref):
            ref[...] = jnp.zeros_like(ref)

    count, width = turned_ref.shape
    column = lax.broadcasted_iota(jnp.int32, (count, cap), 1)
    chosen = column == upright(rows_ref[...])
    places = jnp.sum(jnp.where(chosen, positions_ref[...], 0), axis=1, keepdims=True)
    half_head = HD // 2
    steps = lax.broadcasted_iota(jnp.int32, (count, half_head), 1).astype(jnp.float32)
    freqs = jnp.exp(-(2.0 * steps / HD) * jnp.log(jnp.full(steps.shape, ROPE_BASE, jnp.float32)))
    angles = places.astype(jnp.float32) * freqs
    cosine, sine = jnp.cos(angles), jnp.sin(angles)
    cosine = jnp.concatenate([cosine, cosine], axis=1)
    sine = jnp.concatenate([-sine, sine], axis=1)
    for copy in copies:
        copy.wait()
    pick = chosen.astype(jnp.float32).astype(jnp.bfloat16)
    rows = jnp.dot(pick, input_ref[...], preferred_element_type=jnp.float32).astype(jnp.bfloat16)
    projected = jnp.dot(rows, weight_ref[...], preferred_element_type=jnp.float32)
    squares = jnp.sum(projected * projected, axis=1, keepdims=True)
    lane = lax.broadcasted_iota(jnp.int32, (count, extra_ref.shape[1]), 1)
    diagonal = lax.broadcasted_iota(jnp.int32, lane.shape, 0) == lane
    extra = jnp.sum(jnp.where(diagonal, squares, 0.0), axis=0, keepdims=True)
    for label in range(1, SEGS):
        before = (segments_ref[...] < label).astype(jnp.float32)
        before = jnp.sum(before, axis=1, keepdims=True)
        extra = jnp.where(lane[0:1] == BREAKS + label, before, extra)
    extra_ref[...] = extra
    gained = projected * gain_ref[...]
    for start in range(0, width, HD):
        head = gained[:, start : start + HD]
        turned_ref[:, start : start + HD] = head * cosine + pltpu.roll(head, half_head, 1) * sine


def final_kernel(
    sizes,
    lengths_ref,
    continues_ref,
    got_ref,
    turned_ref,
    logprob_ref,
    entropy_ref,
    mean_ref,
    keys_ref,
):
    groups, shards = sizes
    parts, group = shards // CORES, lax.axis_index("grp")
    cap = logprob_ref.shape[1]
    size = 2 * BAL // shards
    tokens = 2 * parts * size
    columns = [merged(got_ref[:, core]) for core in range(CORES)]

    column, span = lax.rem(group, 2), tokens // 2
    halves = [[both[:, :span], both[:, span:]] for both in columns]
    own = jnp.concatenate([jnp.where(column == 0, a, b) for a, b in halves], axis=1)
    beside = jnp.concatenate([jnp.where(column == 0, b, a) for a, b in halves], axis=1)
    rest = jnp.concatenate([own, beside], axis=0)
    terms = []
    for _ in range(3):
        term = rest.astype(jnp.bfloat16).astype(jnp.float32)
        terms.append(term)
        rest = rest - term
    terms = jnp.concatenate(terms + [jnp.zeros_like(rest)], axis=0).astype(jnp.bfloat16)

    slots = lax.broadcasted_iota(jnp.int32, (1, cap), 1)
    is_first = group < groups // 2
    quarter = jnp.where(is_first, slots % shards, shards - 1 - slots % shards)
    place = jnp.where(is_first, slots // shards, size - 1 - slots // shards)
    home = quarter % CORES * span + quarter // CORES * size + place
    stood = lax.broadcasted_iota(jnp.int32, (CORES * span, cap), 0)
    pick = (stood == home).astype(jnp.float32).astype(jnp.bfloat16)
    found = jnp.dot(terms, pick, preferred_element_type=jnp.float32)
    found = found[0:4] + found[4:8] + found[8:12]
    def summed(who, logprob):
        note = got_ref[who * parts, 0][7:8, LANES // 2 :]
        breaks = [note[:, BREAKS + i : BREAKS + i + 1].astype(jnp.int32) for i in range(1, SEGS)]
        live = slots < chosen(lengths_ref, who)
        logprob = jnp.where(live, logprob, 0.0)
        sums, counts = [], []
        for label in range(SEGS):
            member = live
            if label > 0:
                member = member & (slots >= breaks[label - 1])
            if label < SEGS - 1:
                member = member & (slots < breaks[label])
            sums.append(jnp.sum(jnp.where(member, logprob, 0.0), axis=1, keepdims=True))
            counts.append(jnp.sum(member.astype(jnp.float32), axis=1, keepdims=True))
        return logprob, sums, counts, breaks

    partner = group ^ 1
    logprob, sums, counts, breaks = summed(group, found[0:1])
    _, partner_sums, partner_counts, _ = summed(partner, found[2:3])
    length = chosen(lengths_ref, group)
    entropy = jnp.where(slots < length, found[1:2], 0.0)
    is_even = group % 2 == 0
    joined = chosen(continues_ref, jnp.where(is_even, group, partner)) == 1
    my_last = sum((length - 1 >= begin).astype(jnp.int32) for begin in breaks)
    target = jnp.where(is_even, my_last, jnp.zeros_like(my_last))
    extra_sum, extra_count = partner_sums[0], partner_counts[0]
    for label in range(1, SEGS):
        later = jnp.logical_not(is_even) & (partner_counts[label] > 0)
        extra_sum = jnp.where(later, partner_sums[label], extra_sum)
        extra_count = jnp.where(later, partner_counts[label], extra_count)
    labels = lax.broadcasted_iota(jnp.int32, (1, SEGS), 1)
    means = jnp.zeros((1, SEGS), jnp.float32)
    for label in range(SEGS):
        update = joined & (target == label)
        total_sum = sums[label] + jnp.where(update, extra_sum, 0.0)
        total_count = counts[label] + jnp.where(update, extra_count, 0.0)
        means = jnp.where(labels == label, total_sum / jnp.maximum(total_count, 1.0), means)
    logprob_ref[...] = logprob
    entropy_ref[...] = entropy
    mean_ref[...] = means

    count, width = turned_ref.shape
    squares = jnp.zeros((1, count), jnp.float32)
    for part in range(parts):
        for core in range(CORES):
            squares += got_ref[group * parts + part, core][7:8, LANES // 2 : LANES // 2 + count]
    squares = upright(squares)
    scale = jnp.sqrt(squares / (width * shards) + NORM_EPS)
    keys_ref[...] = (turned_ref[...] / scale).astype(jnp.bfloat16)


def partners(sizes, flips):
    (groups, shards), (group_flip, shard_flip) = sizes, flips
    return [
        (g * shards + v, (g ^ group_flip) * shards + (v ^ shard_flip))
        for g in range(groups)
        for v in range(shards)
    ]


def local(
    sizes,
    final_hidden,
    norm_gain,
    head_weight,
    token_ids,
    group_lengths,
    segment_ids,
    continues,
    layer_input,
    key_weight,
    key_gain,
    positions,
    key_rows,
):
    groups, shards = sizes
    parts, half = shards // CORES, groups // 2
    cap, width = final_hidden.shape
    rows = cap // shards
    size = 2 * BAL // shards
    tokens = 2 * parts * size
    core = lax.axis_index("vocab") % CORES
    axes = ("grp", "vocab")
    swapped = sizes == (8, 4)

    def swap(array, group_flip, shard_flip):
        return lax.ppermute(array, axes, partners(sizes, (group_flip, shard_flip)))

    def lay(kernel, shape, *operands):
        return call(
            kernel,
            jax.ShapeDtypeStruct(shape, jnp.bfloat16),
            [WHOLE] * len(operands),
            size * cap * width,
            4 * size * width,
            out_specs=WHOLE,
        )(*operands)

    gap = size - rows
    hidden = (final_hidden, norm_gain.reshape(1, width))
    here = lay(functools.partial(prep_kernel, sizes, swapped), (rows, width), *hidden)

    count, key_width = key_rows.shape[0], key_weight.shape[1]
    turned, extra, *ids = call(
        functools.partial(side_kernel, sizes, swapped),
        (
            jax.ShapeDtypeStruct((count, key_width), jnp.float32),
            jax.ShapeDtypeStruct((1, LANES // 2), jnp.float32),
            jax.ShapeDtypeStruct((1, 3 * size), jnp.int32),
            jax.ShapeDtypeStruct((1, 2 * size), jnp.int32),
            jax.ShapeDtypeStruct((1, 3 * size), jnp.int32),
        ),
        [SCALARS] + [WHOLE] * 5 + [FAR, FAR],
        2 * count * width * key_width,
        2 * width * key_width,
        scratch_shapes=[
            pltpu.VMEM(layer_input.shape, jnp.bfloat16),
            pltpu.VMEM(key_weight.shape, jnp.bfloat16),
            pltpu.SemaphoreType.DMA((2,)),
        ],
    )(
        group_lengths,
        key_rows.reshape(1, count),
        positions.reshape(1, cap),
        segment_ids.reshape(1, cap),
        token_ids.reshape(1, groups * cap),
        key_gain.reshape(1, key_width),
        layer_input,
        key_weight,
    )

    head_weight, here = lax.optimization_barrier((head_weight, here))
    far_head = swap(head_weight, 0, 1)
    heads = (head_weight, far_head)
    sent_shape = jax.ShapeDtypeStruct((groups * shards, 8, LANES), jnp.float32)
    if swapped:
        other = swap(here, 4, 0)
        ends = lay(functools.partial(ends_kernel, sizes), (parts, gap, width), *hidden, here)
        across = swap(ends, 1, 0)
        beyond = swap(ends, 2, 0)
        corner = swap(ends, 3, 0)
        other, across, beyond, corner, far_head, ids, extra, turned = lax.optimization_barrier(
            (other, across, beyond, corner, far_head, ids, extra, turned)
        )
        heads = (head_weight, far_head)
        rest = lay(
            functools.partial(mix_kernel, sizes), (rows, width), group_lengths.reshape(1, groups), here, other
        )
        far_rest = swap(rest, 2, 0)
        rest_xy = swap(rest, 1, 2)
        rest_x = swap(rest, 1, 0)
        rest_y = swap(rest, 0, 2)
        far_x = swap(far_rest, 1, 0)
        far_y = swap(far_rest, 0, 2)
        far_xy = swap(rest_xy, 2, 0)
        first = score(
            functools.partial(piece_kernel, sizes, (0, 1, 0)),
            jax.ShapeDtypeStruct((8, 3 * size), jnp.float32),
            ids[0],
            heads,
            (ends, across, beyond, rest, rest_xy, far_rest),
            3 * size,
        )
        rest_y, rest_x, first = lax.optimization_barrier((rest_y, rest_x, first))
        second = score(
            functools.partial(piece_kernel, sizes, (1, 0)),
            jax.ShapeDtypeStruct((8, 2 * size), jnp.float32),
            ids[1],
            heads,
            (ends, across, rest_y, rest_x),
            2 * size,
        )
        sent = score(
            functools.partial(send_kernel, sizes),
            sent_shape,
            ids[2],
            heads,
            (first, second, extra, beyond, corner, far_y, far_x, far_xy),
            3 * size,
        )
    else:
        taken = front(group_lengths[:half, None], jnp.arange(shards)[None, :], shards)
        ids = token_ids.reshape(groups, rows, shards).transpose(0, 2, 1)
        lower = jnp.pad(ids[:half], ((0, 0), (0, 0), (0, gap)))
        upper = jnp.pad(ids[half:, ::-1, ::-1], ((0, 0), (0, 0), (gap, 0)))
        is_lower = jnp.arange(size)[None, None, :] < taken[:, :, None]
        ids = jnp.where(is_lower, lower, upper).reshape(half, parts, CORES, size)
        ids = lax.dynamic_index_in_dim(ids, core, 2, False).reshape(1, -1)
        every = lax.all_gather(here, axes).reshape(groups, parts, CORES, rows, width)
        every = lax.dynamic_index_in_dim(every, core, 2, False)
        first = jnp.pad(every[:half], ((0, 0), (0, 0), (0, gap), (0, 0)))
        second = jnp.pad(every[half:], ((0, 0), (0, 0), (gap, 0), (0, 0)))
        is_lower = is_lower.reshape(half, parts, CORES, size)
        is_lower = lax.dynamic_index_in_dim(is_lower, core, 2, False)
        every = jnp.where(is_lower[..., None], first, second)
        stats = score(
            functools.partial(plain_kernel, sizes),
            jax.ShapeDtypeStruct((8, half // 2 * tokens), jnp.float32),
            ids,
            heads,
            (every.reshape(-1, width),),
            half // 2 * tokens,
            scratch=False,
        )
        sets = half // 2
        state = [row.reshape(sets, tokens) for row in stats[:3]]
        extra = jnp.broadcast_to(extra, (sets, LANES // 2))
        stats = packed(state, extra).reshape(8, sets, LANES).transpose(1, 0, 2)
        sent = jnp.broadcast_to(
            stats[None, :, None, None], (2, sets, 2, shards, 8, LANES)
        ).reshape(sent_shape.shape)
    got = lax.all_to_all(sent, axes, 0, 0, tiled=False)

    logprob, entropy, means, keys = call(
        functools.partial(final_kernel, sizes),
        (
            jax.ShapeDtypeStruct((1, cap), jnp.float32),
            jax.ShapeDtypeStruct((1, cap), jnp.float32),
            jax.ShapeDtypeStruct((1, SEGS), jnp.float32),
            jax.ShapeDtypeStruct((count, key_width), jnp.bfloat16),
        ),
        [WHOLE] * 4,
        1 << 24,
        4 * groups * shards * 8 * LANES,
    )(
        group_lengths.reshape(1, groups),
        continues.reshape(1, groups),
        got.reshape(groups * parts, CORES, 8, LANES),
        turned,
    )
    return logprob.reshape(cap), entropy.reshape(cap), means.reshape(SEGS), keys


def solution(mesh):
    sizes = (mesh.shape["grp"], mesh.shape["vocab"])
    in_specs = (
        P("grp", None),
        P(),
        P(("vocab", "grp"), None),
        P(),
        P(),
        P("grp"),
        P(),
        P("grp", None),
        P(None, "vocab"),
        P("vocab"),
        P("grp"),
        P("grp"),
    )
    out_specs = (P("grp"), P("grp"), P("grp"), P("grp", "vocab"))
    return jax.shard_map(
        functools.partial(local, sizes),
        mesh=mesh,
        in_specs=in_specs,
        out_specs=out_specs,
        check_vma=False,
    )
```

```python
import functools

import jax
import jax.numpy as jnp
from jax import lax
from jax.experimental import pallas as pl
from jax.experimental.pallas import tpu as pltpu
from jax.sharding import PartitionSpec as P

HD = 128
SEGS = 4
BAL = 160
CORES = 2
LANES = 128
BREAKS = 31
SLOTS = (0, 3, 4, 1, 2, 5, 6, 7)

NORM_EPS = 1e-06
ROPE_BASE = 500000.0

VMEM_LIMIT = 24 * 1024 * 1024
WHOLE = pl.BlockSpec(memory_space=pltpu.VMEM)
SCALARS = pl.BlockSpec(memory_space=pltpu.SMEM)
FAR = pl.BlockSpec(memory_space=pltpu.HBM)


def call(kernel, out_shape, in_specs, flops, moved, vmem=VMEM_LIMIT, **more):
    return pl.pallas_call(
        kernel,
        out_shape=out_shape,
        in_specs=in_specs,
        compiler_params=pltpu.CompilerParams(vmem_limit_bytes=vmem),
        cost_estimate=pl.CostEstimate(flops=flops, bytes_accessed=moved, transcendentals=0),
        **more,
    )


def place_of(shards):
    shard = lax.axis_index("vocab")
    return lax.axis_index("grp"), lax.div(shard, CORES), lax.rem(shard, CORES)


def source_row(place, quarter, is_first, quarters, rows):
    return jnp.where(
        is_first,
        quarters * place + quarter,
        quarters * (rows - 1 - place) + quarters - 1 - quarter,
    )


def front(length, quarter, shards):
    return (length - quarter + shards - 1) // shards


def chosen(row_ref, index):
    row = row_ref[...]
    lane = lax.broadcasted_iota(jnp.int32, row.shape, 1)
    return jnp.sum(jnp.where(lane == index, row, 0), axis=1, keepdims=True)


def fetch(sources, targets, semaphores):
    copies = [
        pltpu.make_async_copy(source, target, semaphores.at[i])
        for i, (source, target) in enumerate(zip(sources, targets))
    ]
    for copy in copies:
        copy.start()
    return copies


def dealt(sizes, hidden_ref, gain_ref, t, rows, turned):
    groups, shards = sizes
    group, y, core = place_of(shards)
    is_first = group < groups // 2
    count = hidden_ref.shape[0] // shards
    place = lax.broadcasted_iota(jnp.int32, (rows, hidden_ref.shape[0]), 0)
    column = lax.broadcasted_iota(jnp.int32, place.shape, 1)
    if turned:
        gap = 2 * BAL // shards - count
        back = jnp.where(place < gap, place + (count - gap), place - gap)
        place = jnp.where(is_first, place, back)
    row = source_row(place, (y ^ t) * CORES + core, is_first, shards, count)
    pick = (column == row).astype(jnp.float32).astype(jnp.bfloat16)
    found = jnp.dot(pick, hidden_ref[...], preferred_element_type=jnp.float32)
    meansq = jnp.sum(found * found, axis=-1, keepdims=True) / found.shape[1]
    return (found * lax.rsqrt(meansq + NORM_EPS) * gain_ref[...]).astype(jnp.bfloat16)


def prep_kernel(sizes, turned, hidden_ref, gain_ref, out_ref):
    out_ref[...] = dealt(sizes, hidden_ref, gain_ref, 0, out_ref.shape[0], turned)


def ends_kernel(sizes, hidden_ref, gain_ref, here_ref, out_ref):
    rows = out_ref.shape[1]
    out_ref[0] = here_ref[0:rows, :]
    for t in range(1, out_ref.shape[0]):
        out_ref[t] = dealt(sizes, hidden_ref, gain_ref, t, rows, True)


def mix_kernel(sizes, lengths_ref, here_ref, other_ref, out_ref):
    groups, shards = sizes
    half = groups // 2
    group, y, core = place_of(shards)
    rows, width = here_ref.shape
    gap = 2 * BAL // shards - rows
    length = front(chosen(lengths_ref, lax.rem(group, half)), y * CORES + core, shards)
    is_lower = lax.broadcasted_iota(jnp.int32, (rows - gap, width), 0) + gap < length

    def lay(lower_ref, upper_ref):
        lower, upper = (ref[gap:rows, :].astype(jnp.float32) for ref in (lower_ref, upper_ref))
        out_ref[0 : rows - gap, :] = jnp.where(is_lower, lower, upper).astype(jnp.bfloat16)

    @pl.when(group < half)
    def _():
        lay(here_ref, other_ref)

    @pl.when(group >= half)
    def _():
        lay(other_ref, here_ref)

    out_ref[rows - gap : rows, :] = other_ref[0:gap, :]


def gather_pieces(sizes, pieces, tokens_ref):
    is_first = lax.axis_index("grp") < sizes[0] // 2
    start = 0
    for end, rest_ref in pieces:
        gap, rows = end.shape[0], rest_ref.shape[0]
        last = start + rows
        own, partner = jnp.where(is_first, start, last), jnp.where(is_first, last, start)
        tokens_ref[pl.ds(pl.multiple_of(own, 16), gap), :] = end[...]
        tokens_ref[start + gap : last, :] = rest_ref[0 : rows - gap, :]
        tokens_ref[pl.ds(pl.multiple_of(partner, 16), gap), :] = rest_ref[rows - gap : rows, :]
        start += gap + rows
    return tokens_ref[...]


def statistics(bases, targets, tokens, heads):
    vocab = heads[0].shape[0]
    cuts = [0, vocab]
    if vocab % 16 == 0:
        cuts = [vocab * i // 2 // 16 * 16 for i in range(2)] + [vocab]
    chunks = [
        (base + start, head_ref, start, stop)
        for base, head_ref in zip(bases, heads)
        for start, stop in zip(cuts, cuts[1:])
    ]

    def logits_of(chunk):
        _, head_ref, start, stop = chunk
        product = lax.dot_general(
            head_ref[start:stop, :], tokens, (((1,), (1,)), ((), ())), preferred_element_type=jnp.float32
        )
        return product.astype(jnp.bfloat16).astype(jnp.float32)

    state = None
    ready = [logits_of(chunk) for chunk in chunks[:1]]
    for i, chunk in enumerate(chunks):
        if i + 1 < len(chunks):
            ready.append(logits_of(chunks[i + 1]))
        logits = ready[i]
        entry = lax.broadcasted_iota(jnp.int32, logits.shape, 0)
        found = jnp.where(entry == targets - chunk[0], logits, 0.0)
        picked = jnp.sum(found, axis=0, keepdims=True)
        top = jnp.max(logits, axis=0, keepdims=True)
        if state is not None:
            top = jnp.maximum(top, state[0])
        shifted = jnp.exp(logits - top)
        expsum = jnp.sum(shifted, axis=0, keepdims=True)
        moment = jnp.sum(shifted * logits, axis=0, keepdims=True)
        if state is not None:
            scale = jnp.exp(state[0] - top)
            expsum += state[1] * scale
            moment += state[2] * scale
            picked += state[3]
        state = (top, expsum, moment, picked)
    top, expsum, moment, picked = state
    return top + jnp.log(expsum), moment / expsum, picked


def packed(state, extra):
    flat = [row[:, : 2 * LANES] for row in state] + [row[:, 2 * LANES :] for row in state] + [extra]
    flat = jnp.concatenate(flat, axis=1)
    return jnp.concatenate(
        [flat[:, i : i + LANES] for i in range(0, flat.shape[1], LANES)], axis=0
    )


def merged(every):
    half = LANES // 2
    row = lax.broadcasted_iota(jnp.int32, every.shape[1:], 0)
    top = jnp.max(every, axis=0)
    scale = jnp.exp(every - top[None])
    means = [
        jnp.where(row == 6, pltpu.roll(one, half, 1), pltpu.roll(one, one.shape[0] - 2, 0))
        for one in (every[i] for i in range(every.shape[0]))
    ]
    expsum = jnp.sum(scale, axis=0)
    moment = sum(scale[i] * mean for i, mean in enumerate(means))
    picked = jnp.sum(every, axis=0)
    lse = top + jnp.log(expsum)
    entropy = lse - moment / expsum

    def lay(block, first, last):
        return jnp.concatenate([block[first : first + 1], block[first + 1 : first + 2], last], axis=1)

    lse_row = lay(lse, 0, lse[6:7, :half])
    return jnp.concatenate(
        [lay(picked, 4, picked[7:8, :half]) - lse_row, lay(entropy, 0, entropy[6:7, :half])], axis=0
    )


def bases_of(sizes, head_ref):
    groups, shards = sizes
    group, shard = lax.axis_index("grp"), lax.axis_index("vocab")
    return [((shard ^ flip) * groups + group) * head_ref.shape[0] for flip in (0, 1)]


def rows_of(state, out_ref):
    rows = jnp.concatenate([*state, jnp.zeros((5, out_ref.shape[1]), jnp.float32)], axis=0)
    out_ref[...] = rows


def plain_kernel(sizes, targets_ref, near_ref, far_ref, tokens_ref, out_ref):
    state = statistics(
        bases_of(sizes, near_ref), targets_ref[...], tokens_ref[...], (near_ref, far_ref)
    )
    rows_of(state, out_ref)


def piece_kernel(sizes, picks, targets_ref, near_ref, far_ref, *refs):
    *pieces, out_ref, tokens_ref = refs
    ends = [ref.at[which] for ref, which in zip(pieces, picks)]
    tokens = gather_pieces(sizes, zip(ends, pieces[len(picks) :]), tokens_ref)
    state = statistics(bases_of(sizes, near_ref), targets_ref[...], tokens, (near_ref, far_ref))
    rows_of(state, out_ref)


def send_kernel(
    sizes, targets_ref, near_ref, far_ref, first_ref, second_ref, extra_ref, beyond_ref, corner_ref, *refs
):
    *rests, out_ref, tokens_ref = refs
    groups, shards = sizes
    size = 2 * BAL // shards
    ends = (beyond_ref.at[1], corner_ref.at[0], corner_ref.at[1])
    tokens = gather_pieces(sizes, zip(ends, rests), tokens_ref)
    state = statistics(bases_of(sizes, near_ref), targets_ref[...], tokens, (near_ref, far_ref))
    group, y, _ = place_of(shards)

    def settled(rows):
        turned = jnp.concatenate([rows[:, 2 * size :], rows[:, : 2 * size]], axis=1)
        rows = jnp.where(lax.rem(group, 2) == 1, turned, rows)
        quarters = [rows[:, i * size : (i + 1) * size] for i in (1, 0, 3, 2)]
        return jnp.where(y == 1, jnp.concatenate(quarters, axis=1), rows)

    first, second = first_ref[0:4, :], second_ref[0:4, :]
    third = jnp.concatenate([*state, jnp.zeros_like(state[0])], axis=0)
    own = settled(jnp.concatenate([first[:, :size], second, first[:, size : 2 * size]], axis=1))
    beyond = settled(jnp.concatenate([first[:, 2 * size :], third], axis=1))
    own, beyond = (
        packed([rows[i : i + 1] for i in range(3)], extra_ref[...]) for rows in (own, beyond)
    )
    mine = lax.div(lax.rem(group, groups // 2), 2)
    for which in range(groups // 4):
        block = jnp.where(mine == which, own, beyond)
        for group in range(groups):
            if group % (groups // 2) // 2 == which:
                for shard in range(shards):
                    out_ref[shard * groups + group] = block


def score(kernel, out_shape, targets, heads, extras, count, scratch=True):
    vocab, width = heads[0].shape
    return call(
        kernel,
        out_shape,
        [WHOLE] * (3 + len(extras)),
        4 * vocab * count * width,
        4 * vocab * width + 2 * count * width,
        out_specs=WHOLE,
        scratch_shapes=[pltpu.VMEM((count, width), jnp.bfloat16)] if scratch else [],
    )(targets, *heads, *extras)


def upright(row):
    count = row.shape[1]
    diagonal = lax.broadcasted_iota(jnp.int32, (count, count), 0) == lax.broadcasted_iota(
        jnp.int32, (count, count), 1
    )
    return jnp.sum(jnp.where(diagonal, row, 0), axis=1, keepdims=True)


def side_kernel(
    sizes,
    swapped,
    lengths_ref,
    rows_ref,
    positions_ref,
    segments_ref,
    ids_ref,
    gain_ref,
    input_hbm,
    weight_hbm,
    turned_ref,
    extra_ref,
    first_ref,
    second_ref,
    third_ref,
    input_ref,
    weight_ref,
    semaphores,
):
    groups, shards = sizes
    copies = fetch((input_hbm, weight_hbm), (input_ref, weight_ref), semaphores)
    cap = segments_ref.shape[1]
    if swapped:
        tokens = first_ref.shape[1] + second_ref.shape[1] // 2
        half, size = groups // 2, 2 * BAL // shards
        group, y, core = place_of(shards)
        lane = lax.broadcasted_iota(jnp.int32, (1, 2 * tokens), 1)
        row = jnp.zeros((1, 2 * tokens), jnp.int32)
        source = jnp.zeros((1, 2 * tokens), jnp.int32)
        for start, slot in enumerate(SLOTS):
            place = lane - start * size
            here = (place >= 0) & (place < size)
            lower = lax.rem(group, half) ^ (slot // 4 * 2) ^ (slot // 2 % 2)
            quarter = (y ^ (slot % 2)) * CORES + core
            is_lower = place < front(lengths_ref[lower], quarter, shards)
            stands = jnp.where(
                is_lower, shards * place + quarter, shards * (size - 1 - place) + shards - 1 - quarter
            )
            row = jnp.where(here, stands, row)
            source = jnp.where(here, jnp.where(is_lower, lower, lower + half), source)
        ids = jnp.concatenate([ids_ref[0:1, g * cap : (g + 1) * cap] for g in range(groups)], axis=0)
        halves = jnp.concatenate([ids >> 8, ids & 255], axis=0)
        stood = lax.broadcasted_iota(jnp.int32, (cap, 2 * tokens), 0)
        pick = (stood == row).astype(jnp.float32).astype(jnp.bfloat16)
        found = jnp.dot(
            halves.astype(jnp.float32).astype(jnp.bfloat16), pick, preferred_element_type=jnp.float32
        )
        found = found[:groups] * 256.0 + found[groups:]
        of_group = lax.broadcasted_iota(jnp.int32, found.shape, 0) == source
        targets = jnp.sum(jnp.where(of_group, found, 0.0), axis=0, keepdims=True).astype(jnp.int32)
        start = 0
        for ref in (first_ref, second_ref, third_ref):
            ref[...] = targets[:, start : start + ref.shape[1]]
            start += ref.shape[1]
    else:
        for ref in (first_ref, second_ref, third_ref):
            ref[...] = jnp.zeros_like(ref)

    count, width = turned_ref.shape
    column = lax.broadcasted_iota(jnp.int32, (count, cap), 1)
    chosen = column == upright(rows_ref[...])
    places = jnp.sum(jnp.where(chosen, positions_ref[...], 0), axis=1, keepdims=True)
    half_head = HD // 2
    steps = lax.broadcasted_iota(jnp.int32, (count, half_head), 1).astype(jnp.float32)
    freqs = jnp.exp(-(2.0 * steps / HD) * jnp.log(jnp.full(steps.shape, ROPE_BASE, jnp.float32)))
    angles = places.astype(jnp.float32) * freqs
    cosine, sine = jnp.cos(angles), jnp.sin(angles)
    cosine = jnp.concatenate([cosine, cosine], axis=1)
    sine = jnp.concatenate([-sine, sine], axis=1)
    for copy in copies:
        copy.wait()
    pick = chosen.astype(jnp.float32).astype(jnp.bfloat16)
    rows = jnp.dot(pick, input_ref[...], preferred_element_type=jnp.float32).astype(jnp.bfloat16)
    projected = jnp.dot(rows, weight_ref[...], preferred_element_type=jnp.float32)
    squares = jnp.sum(projected * projected, axis=1, keepdims=True)
    lane = lax.broadcasted_iota(jnp.int32, (count, extra_ref.shape[1]), 1)
    diagonal = lax.broadcasted_iota(jnp.int32, lane.shape, 0) == lane
    extra = jnp.sum(jnp.where(diagonal, squares, 0.0), axis=0, keepdims=True)
    for label in range(1, SEGS):
        before = (segments_ref[...] < label).astype(jnp.float32)
        before = jnp.sum(before, axis=1, keepdims=True)
        extra = jnp.where(lane[0:1] == BREAKS + label, before, extra)
    extra_ref[...] = extra
    gained = projected * gain_ref[...]
    for start in range(0, width, HD):
        head = gained[:, start : start + HD]
        turned_ref[:, start : start + HD] = head * cosine + pltpu.roll(head, half_head, 1) * sine


def final_kernel(
    sizes,
    lengths_ref,
    continues_ref,
    got_ref,
    turned_ref,
    logprob_ref,
    entropy_ref,
    mean_ref,
    keys_ref,
):
    groups, shards = sizes
    parts, group = shards // CORES, lax.axis_index("grp")
    cap = logprob_ref.shape[1]
    size = 2 * BAL // shards
    tokens = 2 * parts * size
    columns = [
        merged(jnp.concatenate([got_ref[part, core] for part in range(parts)], axis=0)) for core in range(CORES)
    ]

    column, span = lax.rem(group, 2), tokens // 2
    halves = [[both[:, :span], both[:, span:]] for both in columns]
    own = jnp.concatenate([jnp.where(column == 0, a, b) for a, b in halves], axis=1)
    beside = jnp.concatenate([jnp.where(column == 0, b, a) for a, b in halves], axis=1)
    rest = jnp.concatenate([own, beside], axis=0)
    terms = []
    for _ in range(3):
        term = rest.astype(jnp.bfloat16).astype(jnp.float32)
        terms.append(term)
        rest = rest - term
    terms = jnp.concatenate(terms + [jnp.zeros_like(rest)], axis=0).astype(jnp.bfloat16)

    slots = lax.broadcasted_iota(jnp.int32, (1, cap), 1)
    is_first = group < groups // 2
    quarter = jnp.where(is_first, slots % shards, shards - 1 - slots % shards)
    place = jnp.where(is_first, slots // shards, size - 1 - slots // shards)
    home = quarter % CORES * span + quarter // CORES * size + place
    stood = lax.broadcasted_iota(jnp.int32, (CORES * span, cap), 0)
    pick = (stood == home).astype(jnp.float32).astype(jnp.bfloat16)
    found = jnp.dot(terms, pick, preferred_element_type=jnp.float32)
    found = found[0:4] + found[4:8] + found[8:12]
    def summed(who, logprob):
        note = got_ref[0, 0, who][7:8, LANES // 2 :]
        breaks = [note[:, BREAKS + i : BREAKS + i + 1].astype(jnp.int32) for i in range(1, SEGS)]
        live = slots < chosen(lengths_ref, who)
        logprob = jnp.where(live, logprob, 0.0)
        sums, counts = [], []
        for label in range(SEGS):
            member = live
            if label > 0:
                member = member & (slots >= breaks[label - 1])
            if label < SEGS - 1:
                member = member & (slots < breaks[label])
            sums.append(jnp.sum(jnp.where(member, logprob, 0.0), axis=1, keepdims=True))
            counts.append(jnp.sum(member.astype(jnp.float32), axis=1, keepdims=True))
        return logprob, sums, counts, breaks

    partner = group ^ 1
    logprob, sums, counts, breaks = summed(group, found[0:1])
    _, partner_sums, partner_counts, _ = summed(partner, found[2:3])
    length = chosen(lengths_ref, group)
    entropy = jnp.where(slots < length, found[1:2], 0.0)
    is_even = group % 2 == 0
    joined = chosen(continues_ref, jnp.where(is_even, group, partner)) == 1
    my_last = sum((length - 1 >= begin).astype(jnp.int32) for begin in breaks)
    target = jnp.where(is_even, my_last, jnp.zeros_like(my_last))
    extra_sum, extra_count = partner_sums[0], partner_counts[0]
    for label in range(1, SEGS):
        later = jnp.logical_not(is_even) & (partner_counts[label] > 0)
        extra_sum = jnp.where(later, partner_sums[label], extra_sum)
        extra_count = jnp.where(later, partner_counts[label], extra_count)
    labels = lax.broadcasted_iota(jnp.int32, (1, SEGS), 1)
    means = jnp.zeros((1, SEGS), jnp.float32)
    for label in range(SEGS):
        update = joined & (target == label)
        total_sum = sums[label] + jnp.where(update, extra_sum, 0.0)
        total_count = counts[label] + jnp.where(update, extra_count, 0.0)
        means = jnp.where(labels == label, total_sum / jnp.maximum(total_count, 1.0), means)
    logprob_ref[...] = logprob
    entropy_ref[...] = entropy
    mean_ref[...] = means

    count, width = turned_ref.shape
    squares = jnp.zeros((1, count), jnp.float32)
    for part in range(parts):
        for core in range(CORES):
            squares += got_ref[part, core, group][7:8, LANES // 2 : LANES // 2 + count]
    squares = upright(squares)
    scale = jnp.sqrt(squares / (width * shards) + NORM_EPS)
    keys_ref[...] = (turned_ref[...] / scale).astype(jnp.bfloat16)


def partners(sizes, flips):
    (groups, shards), (group_flip, shard_flip) = sizes, flips
    return [
        (g * shards + v, (g ^ group_flip) * shards + (v ^ shard_flip))
        for g in range(groups)
        for v in range(shards)
    ]


def local(
    sizes,
    final_hidden,
    norm_gain,
    head_weight,
    token_ids,
    group_lengths,
    segment_ids,
    continues,
    layer_input,
    key_weight,
    key_gain,
    positions,
    key_rows,
):
    groups, shards = sizes
    parts, half = shards // CORES, groups // 2
    cap, width = final_hidden.shape
    rows = cap // shards
    size = 2 * BAL // shards
    tokens = 2 * parts * size
    core = lax.axis_index("vocab") % CORES
    axes = ("grp", "vocab")
    swapped = sizes == (8, 4)

    def swap(array, group_flip, shard_flip):
        return lax.ppermute(array, axes, partners(sizes, (group_flip, shard_flip)))

    def lay(kernel, shape, *operands):
        return call(
            kernel,
            jax.ShapeDtypeStruct(shape, jnp.bfloat16),
            [WHOLE] * len(operands),
            size * cap * width,
            4 * size * width,
            out_specs=WHOLE,
        )(*operands)

    gap = size - rows
    hidden = (final_hidden, norm_gain.reshape(1, width))
    here = lay(functools.partial(prep_kernel, sizes, swapped), (rows, width), *hidden)

    count, key_width = key_rows.shape[0], key_weight.shape[1]
    turned, extra, *ids = call(
        functools.partial(side_kernel, sizes, swapped),
        (
            jax.ShapeDtypeStruct((count, key_width), jnp.float32),
            jax.ShapeDtypeStruct((1, LANES // 2), jnp.float32),
            jax.ShapeDtypeStruct((1, 3 * size), jnp.int32),
            jax.ShapeDtypeStruct((1, 2 * size), jnp.int32),
            jax.ShapeDtypeStruct((1, 3 * size), jnp.int32),
        ),
        [SCALARS] + [WHOLE] * 5 + [FAR, FAR],
        2 * count * width * key_width,
        2 * width * key_width,
        scratch_shapes=[
            pltpu.VMEM(layer_input.shape, jnp.bfloat16),
            pltpu.VMEM(key_weight.shape, jnp.bfloat16),
            pltpu.SemaphoreType.DMA((2,)),
        ],
    )(
        group_lengths,
        key_rows.reshape(1, count),
        positions.reshape(1, cap),
        segment_ids.reshape(1, cap),
        token_ids.reshape(1, groups * cap),
        key_gain.reshape(1, key_width),
        layer_input,
        key_weight,
    )

    head_weight, here = lax.optimization_barrier((head_weight, here))
    far_head = swap(head_weight, 0, 1)
    heads = (head_weight, far_head)
    sent_shape = jax.ShapeDtypeStruct((groups * shards, 8, LANES), jnp.float32)
    if swapped:
        other = swap(here, 4, 0)
        ends = lay(functools.partial(ends_kernel, sizes), (parts, gap, width), *hidden, here)
        across = swap(ends, 1, 0)
        beyond = swap(ends, 2, 0)
        corner = swap(ends, 3, 0)
        other, across, beyond, corner, far_head, ids, extra, turned = lax.optimization_barrier(
            (other, across, beyond, corner, far_head, ids, extra, turned)
        )
        heads = (head_weight, far_head)
        rest = lay(
            functools.partial(mix_kernel, sizes), (rows, width), group_lengths.reshape(1, groups), here, other
        )
        far_rest = swap(rest, 2, 0)
        rest_xy = swap(rest, 1, 2)
        rest_x = swap(rest, 1, 0)
        rest_y = swap(rest, 0, 2)
        far_x = swap(far_rest, 1, 0)
        far_y = swap(far_rest, 0, 2)
        far_xy = swap(rest_xy, 2, 0)
        first = score(
            functools.partial(piece_kernel, sizes, (0, 1, 0)),
            jax.ShapeDtypeStruct((8, 3 * size), jnp.float32),
            ids[0],
            heads,
            (ends, across, beyond, rest, rest_xy, far_rest),
            3 * size,
        )
        rest_y, rest_x, first = lax.optimization_barrier((rest_y, rest_x, first))
        second = score(
            functools.partial(piece_kernel, sizes, (1, 0)),
            jax.ShapeDtypeStruct((8, 2 * size), jnp.float32),
            ids[1],
            heads,
            (ends, across, rest_y, rest_x),
            2 * size,
        )
        sent = score(
            functools.partial(send_kernel, sizes),
            sent_shape,
            ids[2],
            heads,
            (first, second, extra, beyond, corner, far_y, far_x, far_xy),
            3 * size,
        )
    else:
        taken = front(group_lengths[:half, None], jnp.arange(shards)[None, :], shards)
        ids = token_ids.reshape(groups, rows, shards).transpose(0, 2, 1)
        lower = jnp.pad(ids[:half], ((0, 0), (0, 0), (0, gap)))
        upper = jnp.pad(ids[half:, ::-1, ::-1], ((0, 0), (0, 0), (gap, 0)))
        is_lower = jnp.arange(size)[None, None, :] < taken[:, :, None]
        ids = jnp.where(is_lower, lower, upper).reshape(half, parts, CORES, size)
        ids = lax.dynamic_index_in_dim(ids, core, 2, False).reshape(1, -1)
        every = lax.all_gather(here, axes).reshape(groups, parts, CORES, rows, width)
        every = lax.dynamic_index_in_dim(every, core, 2, False)
        first = jnp.pad(every[:half], ((0, 0), (0, 0), (0, gap), (0, 0)))
        second = jnp.pad(every[half:], ((0, 0), (0, 0), (gap, 0), (0, 0)))
        is_lower = is_lower.reshape(half, parts, CORES, size)
        is_lower = lax.dynamic_index_in_dim(is_lower, core, 2, False)
        every = jnp.where(is_lower[..., None], first, second)
        stats = score(
            functools.partial(plain_kernel, sizes),
            jax.ShapeDtypeStruct((8, half // 2 * tokens), jnp.float32),
            ids,
            heads,
            (every.reshape(-1, width),),
            half // 2 * tokens,
            scratch=False,
        )
        sets = half // 2
        state = [row.reshape(sets, tokens) for row in stats[:3]]
        extra = jnp.broadcast_to(extra, (sets, LANES // 2))
        stats = packed(state, extra).reshape(8, sets, LANES).transpose(1, 0, 2)
        sent = jnp.broadcast_to(
            stats[None, None, :, None], (shards, 2, sets, 2, 8, LANES)
        ).reshape(sent_shape.shape)
    got = lax.all_to_all(sent, ("vocab", "grp"), 0, 0, tiled=False)

    logprob, entropy, means, keys = call(
        functools.partial(final_kernel, sizes),
        (
            jax.ShapeDtypeStruct((1, cap), jnp.float32),
            jax.ShapeDtypeStruct((1, cap), jnp.float32),
            jax.ShapeDtypeStruct((1, SEGS), jnp.float32),
            jax.ShapeDtypeStruct((count, key_width), jnp.bfloat16),
        ),
        [WHOLE] * 4,
        1 << 24,
        4 * groups * shards * 8 * LANES,
    )(
        group_lengths.reshape(1, groups),
        continues.reshape(1, groups),
        got.reshape(parts, CORES, groups, 8, LANES),
        turned,
    )
    return logprob.reshape(cap), entropy.reshape(cap), means.reshape(SEGS), keys


def solution(mesh):
    sizes = (mesh.shape["grp"], mesh.shape["vocab"])
    in_specs = (
        P("grp", None),
        P(),
        P(("vocab", "grp"), None),
        P(),
        P(),
        P("grp"),
        P(),
        P("grp", None),
        P(None, "vocab"),
        P("vocab"),
        P("grp"),
        P("grp"),
    )
    out_specs = (P("grp"), P("grp"), P("grp"), P("grp", "vocab"))
    return jax.shard_map(
        functools.partial(local, sizes),
        mesh=mesh,
        in_specs=in_specs,
        out_specs=out_specs,
        check_vma=False,
    )
```

```python
import functools

import jax
import jax.numpy as jnp
from jax import lax
from jax.experimental import pallas as pl
from jax.experimental.pallas import tpu as pltpu
from jax.sharding import PartitionSpec as P

HD = 128
SEGS = 4
BAL = 160
CORES = 2
LANES = 128
BREAKS = 31
SLOTS = (0, 3, 4, 1, 2, 5, 6, 7)

NORM_EPS = 1e-06
ROPE_BASE = 500000.0

VMEM_LIMIT = 24 * 1024 * 1024
WHOLE = pl.BlockSpec(memory_space=pltpu.VMEM)
SCALARS = pl.BlockSpec(memory_space=pltpu.SMEM)
FAR = pl.BlockSpec(memory_space=pltpu.HBM)


def call(kernel, out_shape, in_specs, flops, moved, vmem=VMEM_LIMIT, **more):
    return pl.pallas_call(
        kernel,
        out_shape=out_shape,
        in_specs=in_specs,
        compiler_params=pltpu.CompilerParams(vmem_limit_bytes=vmem),
        cost_estimate=pl.CostEstimate(flops=flops, bytes_accessed=moved, transcendentals=0),
        **more,
    )


def place_of(shards):
    shard = lax.axis_index("vocab")
    return lax.axis_index("grp"), lax.div(shard, CORES), lax.rem(shard, CORES)


def source_row(place, quarter, is_first, quarters, rows):
    return jnp.where(
        is_first,
        quarters * place + quarter,
        quarters * (rows - 1 - place) + quarters - 1 - quarter,
    )


def front(length, quarter, shards):
    return (length - quarter + shards - 1) // shards


def chosen(row_ref, index):
    row = row_ref[...]
    lane = lax.broadcasted_iota(jnp.int32, row.shape, 1)
    return jnp.sum(jnp.where(lane == index, row, 0), axis=1, keepdims=True)


def fetch(sources, targets, semaphores):
    copies = [
        pltpu.make_async_copy(source, target, semaphores.at[i])
        for i, (source, target) in enumerate(zip(sources, targets))
    ]
    for copy in copies:
        copy.start()
    return copies


def dealt(sizes, hidden_ref, gain_ref, t, rows, turned):
    groups, shards = sizes
    group, y, core = place_of(shards)
    is_first = group < groups // 2
    count = hidden_ref.shape[0] // shards
    place = lax.broadcasted_iota(jnp.int32, (rows, hidden_ref.shape[0]), 0)
    column = lax.broadcasted_iota(jnp.int32, place.shape, 1)
    if turned:
        gap = 2 * BAL // shards - count
        back = jnp.where(place < gap, place + (count - gap), place - gap)
        place = jnp.where(is_first, place, back)
    row = source_row(place, (y ^ t) * CORES + core, is_first, shards, count)
    pick = (column == row).astype(jnp.float32).astype(jnp.bfloat16)
    found = jnp.dot(pick, hidden_ref[...], preferred_element_type=jnp.float32)
    meansq = jnp.sum(found * found, axis=-1, keepdims=True) / found.shape[1]
    return (found * lax.rsqrt(meansq + NORM_EPS) * gain_ref[...]).astype(jnp.bfloat16)


def prep_kernel(sizes, turned, hidden_ref, gain_ref, out_ref):
    out_ref[...] = dealt(sizes, hidden_ref, gain_ref, 0, out_ref.shape[0], turned)


def ends_kernel(sizes, hidden_ref, gain_ref, here_ref, out_ref):
    rows = out_ref.shape[1]
    out_ref[0] = here_ref[0:rows, :]
    for t in range(1, out_ref.shape[0]):
        out_ref[t] = dealt(sizes, hidden_ref, gain_ref, t, rows, True)


def mix_kernel(sizes, lengths_ref, here_ref, other_ref, out_ref):
    groups, shards = sizes
    half = groups // 2
    group, y, core = place_of(shards)
    rows, width = here_ref.shape
    gap = 2 * BAL // shards - rows
    length = front(chosen(lengths_ref, lax.rem(group, half)), y * CORES + core, shards)
    is_lower = lax.broadcasted_iota(jnp.int32, (rows - gap, width), 0) + gap < length

    def lay(lower_ref, upper_ref):
        lower, upper = (ref[gap:rows, :].astype(jnp.float32) for ref in (lower_ref, upper_ref))
        out_ref[0 : rows - gap, :] = jnp.where(is_lower, lower, upper).astype(jnp.bfloat16)

    @pl.when(group < half)
    def _():
        lay(here_ref, other_ref)

    @pl.when(group >= half)
    def _():
        lay(other_ref, here_ref)

    out_ref[rows - gap : rows, :] = other_ref[0:gap, :]


def gather_pieces(sizes, pieces, tokens_ref):
    is_first = lax.axis_index("grp") < sizes[0] // 2
    start = 0
    for end, rest_ref in pieces:
        gap, rows = end.shape[0], rest_ref.shape[0]
        last = start + rows
        own, partner = jnp.where(is_first, start, last), jnp.where(is_first, last, start)
        tokens_ref[pl.ds(pl.multiple_of(own, 16), gap), :] = end[...]
        tokens_ref[start + gap : last, :] = rest_ref[0 : rows - gap, :]
        tokens_ref[pl.ds(pl.multiple_of(partner, 16), gap), :] = rest_ref[rows - gap : rows, :]
        start += gap + rows
    return tokens_ref[...]


def statistics(bases, targets, tokens, heads):
    vocab = heads[0].shape[0]
    cuts = [0, vocab]
    if vocab % 16 == 0:
        cuts = [vocab * i // 2 // 16 * 16 for i in range(2)] + [vocab]
    chunks = [
        (base + start, head_ref, start, stop)
        for base, head_ref in zip(bases, heads)
        for start, stop in zip(cuts, cuts[1:])
    ]

    def logits_of(chunk):
        _, head_ref, start, stop = chunk
        product = lax.dot_general(
            head_ref[start:stop, :], tokens, (((1,), (1,)), ((), ())), preferred_element_type=jnp.float32
        )
        return product.astype(jnp.bfloat16).astype(jnp.float32)

    state = None
    ready = [logits_of(chunk) for chunk in chunks[:1]]
    for i, chunk in enumerate(chunks):
        if i + 1 < len(chunks):
            ready.append(logits_of(chunks[i + 1]))
        logits = ready[i]
        entry = lax.broadcasted_iota(jnp.int32, logits.shape, 0)
        found = jnp.where(entry == targets - chunk[0], logits, 0.0)
        picked = jnp.sum(found, axis=0, keepdims=True)
        top = jnp.max(logits, axis=0, keepdims=True)
        if state is not None:
            top = jnp.maximum(top, state[0])
        shifted = jnp.exp(logits - top)
        expsum = jnp.sum(shifted, axis=0, keepdims=True)
        moment = jnp.sum(shifted * logits, axis=0, keepdims=True)
        if state is not None:
            scale = jnp.exp(state[0] - top)
            expsum += state[1] * scale
            moment += state[2] * scale
            picked += state[3]
        state = (top, expsum, moment, picked)
    top, expsum, moment, picked = state
    return top + jnp.log(expsum), moment / expsum, picked


def packed(state, extra):
    flat = [row[:, : 2 * LANES] for row in state] + [row[:, 2 * LANES :] for row in state] + [extra]
    flat = jnp.concatenate(flat, axis=1)
    return jnp.concatenate(
        [flat[:, i : i + LANES] for i in range(0, flat.shape[1], LANES)], axis=0
    )


def merged(every):
    half = LANES // 2
    row = lax.broadcasted_iota(jnp.int32, every.shape[1:], 0)
    top = jnp.max(every, axis=0)
    scale = jnp.exp(every - top[None])
    means = [
        jnp.where(row == 6, pltpu.roll(one, half, 1), pltpu.roll(one, one.shape[0] - 2, 0))
        for one in (every[i] for i in range(every.shape[0]))
    ]
    expsum = jnp.sum(scale, axis=0)
    moment = sum(scale[i] * mean for i, mean in enumerate(means))
    picked = jnp.sum(every, axis=0)
    lse = top + jnp.log(expsum)
    entropy = lse - moment / expsum

    def lay(block, first, last):
        return jnp.concatenate([block[first : first + 1], block[first + 1 : first + 2], last], axis=1)

    lse_row = lay(lse, 0, lse[6:7, :half])
    return jnp.concatenate(
        [lay(picked, 4, picked[7:8, :half]) - lse_row, lay(entropy, 0, entropy[6:7, :half])], axis=0
    )


def bases_of(sizes, head_ref):
    groups, shards = sizes
    group, shard = lax.axis_index("grp"), lax.axis_index("vocab")
    return [((shard ^ flip) * groups + group) * head_ref.shape[0] for flip in (0, 1)]


def rows_of(state, out_ref):
    rows = jnp.concatenate([*state, jnp.zeros((5, out_ref.shape[1]), jnp.float32)], axis=0)
    out_ref[...] = rows


def plain_kernel(sizes, targets_ref, near_ref, far_ref, tokens_ref, out_ref):
    state = statistics(
        bases_of(sizes, near_ref), targets_ref[...], tokens_ref[...], (near_ref, far_ref)
    )
    rows_of(state, out_ref)


def piece_kernel(sizes, picks, targets_ref, near_ref, far_ref, *refs):
    *pieces, out_ref, tokens_ref = refs
    ends = [ref.at[which] for ref, which in zip(pieces, picks)]
    tokens = gather_pieces(sizes, zip(ends, pieces[len(picks) :]), tokens_ref)
    state = statistics(bases_of(sizes, near_ref), targets_ref[...], tokens, (near_ref, far_ref))
    rows_of(state, out_ref)


def send_kernel(
    sizes, targets_ref, near_ref, far_ref, first_ref, second_ref, extra_ref, beyond_ref, corner_ref, *refs
):
    *rests, out_ref, tokens_ref = refs
    groups, shards = sizes
    size = 2 * BAL // shards
    ends = (beyond_ref.at[1], corner_ref.at[0], corner_ref.at[1])
    tokens = gather_pieces(sizes, zip(ends, rests), tokens_ref)
    state = statistics(bases_of(sizes, near_ref), targets_ref[...], tokens, (near_ref, far_ref))
    group, y, _ = place_of(shards)

    def settled(rows):
        turned = jnp.concatenate([rows[:, 2 * size :], rows[:, : 2 * size]], axis=1)
        rows = jnp.where(lax.rem(group, 2) == 1, turned, rows)
        quarters = [rows[:, i * size : (i + 1) * size] for i in (1, 0, 3, 2)]
        return jnp.where(y == 1, jnp.concatenate(quarters, axis=1), rows)

    first, second = first_ref[0:4, :], second_ref[0:4, :]
    third = jnp.concatenate([*state, jnp.zeros_like(state[0])], axis=0)
    own = settled(jnp.concatenate([first[:, :size], second, first[:, size : 2 * size]], axis=1))
    beyond = settled(jnp.concatenate([first[:, 2 * size :], third], axis=1))
    own, beyond = (
        packed([rows[i : i + 1] for i in range(3)], extra_ref[...]) for rows in (own, beyond)
    )
    mine = lax.div(lax.rem(group, groups // 2), 2)
    for which in range(groups // 4):
        block = jnp.where(mine == which, own, beyond)
        for group in range(groups):
            if group % (groups // 2) // 2 == which:
                for shard in range(shards):
                    out_ref[shard * groups + group] = block


def score(kernel, out_shape, targets, heads, extras, count, scratch=True):
    vocab, width = heads[0].shape
    return call(
        kernel,
        out_shape,
        [WHOLE] * (3 + len(extras)),
        4 * vocab * count * width,
        4 * vocab * width + 2 * count * width,
        out_specs=WHOLE,
        scratch_shapes=[pltpu.VMEM((count, width), jnp.bfloat16)] if scratch else [],
    )(targets, *heads, *extras)


def upright(row):
    count = row.shape[1]
    diagonal = lax.broadcasted_iota(jnp.int32, (count, count), 0) == lax.broadcasted_iota(
        jnp.int32, (count, count), 1
    )
    return jnp.sum(jnp.where(diagonal, row, 0), axis=1, keepdims=True)


def side_kernel(
    sizes,
    swapped,
    lengths_ref,
    rows_ref,
    positions_ref,
    segments_ref,
    ids_ref,
    gain_ref,
    input_hbm,
    weight_hbm,
    turned_ref,
    extra_ref,
    first_ref,
    second_ref,
    third_ref,
    input_ref,
    weight_ref,
    semaphores,
):
    groups, shards = sizes
    copies = fetch((input_hbm, weight_hbm), (input_ref, weight_ref), semaphores)
    cap = segments_ref.shape[1]
    if swapped:
        tokens = first_ref.shape[1] + second_ref.shape[1] // 2
        half, size = groups // 2, 2 * BAL // shards
        group, y, core = place_of(shards)
        lane = lax.broadcasted_iota(jnp.int32, (1, 2 * tokens), 1)
        row = jnp.zeros((1, 2 * tokens), jnp.int32)
        source = jnp.zeros((1, 2 * tokens), jnp.int32)
        for start, slot in enumerate(SLOTS):
            place = lane - start * size
            here = (place >= 0) & (place < size)
            lower = lax.rem(group, half) ^ (slot // 4 * 2) ^ (slot // 2 % 2)
            quarter = (y ^ (slot % 2)) * CORES + core
            is_lower = place < front(lengths_ref[lower], quarter, shards)
            stands = jnp.where(
                is_lower, shards * place + quarter, shards * (size - 1 - place) + shards - 1 - quarter
            )
            row = jnp.where(here, stands, row)
            source = jnp.where(here, jnp.where(is_lower, lower, lower + half), source)
        ids = jnp.concatenate([ids_ref[0:1, g * cap : (g + 1) * cap] for g in range(groups)], axis=0)
        halves = jnp.concatenate([ids >> 8, ids & 255], axis=0)
        stood = lax.broadcasted_iota(jnp.int32, (cap, 2 * tokens), 0)
        pick = (stood == row).astype(jnp.float32).astype(jnp.bfloat16)
        found = jnp.dot(
            halves.astype(jnp.float32).astype(jnp.bfloat16), pick, preferred_element_type=jnp.float32
        )
        found = found[:groups] * 256.0 + found[groups:]
        of_group = lax.broadcasted_iota(jnp.int32, found.shape, 0) == source
        targets = jnp.sum(jnp.where(of_group, found, 0.0), axis=0, keepdims=True).astype(jnp.int32)
        start = 0
        for ref in (first_ref, second_ref, third_ref):
            ref[...] = targets[:, start : start + ref.shape[1]]
            start += ref.shape[1]
    else:
        for ref in (first_ref, second_ref, third_ref):
            ref[...] = jnp.zeros_like(ref)

    count, width = turned_ref.shape
    column = lax.broadcasted_iota(jnp.int32, (count, cap), 1)
    chosen = column == upright(rows_ref[...])
    places = jnp.sum(jnp.where(chosen, positions_ref[...], 0), axis=1, keepdims=True)
    half_head = HD // 2
    steps = lax.broadcasted_iota(jnp.int32, (count, half_head), 1).astype(jnp.float32)
    freqs = jnp.exp(-(2.0 * steps / HD) * jnp.log(jnp.full(steps.shape, ROPE_BASE, jnp.float32)))
    angles = places.astype(jnp.float32) * freqs
    cosine, sine = jnp.cos(angles), jnp.sin(angles)
    cosine = jnp.concatenate([cosine, cosine], axis=1)
    sine = jnp.concatenate([-sine, sine], axis=1)
    for copy in copies:
        copy.wait()
    pick = chosen.astype(jnp.float32).astype(jnp.bfloat16)
    rows = jnp.dot(pick, input_ref[...], preferred_element_type=jnp.float32).astype(jnp.bfloat16)
    projected = jnp.dot(rows, weight_ref[...], preferred_element_type=jnp.float32)
    squares = jnp.sum(projected * projected, axis=1, keepdims=True)
    lane = lax.broadcasted_iota(jnp.int32, (count, extra_ref.shape[1]), 1)
    diagonal = lax.broadcasted_iota(jnp.int32, lane.shape, 0) == lane
    extra = jnp.sum(jnp.where(diagonal, squares, 0.0), axis=0, keepdims=True)
    for label in range(1, SEGS):
        before = (segments_ref[...] < label).astype(jnp.float32)
        before = jnp.sum(before, axis=1, keepdims=True)
        extra = jnp.where(lane[0:1] == BREAKS + label, before, extra)
    extra_ref[...] = extra
    gained = projected * gain_ref[...]
    for start in range(0, width, HD):
        head = gained[:, start : start + HD]
        turned_ref[:, start : start + HD] = head * cosine + pltpu.roll(head, half_head, 1) * sine


def final_kernel(
    sizes,
    lengths_ref,
    continues_ref,
    got_ref,
    turned_ref,
    logprob_ref,
    entropy_ref,
    mean_ref,
    keys_ref,
):
    groups, shards = sizes
    parts, group = shards // CORES, lax.axis_index("grp")
    cap = logprob_ref.shape[1]
    size = 2 * BAL // shards
    tokens = 2 * parts * size
    columns = [
        merged(jnp.concatenate([got_ref[part, core] for part in range(parts)], axis=0)) for core in range(CORES)
    ]

    column, span = lax.rem(group, 2), tokens // 2
    halves = [[both[:, :span], both[:, span:]] for both in columns]
    own = jnp.concatenate([jnp.where(column == 0, a, b) for a, b in halves], axis=1)
    beside = jnp.concatenate([jnp.where(column == 0, b, a) for a, b in halves], axis=1)
    rest = jnp.concatenate([own, beside], axis=0)
    terms = []
    for _ in range(3):
        term = rest.astype(jnp.bfloat16).astype(jnp.float32)
        terms.append(term)
        rest = rest - term
    terms = jnp.concatenate(terms + [jnp.zeros_like(rest)], axis=0).astype(jnp.bfloat16)

    slots = lax.broadcasted_iota(jnp.int32, (1, cap), 1)
    is_first = group < groups // 2
    quarter = jnp.where(is_first, slots % shards, shards - 1 - slots % shards)
    place = jnp.where(is_first, slots // shards, size - 1 - slots // shards)
    home = quarter % CORES * span + quarter // CORES * size + place
    stood = lax.broadcasted_iota(jnp.int32, (CORES * span, cap), 0)
    pick = (stood == home).astype(jnp.float32).astype(jnp.bfloat16)
    found = jnp.dot(terms, pick, preferred_element_type=jnp.float32)
    found = found[0:4] + found[4:8] + found[8:12]
    def summed(who, logprob):
        note = got_ref[0, 0, who][7:8, LANES // 2 :]
        breaks = [note[:, BREAKS + i : BREAKS + i + 1].astype(jnp.int32) for i in range(1, SEGS)]
        live = slots < chosen(lengths_ref, who)
        logprob = jnp.where(live, logprob, 0.0)
        sums, counts = [], []
        for label in range(SEGS):
            member = live
            if label > 0:
                member = member & (slots >= breaks[label - 1])
            if label < SEGS - 1:
                member = member & (slots < breaks[label])
            sums.append(jnp.sum(jnp.where(member, logprob, 0.0), axis=1, keepdims=True))
            counts.append(jnp.sum(member.astype(jnp.float32), axis=1, keepdims=True))
        return logprob, sums, counts, breaks

    partner = group ^ 1
    logprob, sums, counts, breaks = summed(group, found[0:1])
    _, partner_sums, partner_counts, _ = summed(partner, found[2:3])
    length = chosen(lengths_ref, group)
    entropy = jnp.where(slots < length, found[1:2], 0.0)
    is_even = group % 2 == 0
    joined = chosen(continues_ref, jnp.where(is_even, group, partner)) == 1
    my_last = sum((length - 1 >= begin).astype(jnp.int32) for begin in breaks)
    target = jnp.where(is_even, my_last, jnp.zeros_like(my_last))
    extra_sum, extra_count = partner_sums[0], partner_counts[0]
    for label in range(1, SEGS):
        later = jnp.logical_not(is_even) & (partner_counts[label] > 0)
        extra_sum = jnp.where(later, partner_sums[label], extra_sum)
        extra_count = jnp.where(later, partner_counts[label], extra_count)
    labels = lax.broadcasted_iota(jnp.int32, (1, SEGS), 1)
    means = jnp.zeros((1, SEGS), jnp.float32)
    for label in range(SEGS):
        update = joined & (target == label)
        total_sum = sums[label] + jnp.where(update, extra_sum, 0.0)
        total_count = counts[label] + jnp.where(update, extra_count, 0.0)
        means = jnp.where(labels == label, total_sum / jnp.maximum(total_count, 1.0), means)
    logprob_ref[...] = logprob
    entropy_ref[...] = entropy
    mean_ref[...] = means

    count, width = turned_ref.shape
    squares = jnp.zeros((1, count), jnp.float32)
    for part in range(parts):
        for core in range(CORES):
            squares += got_ref[part, core, group][7:8, LANES // 2 : LANES // 2 + count]
    squares = upright(squares)
    scale = jnp.sqrt(squares / (width * shards) + NORM_EPS)
    keys_ref[...] = (turned_ref[...] * (1.0 / scale)).astype(jnp.bfloat16)


def partners(sizes, flips):
    (groups, shards), (group_flip, shard_flip) = sizes, flips
    return [
        (g * shards + v, (g ^ group_flip) * shards + (v ^ shard_flip))
        for g in range(groups)
        for v in range(shards)
    ]


def local(
    sizes,
    final_hidden,
    norm_gain,
    head_weight,
    token_ids,
    group_lengths,
    segment_ids,
    continues,
    layer_input,
    key_weight,
    key_gain,
    positions,
    key_rows,
):
    groups, shards = sizes
    parts, half = shards // CORES, groups // 2
    cap, width = final_hidden.shape
    rows = cap // shards
    size = 2 * BAL // shards
    tokens = 2 * parts * size
    core = lax.axis_index("vocab") % CORES
    axes = ("grp", "vocab")
    swapped = sizes == (8, 4)

    def swap(array, group_flip, shard_flip):
        return lax.ppermute(array, axes, partners(sizes, (group_flip, shard_flip)))

    def lay(kernel, shape, *operands):
        return call(
            kernel,
            jax.ShapeDtypeStruct(shape, jnp.bfloat16),
            [WHOLE] * len(operands),
            size * cap * width,
            4 * size * width,
            out_specs=WHOLE,
        )(*operands)

    gap = size - rows
    hidden = (final_hidden, norm_gain.reshape(1, width))
    here = lay(functools.partial(prep_kernel, sizes, swapped), (rows, width), *hidden)

    count, key_width = key_rows.shape[0], key_weight.shape[1]
    turned, extra, *ids = call(
        functools.partial(side_kernel, sizes, swapped),
        (
            jax.ShapeDtypeStruct((count, key_width), jnp.float32),
            jax.ShapeDtypeStruct((1, LANES // 2), jnp.float32),
            jax.ShapeDtypeStruct((1, 3 * size), jnp.int32),
            jax.ShapeDtypeStruct((1, 2 * size), jnp.int32),
            jax.ShapeDtypeStruct((1, 3 * size), jnp.int32),
        ),
        [SCALARS] + [WHOLE] * 5 + [FAR, FAR],
        2 * count * width * key_width,
        2 * width * key_width,
        scratch_shapes=[
            pltpu.VMEM(layer_input.shape, jnp.bfloat16),
            pltpu.VMEM(key_weight.shape, jnp.bfloat16),
            pltpu.SemaphoreType.DMA((2,)),
        ],
    )(
        group_lengths,
        key_rows.reshape(1, count),
        positions.reshape(1, cap),
        segment_ids.reshape(1, cap),
        token_ids.reshape(1, groups * cap),
        key_gain.reshape(1, key_width),
        layer_input,
        key_weight,
    )

    head_weight, here = lax.optimization_barrier((head_weight, here))
    far_head = swap(head_weight, 0, 1)
    heads = (head_weight, far_head)
    sent_shape = jax.ShapeDtypeStruct((groups * shards, 8, LANES), jnp.float32)
    if swapped:
        other = swap(here, 4, 0)
        ends = lay(functools.partial(ends_kernel, sizes), (parts, gap, width), *hidden, here)
        across = swap(ends, 1, 0)
        beyond = swap(ends, 2, 0)
        corner = swap(ends, 3, 0)
        other, across, beyond, corner, far_head, ids, extra, turned = lax.optimization_barrier(
            (other, across, beyond, corner, far_head, ids, extra, turned)
        )
        heads = (head_weight, far_head)
        rest = lay(
            functools.partial(mix_kernel, sizes), (rows, width), group_lengths.reshape(1, groups), here, other
        )
        far_rest = swap(rest, 2, 0)
        rest_xy = swap(rest, 1, 2)
        rest_x = swap(rest, 1, 0)
        rest_y = swap(rest, 0, 2)
        far_x = swap(far_rest, 1, 0)
        far_y = swap(far_rest, 0, 2)
        far_xy = swap(rest_xy, 2, 0)
        first = score(
            functools.partial(piece_kernel, sizes, (0, 1, 0)),
            jax.ShapeDtypeStruct((8, 3 * size), jnp.float32),
            ids[0],
            heads,
            (ends, across, beyond, rest, rest_xy, far_rest),
            3 * size,
        )
        rest_y, rest_x, first = lax.optimization_barrier((rest_y, rest_x, first))
        second = score(
            functools.partial(piece_kernel, sizes, (1, 0)),
            jax.ShapeDtypeStruct((8, 2 * size), jnp.float32),
            ids[1],
            heads,
            (ends, across, rest_y, rest_x),
            2 * size,
        )
        sent = score(
            functools.partial(send_kernel, sizes),
            sent_shape,
            ids[2],
            heads,
            (first, second, extra, beyond, corner, far_y, far_x, far_xy),
            3 * size,
        )
    else:
        taken = front(group_lengths[:half, None], jnp.arange(shards)[None, :], shards)
        ids = token_ids.reshape(groups, rows, shards).transpose(0, 2, 1)
        lower = jnp.pad(ids[:half], ((0, 0), (0, 0), (0, gap)))
        upper = jnp.pad(ids[half:, ::-1, ::-1], ((0, 0), (0, 0), (gap, 0)))
        is_lower = jnp.arange(size)[None, None, :] < taken[:, :, None]
        ids = jnp.where(is_lower, lower, upper).reshape(half, parts, CORES, size)
        ids = lax.dynamic_index_in_dim(ids, core, 2, False).reshape(1, -1)
        every = lax.all_gather(here, axes).reshape(groups, parts, CORES, rows, width)
        every = lax.dynamic_index_in_dim(every, core, 2, False)
        first = jnp.pad(every[:half], ((0, 0), (0, 0), (0, gap), (0, 0)))
        second = jnp.pad(every[half:], ((0, 0), (0, 0), (gap, 0), (0, 0)))
        is_lower = is_lower.reshape(half, parts, CORES, size)
        is_lower = lax.dynamic_index_in_dim(is_lower, core, 2, False)
        every = jnp.where(is_lower[..., None], first, second)
        stats = score(
            functools.partial(plain_kernel, sizes),
            jax.ShapeDtypeStruct((8, half // 2 * tokens), jnp.float32),
            ids,
            heads,
            (every.reshape(-1, width),),
            half // 2 * tokens,
            scratch=False,
        )
        sets = half // 2
        state = [row.reshape(sets, tokens) for row in stats[:3]]
        extra = jnp.broadcast_to(extra, (sets, LANES // 2))
        stats = packed(state, extra).reshape(8, sets, LANES).transpose(1, 0, 2)
        sent = jnp.broadcast_to(
            stats[None, None, :, None], (shards, 2, sets, 2, 8, LANES)
        ).reshape(sent_shape.shape)
    got = lax.all_to_all(sent, ("vocab", "grp"), 0, 0, tiled=False)

    logprob, entropy, means, keys = call(
        functools.partial(final_kernel, sizes),
        (
            jax.ShapeDtypeStruct((1, cap), jnp.float32),
            jax.ShapeDtypeStruct((1, cap), jnp.float32),
            jax.ShapeDtypeStruct((1, SEGS), jnp.float32),
            jax.ShapeDtypeStruct((count, key_width), jnp.bfloat16),
        ),
        [WHOLE] * 4,
        1 << 24,
        4 * groups * shards * 8 * LANES,
    )(
        group_lengths.reshape(1, groups),
        continues.reshape(1, groups),
        got.reshape(parts, CORES, groups, 8, LANES),
        turned,
    )
    return logprob.reshape(cap), entropy.reshape(cap), means.reshape(SEGS), keys


def solution(mesh):
    sizes = (mesh.shape["grp"], mesh.shape["vocab"])
    in_specs = (
        P("grp", None),
        P(),
        P(("vocab", "grp"), None),
        P(),
        P(),
        P("grp"),
        P(),
        P("grp", None),
        P(None, "vocab"),
        P("vocab"),
        P("grp"),
        P("grp"),
    )
    out_specs = (P("grp"), P("grp"), P("grp"), P("grp", "vocab"))
    return jax.shard_map(
        functools.partial(local, sizes),
        mesh=mesh,
        in_specs=in_specs,
        out_specs=out_specs,
        check_vma=False,
    )
```
